32 devices in a mesh: groups: 2 (over x), inp: 16 (over z, y, core).
Axes of the slice: x: 2, y: 2, z: 4, core: 2. Of those that a mesh axis runs over, the one named last changes fastest.
Arguments:
- tokens: bfloat16 [512, 6144], P(('groups', 'inp')), parts along dimension 0, may hold values from -6 to 6
- dropout_masks: int32 [8, 512, 48], P(None, 'groups'), parts along dimension 1, may hold values 0 or 1
- input_gain: float32 [6144], replicated, may hold values from 0.5 to 1.5
- w_qkv: bfloat16 [128, 3, 48, 6144], P('inp'), may hold values from -0.078125 to 0.078125
- w_up: bfloat16 [24576, 6144], P('inp'), may hold values from -0.078125 to 0.078125
- query_gain: float32 [128], replicated, may hold values from 0.1 to 1.9
- key_gain: float32 [128], replicated, may hold values from 0.1 to 1.9
- w_proj: bfloat16 [128, 48, 6144], P('inp'), may hold values from -0.109375 to 0.109375
- w_down: bfloat16 [24576, 6144], P('inp'), may hold values from -0.0546875 to 0.0546875
- final_gain: float32 [6144], replicated, may hold values from 0.5 to 1.5
- w_head: bfloat16 [6144, 1000], P('inp'), may hold values from -0.625 to 0.625
Outputs:
- embedding: float32 [2, 8, 6144], P('groups', None, 'inp'), parts along dimension 0
- bald: float32 [2], P('groups'), parts along dimension 0
The draws below stay inside these ranges and needn't reach their ends.
There are 2 independent parts, one for each index of `groups`. The reference program is written for one: setup_inputs(seed, part) draws one part's arguments, and reference() takes and returns one part's arrays. A program takes and returns all parts, laid end to end along the dimension named above; an argument that names none is the same for every part. Nothing has to cross between parts.
All inputs are finite; a program needn't handle non-finite values.
Results may differ from the reference program's by a relative error of at most 0.0093.
Values may be sent and summed in bfloat16 or wider, within the bound.
No kernel may reach another device: no remote copies, remote signals or barrier semaphores. Data moves between devices by JAX's collectives and lax.ppermute only.
A program may use at most 256 MiB of HBM per device.

```python
import math
import jax
import jax.numpy as jnp
from jax import lax

D = 6144
FF = 24576
HEADS = 48
HEAD = 128
PATCHES = 256
CLASSES = 1000
MASKS = 8
BLOCK = 128
IMAGES = 1
ROWS = 256
BLOCKS = 48


def plant(result, rng, least, largest):
    shape = result.shape
    spot = [jax.random.randint(jax.random.fold_in(rng, axis), (), 0, shape[axis]) for axis in range(len(shape))]
    result = result.at[tuple(spot)].set(least)
    longest = shape.index(max(shape))
    spot[longest] = (spot[longest] + 1) % shape[longest]
    return result.at[tuple(spot)].set(largest)


def strengthened(array, rng, source, target, shards_of, factor):
    def block_of(axis_at):
        return (jnp.arange(array.shape[axis_at]) // (array.shape[axis_at] // shards_of)).reshape((-1,) + (1,) * (array.ndim - 1 - axis_at))

    near = jax.random.permutation(rng, shards_of)[block_of(target)]
    far = (block_of(target) + shards_of // 2) % shards_of
    return jnp.where((block_of(source) == near) | (block_of(source) == far), factor * array, array)


def shard_levels(stream_key, shape, cuts, low, largest):
    level, own = 1.0, jax.random.fold_in(stream_key, 6)
    for axis_at, blocks in cuts:
        steps = jnp.exp(jax.random.uniform(jax.random.fold_in(own, axis_at), (blocks,), jnp.float32, low / len(cuts), largest / len(cuts)))
        level = level * jnp.repeat(steps, shape[axis_at] // blocks).reshape([-1 if axis == axis_at else 1 for axis in range(len(shape))])
    return level


def scatter_about(rng, dims, scale, reach, pieces=(), kind=jnp.bfloat16):
    values = scale * jax.random.normal(rng, dims, jnp.float32)
    if pieces:
        values = values * shard_levels(rng, dims, pieces, -0.22, 0.18)
    return jnp.clip(values, -reach, reach).astype(kind)


def bell_draw_with(stream_key, shape, deviation, bound, split, heavy, dtype=jnp.bfloat16):
    array = deviation * jax.random.normal(stream_key, shape, jnp.float32)
    if split:
        array = array * shard_levels(stream_key, shape, split, -0.22, 0.18)
    return jnp.clip(strengthened(array, jax.random.fold_in(stream_key, 3), *heavy), -bound, bound).astype(dtype)


def setup_inputs(seed: int = 0, part: int = 0) -> dict:
    keys = jax.random.split(jax.random.key(seed), 12)
    own_keys = jax.random.split(jax.random.fold_in(keys[11], part), 12)
    return {
        "tokens": scatter_about(own_keys[0], (ROWS, D), 1.0, 6.0, ((0, 16),)),
        "dropout_masks": plant((jax.random.randint(own_keys[1], (MASKS, ROWS, BLOCKS), 0, 2) < 1).astype(jnp.int32), jax.random.fold_in(own_keys[1], 1), 0, 1),
        "input_gain": jnp.clip(1.0 + 0.1 * jax.random.normal(keys[2], (D,), jnp.float32), 0.5, 1.5),
        "w_qkv": scatter_about(keys[3], (HEAD, 3, HEADS, D), D ** -0.5, 0.078125, ((0, 16),)),
        "w_up": scatter_about(keys[4], (FF, D), D ** -0.5, 0.078125, ((0, 16),)),
        "query_gain": jnp.clip(1.0 + 0.18 * jax.random.normal(keys[5], (HEAD,), jnp.float32), 0.1, 1.9),
        "key_gain": jnp.clip(1.0 + 0.18 * jax.random.normal(keys[6], (HEAD,), jnp.float32), 0.1, 1.9),
        "w_proj": bell_draw_with(keys[7], (HEAD, HEADS, D), (HEADS * HEAD) ** -0.5, 0.109375, ((0, 16),), (0, 2, 16, 2.0)),
        "w_down": bell_draw_with(keys[8], (FF, D), FF ** -0.5, 0.0546875, ((0, 16),), (0, 1, 16, 2.0)),
        "final_gain": jnp.clip(1.0 + 0.1 * jax.random.normal(keys[9], (D,), jnp.float32), 0.5, 1.5),
        "w_head": scatter_about(keys[10], (D, CLASSES), (D // 64) ** -0.5, 0.625, ((0, 16),)),
    }


soft_cap = 20.0

def norm_last(values, gain):
    average = lax.optimization_barrier(jnp.mean(values, axis=-1, keepdims=True))
    centered = values - average
    spread_sq = lax.optimization_barrier(jnp.mean(centered * centered, axis=-1, keepdims=True))
    return centered * lax.rsqrt(spread_sq + 1e-06) * gain

def bald_score(logits):
    exp_logits = jnp.exp(logits)
    totals = lax.optimization_barrier(jnp.sum(exp_logits, axis=-1, keepdims=True))
    sample_probs = exp_logits / totals
    entropy = jnp.log(totals[..., 0]) - lax.optimization_barrier(jnp.sum(sample_probs * logits, axis=-1))
    mean_probs = lax.optimization_barrier(jnp.mean(sample_probs, axis=1))
    joint = -lax.optimization_barrier(jnp.sum(mean_probs * jnp.log(mean_probs), axis=-1))
    return joint - lax.optimization_barrier(jnp.mean(entropy, axis=1))

def reference(tokens, dropout_masks, input_gain, w_qkv, w_up, query_gain, key_gain, w_proj, w_down, final_gain, w_head):
    n_rows = IMAGES * PATCHES
    n_blocks = D // BLOCK
    qkv_cols = 3 * HEADS * HEAD
    n_cols = qkv_cols + FF
    highest = lax.Precision.HIGHEST
    tok_float = tokens.astype(jnp.float32)
    normed = norm_last(tok_float, input_gain).astype(jnp.bfloat16)
    joined_weight = jnp.concatenate([jnp.transpose(w_qkv, (1, 2, 0, 3)).reshape(qkv_cols, D), w_up], axis=0)
    normed_blocks = jnp.transpose(normed.reshape(n_rows, n_blocks, BLOCK), (1, 0, 2))
    weight_blocks = jnp.transpose(joined_weight.reshape(n_cols, n_blocks, BLOCK), (1, 2, 0))
    gate_blocks = jnp.transpose(dropout_masks, (2, 0, 1)).astype(jnp.float32)

    def add_block(totals, blocks_in):
        normed_part, weight_part, gate_part = blocks_in
        product = jnp.dot(normed_part, weight_part, preferred_element_type=jnp.float32)
        return (totals + gate_part[:, :, None] * product[None], None)
    start_totals = jnp.zeros((MASKS, n_rows, n_cols), jnp.float32)
    totals, ignored = lax.scan(add_block, start_totals, (normed_blocks, weight_blocks, gate_blocks))
    projected = 2.0 * totals
    qkv_values = projected[:, :, :qkv_cols].astype(jnp.bfloat16).reshape(MASKS, IMAGES, PATCHES, 3, HEADS, HEAD)
    activated = jax.nn.gelu(projected[:, :, qkv_cols:], approximate=False)
    pooled_hidden = lax.optimization_barrier(jnp.mean(activated.reshape(MASKS, IMAGES, PATCHES, FF), axis=2)).astype(jnp.bfloat16)
    queries = norm_last(qkv_values[:, :, :, 0].astype(jnp.float32), query_gain).astype(jnp.bfloat16)
    keys_normed = norm_last(qkv_values[:, :, :, 1].astype(jnp.float32), key_gain).astype(jnp.bfloat16)
    values_in = qkv_values[:, :, :, 2]
    scores = jnp.einsum('mipha,miqha->mihpq', queries.astype(jnp.float32), keys_normed.astype(jnp.float32), precision=highest) / math.sqrt(HEAD)
    exp_scores = jnp.exp(scores)
    weights = (exp_scores / lax.optimization_barrier(jnp.sum(exp_scores, axis=-1, keepdims=True))).astype(jnp.bfloat16)
    attended = jnp.einsum('mihpq,miqha->mipha', weights.astype(jnp.float32), values_in.astype(jnp.float32), precision=highest)
    pooled_attended = lax.optimization_barrier(jnp.mean(attended, axis=2)).astype(jnp.bfloat16)
    mixed_sum = jnp.einsum('miha,ahd->imd', pooled_attended.astype(jnp.float32), w_proj.astype(jnp.float32), precision=highest)
    mixed_sum = mixed_sum + jnp.einsum('mif,fd->imd', pooled_hidden.astype(jnp.float32), w_down.astype(jnp.float32), precision=highest)
    pooled_input = lax.optimization_barrier(jnp.mean(tok_float.reshape(IMAGES, PATCHES, D), axis=1))
    feature = pooled_input[:, None, :] + mixed_sum
    embedding = norm_last(feature, final_gain)
    embedding_half = embedding.astype(jnp.bfloat16)
    raw_logits = jnp.dot(embedding_half.reshape(IMAGES * MASKS, D), w_head, preferred_element_type=jnp.float32)
    logits = soft_cap * jnp.tanh(raw_logits.reshape(IMAGES, MASKS, CLASSES) / soft_cap)
    return (embedding, bald_score(logits))
```

```python
import functools
import math

import jax
import jax.numpy as jnp
from jax import lax
from jax.experimental import pallas as pl
from jax.experimental.pallas import tpu as pltpu
from jax.sharding import PartitionSpec as P

PATCHES = 256


soft_cap = 20.0
PIPELINED_PARTS = 16
CHUNKS = 4
F32 = jnp.float32
BF16 = jnp.bfloat16
VMEM_LIMIT = 60 * 1024 * 1024


def norm_last(values, gain):
    average = jnp.mean(values, axis=-1, keepdims=True)
    centered = values - average
    spread_sq = jnp.mean(centered * centered, axis=-1, keepdims=True)
    return centered * lax.rsqrt(spread_sq + 1e-06) * gain


def norm_second(values, gain):
    average = jnp.mean(values, axis=1, keepdims=True)
    centered = values - average
    spread_sq = jnp.mean(centered * centered, axis=1, keepdims=True)
    return centered * lax.rsqrt(spread_sq + 1e-06) * gain[None, :, None, None]


def bald_score(logits):
    exp_logits = jnp.exp(logits)
    totals = jnp.sum(exp_logits, axis=-1, keepdims=True)
    sample_probs = exp_logits / totals
    entropy = jnp.log(totals[..., 0]) - jnp.sum(sample_probs * logits, axis=-1)
    mean_probs = jnp.mean(sample_probs, axis=1)
    joint = -jnp.sum(mean_probs * jnp.log(mean_probs), axis=-1)
    return joint - jnp.mean(entropy, axis=1)


def permuted(array, bits):
    count = lax.axis_size("inp")
    return lax.ppermute(array, "inp", [(i, i ^ bits) for i in range(count)])


def gathered_pieces(rows):
    half = rows.shape[1] // 2
    first, second = rows[:, :half], rows[:, half:]
    along_z = jnp.stack([first] + [permuted(first, 4 * k) for k in range(1, 4)])
    across_y = permuted(along_z, 2)
    pieces = [
        (0, [4 * k for k in range(4)], along_z),
        (0, [4 * k + 2 for k in range(4)], across_y),
    ]
    pair = jnp.stack([second, permuted(second, 2)])
    for k in range(4):
        moved = pair if k == 0 else permuted(pair, 4 * k)
        pieces.append((1, [4 * k, 4 * k + 2], moved))
    return pieces + [
        (side, [b ^ 1 for b in bits], permuted(array, 1)) for side, bits, array in pieces
    ]


def turn_kernel(layout, me_ref, *refs):
    sources, out_ref, held = refs[:-2], refs[-2], refs[-1]
    me = me_ref[0]
    rows = sources[0].shape[1]
    half = sources[0].shape[2]
    for (side, bits), source in zip(layout, sources, strict=True):
        for at, bit in enumerate(bits):
            start = pl.multiple_of((me ^ bit) * rows, rows)
            held[pl.ds(start, rows), side * half : (side + 1) * half] = source[at]
    for block in range(2 * half // 128):
        part = held[:, block * 128 : (block + 1) * 128].astype(F32)
        out_ref[block * 128 : (block + 1) * 128, :] = part.T.astype(BF16)


def turned(pieces, me):
    rows, half = pieces[0][2].shape[1:]
    total = rows * sum(len(bits) for side, bits, _ in pieces if side == 0)
    layout = [(side, bits) for side, bits, _ in pieces]
    return pl.pallas_call(
        functools.partial(turn_kernel, layout),
        out_shape=jax.ShapeDtypeStruct((2 * half, total), BF16),
        in_specs=[pl.BlockSpec(memory_space=pltpu.SMEM)]
        + [pl.BlockSpec(memory_space=pltpu.VMEM)] * len(pieces),
        out_specs=pl.BlockSpec(memory_space=pltpu.VMEM),
        scratch_shapes=[pltpu.VMEM((total, 2 * half), BF16)],
        compiler_params=pltpu.CompilerParams(vmem_limit_bytes=VMEM_LIMIT),
        name="turn_rows",
    )(me.reshape(1), *[array for _, _, array in pieces])


def store_masked(norm_ref, gates_ref, masked, first_block, blocks, samples, rows):
    for block in range(blocks):
        values = norm_ref[block * 128 : (block + 1) * 128, :].reshape(8, 16, rows)
        for m in range(samples):
            gate = gates_ref[m, pl.ds(first_block + block, 1), :]
            gate = jnp.broadcast_to(gate, (16, rows)).astype(BF16)
            masked[block * 128 : (block + 1) * 128, m * rows : (m + 1) * rows] = (
                values * gate[None]
            ).reshape(128, rows)


def query_key_kernel(samples, norm_ref, gates_ref, w_ref, out_ref, masked, total):
    step = pl.program_id(0)
    depth, rows = norm_ref.shape
    blocks = depth // 128
    comps, kinds, heads, _ = w_ref.shape
    store_masked(norm_ref, gates_ref, masked, step * blocks, blocks, samples, rows)
    weight = w_ref[...].reshape(comps * kinds * heads, depth)

    @pl.when(step == 0)
    def _():
        total[...] = jnp.zeros_like(total)

    for m in range(samples):
        product = jnp.dot(
            weight, masked[:, m * rows : (m + 1) * rows], preferred_element_type=F32
        )
        for part in range(rows // 128):
            total[m * (rows // 128) + part] += product[:, part * 128 : (part + 1) * 128]

    @pl.when(step == pl.num_programs(0) - 1)
    def _():
        stride = kinds * heads
        for h in range(heads):
            for tile in range(samples * rows // 128):
                both = [
                    total.at[tile][pl.ds(t * heads + h, comps, stride=stride), :]
                    for t in range(kinds)
                ]
                m, part = divmod(tile, rows // 128)
                out_ref[h, m, :, part * 128 : (part + 1) * 128] = jnp.concatenate(
                    both, axis=0
                ).astype(BF16)


def query_key(norm, gates, w_qkv, first, samples):
    width, rows = norm.shape
    comps, _, heads, _ = w_qkv.shape
    depth = 1024
    return pl.pallas_call(
        functools.partial(query_key_kernel, samples),
        grid=(width // depth,),
        out_shape=jax.ShapeDtypeStruct((heads, samples, 2 * comps, rows), BF16),
        in_specs=[
            pl.BlockSpec((depth, rows), lambda k: (k, 0)),
            pl.BlockSpec((samples, gates.shape[1], rows), lambda k: (first // samples, 0, 0)),
            pl.BlockSpec((comps, 2, heads, depth), lambda k: (0, 0, 0, k)),
        ],
        out_specs=pl.BlockSpec((heads, samples, 2 * comps, rows), lambda k: (0, 0, 0, 0)),
        scratch_shapes=[
            pltpu.VMEM((depth, samples * rows), BF16),
            pltpu.VMEM((samples * rows // 128, 2 * comps * heads, 128), F32),
        ],
        compiler_params=pltpu.CompilerParams(vmem_limit_bytes=VMEM_LIMIT),
        cost_estimate=pl.CostEstimate(
            flops=2 * samples * rows * width * 2 * comps * heads,
            bytes_accessed=2 * (norm.size + 2 * comps * heads * width),
            transcendentals=0,
        ),
        name="query_key",
    )(norm, gates, w_qkv)


def value_kernel(samples, norm_ref, gates_ref, w_ref, out_ref, masked, total):
    step = pl.program_id(0)
    depth, rows = norm_ref.shape
    blocks = depth // 128
    comps, _, heads, _ = w_ref.shape
    store_masked(norm_ref, gates_ref, masked, step * blocks, blocks, samples, rows)
    weight = w_ref[:, 0].reshape(comps * heads, depth)

    @pl.when(step == 0)
    def _():
        total[...] = jnp.zeros_like(total)

    for m in range(samples):
        at = slice(m * rows, (m + 1) * rows)
        total[:, at] += jnp.dot(weight, masked[:, at], preferred_element_type=F32)

    @pl.when(step == pl.num_programs(0) - 1)
    def _():
        for m in range(samples):
            out_ref[m] = total[:, m * rows : (m + 1) * rows].astype(BF16)


def values_of(norm, gates, w_qkv):
    width, rows = norm.shape
    samples = gates.shape[0]
    comps, _, heads, _ = w_qkv.shape
    depth = 1024
    return pl.pallas_call(
        functools.partial(value_kernel, samples),
        grid=(width // depth,),
        out_shape=jax.ShapeDtypeStruct((samples, comps * heads, rows), BF16),
        in_specs=[
            pl.BlockSpec((depth, rows), lambda k: (k, 0)),
            pl.BlockSpec(gates.shape, lambda k: (0, 0, 0)),
            pl.BlockSpec((comps, 1, heads, depth), lambda k: (0, 2, 0, k)),
        ],
        out_specs=pl.BlockSpec((samples, comps * heads, rows), lambda k: (0, 0, 0)),
        scratch_shapes=[
            pltpu.VMEM((depth, samples * rows), BF16),
            pltpu.VMEM((comps * heads, samples * rows), F32),
        ],
        compiler_params=pltpu.CompilerParams(vmem_limit_bytes=VMEM_LIMIT),
        cost_estimate=pl.CostEstimate(
            flops=2 * samples * rows * width * comps * heads,
            bytes_accessed=2 * (norm.size + comps * heads * width),
            transcendentals=0,
        ),
        name="value_rows",
    )(norm, gates, w_qkv)


def erf(x):
    x = jnp.clip(x, -4.0, 4.0)
    s = x * x
    top = s * -2.72614225801306e-10 + 2.77068142495902e-08
    for c in (
        -2.10102402082508e-06,
        -5.69250639462346e-05,
        -7.34990630326855e-04,
        -2.95459980854025e-03,
        -1.60960333262415e-02,
    ):
        top = top * s + c
    low = s * -1.45660718464996e-05 + -2.13374055278905e-04
    for c in (-1.68282697438203e-03, -7.37332916720468e-03, -1.42647390514189e-02):
        low = low * s + c
    return x * top / low


def hidden_kernel(samples, norm_ref, gates_ref, up_ref, down_ref, out_ref, masked, even, odd, sums):
    step = pl.program_id(0)
    width, rows = norm_ref.shape
    lane = lax.broadcasted_iota(jnp.int32, sums.shape, 1)

    @pl.when(step == 0)
    def _():
        out_ref[...] = jnp.zeros_like(out_ref)

        @pl.loop(0, width // 128)
        def _(block):
            start = pl.multiple_of(block * 128, 128)
            values = norm_ref[pl.ds(start, 128), :].reshape(8, 16, rows)
            for m in range(samples):
                gate = jnp.broadcast_to(gates_ref[m, pl.ds(block, 1), :], (16, rows))
                masked[m, pl.ds(start, 128), :] = (values * gate.astype(BF16)[None]).reshape(
                    128, rows
                )

    def pool(held, m):
        v = held[...]
        active = (0.5 * v) * (1.0 + erf(v * math.sqrt(0.5)))
        pooled = jnp.sum(active, axis=1, keepdims=True) * (1.0 / rows)
        sums[...] = jnp.where(lane == m, pooled, sums[...])

    odd[...] = jnp.zeros_like(odd)
    sums[...] = jnp.zeros_like(sums)

    @pl.loop(0, samples // 2)
    def _(pair):
        even[...] = jnp.dot(up_ref[...], masked[2 * pair], preferred_element_type=F32)
        pool(odd, 2 * pair - 1)
        odd[...] = jnp.dot(up_ref[...], masked[2 * pair + 1], preferred_element_type=F32)
        pool(even, 2 * pair)

    pool(odd, samples - 1)
    pooled = sums[...].T[:16].astype(BF16)
    out_ref[...] += jnp.dot(pooled, down_ref[...], preferred_element_type=F32)[:samples]


def hidden_part(norm, gates, w_up, w_down):
    width, rows = norm.shape
    samples = gates.shape[0]
    units = w_up.shape[0]
    tile = 256
    return pl.pallas_call(
        functools.partial(hidden_kernel, samples),
        grid=(units // tile,),
        out_shape=jax.ShapeDtypeStruct((samples, width), F32),
        in_specs=[
            pl.BlockSpec(norm.shape, lambda i: (0, 0)),
            pl.BlockSpec(gates.shape, lambda i: (0, 0, 0)),
            pl.BlockSpec((tile, width), lambda i: (i, 0)),
            pl.BlockSpec((tile, width), lambda i: (i, 0)),
        ],
        out_specs=pl.BlockSpec((samples, width), lambda i: (0, 0)),
        scratch_shapes=[
            pltpu.VMEM((samples, width, rows), BF16),
            pltpu.VMEM((tile, rows), F32),
            pltpu.VMEM((tile, rows), F32),
            pltpu.VMEM((tile, 128), F32),
        ],
        compiler_params=pltpu.CompilerParams(vmem_limit_bytes=VMEM_LIMIT),
        cost_estimate=pl.CostEstimate(
            flops=2 * samples * rows * width * units,
            bytes_accessed=2 * (norm.size + 2 * units * width),
            transcendentals=samples * rows * units,
        ),
        name="hidden_part",
    )(norm, gates, w_up, w_down)


def attention_kernel(items, x_ref, query_gain_ref, key_gain_ref, out_ref):
    parts, _, both, rows = x_ref.shape
    comps = both // 2
    head_dim = parts * comps

    def normed(values, gain_ref):
        values = values.reshape(head_dim, rows)
        average = jnp.mean(values, axis=0, keepdims=True)
        centered = values - average
        spread_sq = jnp.mean(centered * centered, axis=0, keepdims=True)
        return (centered * lax.rsqrt(spread_sq + 1e-06) * gain_ref[...]).astype(BF16)

    for j in range(items):
        x = x_ref[:, j].astype(F32)
        query = normed(x[:, :comps], query_gain_ref)
        key = normed(x[:, comps:], key_gain_ref)
        scores = lax.dot_general(
            query, key, (((0,), (0,)), ((), ())), preferred_element_type=F32
        ) * (1.0 / math.sqrt(head_dim))
        e = jnp.exp(scores)
        weights = (e / jnp.sum(e, axis=1, keepdims=True)).astype(BF16)
        out_ref[j : j + 1, :] = jnp.sum(weights.astype(F32), axis=0, keepdims=True) * (1.0 / rows)


def key_weights(exchanged, query_gain, key_gain):
    parts, items, both, rows = exchanged.shape
    head_dim = parts * both // 2
    return pl.pallas_call(
        functools.partial(attention_kernel, items),
        out_shape=jax.ShapeDtypeStruct((items, rows), F32),
        compiler_params=pltpu.CompilerParams(vmem_limit_bytes=VMEM_LIMIT),
        cost_estimate=pl.CostEstimate(
            flops=2 * items * rows * rows * head_dim,
            bytes_accessed=2 * exchanged.size,
            transcendentals=items * rows * rows,
        ),
        name="key_weights",
    )(exchanged, query_gain.reshape(head_dim, 1), key_gain.reshape(head_dim, 1))


def pooled_logits(feature, final_gain, w_head):
    highest = lax.Precision.HIGHEST
    gain_head = jnp.dot(final_gain[None], w_head.astype(F32), precision=highest)
    mean = jnp.mean(feature, axis=-1, keepdims=True)
    centered = feature - mean
    spread = jnp.sum(centered * centered, axis=-1, keepdims=True)
    logits = jnp.dot(centered * final_gain, w_head.astype(F32), precision=highest)
    columns = feature.shape[1]
    samples, classes = logits.shape
    bits = 1
    while bits < lax.axis_size("inp"):
        sent = jnp.concatenate(
            [
                jnp.concatenate([logits, mean, spread], axis=1),
                jnp.pad(gain_head, ((0, 0), (0, 2))),
            ],
            axis=0,
        )
        other = permuted(sent, bits)
        other_mean = other[:samples, classes : classes + 1]
        joint = 0.5 * (mean + other_mean)
        logits = (
            logits
            + other[:samples, :classes]
            + (mean - joint) * gain_head
            + (other_mean - joint) * other[samples:, :classes]
        )
        gap = mean - other_mean
        spread = spread + other[:samples, classes + 1 :] + gap * gap * (0.5 * columns)
        gain_head = gain_head + other[samples:, :classes]
        mean = joint
        columns = 2 * columns
        bits = 2 * bits
    scale = lax.rsqrt(spread / columns + 1e-06)
    return mean, scale, logits * scale


def pipelined(
    tokens,
    dropout_masks,
    input_gain,
    w_qkv,
    w_up,
    query_gain,
    key_gain,
    w_proj,
    w_down,
    final_gain,
    w_head,
):
    n_parts = lax.axis_size("inp")
    me = lax.axis_index("inp")
    model_width = tokens.shape[1]
    n_masks, all_rows, _ = dropout_masks.shape
    n_comps, _, n_heads, _ = w_qkv.shape
    own = norm_last(tokens.astype(F32), input_gain).astype(BF16)
    gates = 2.0 * jnp.transpose(dropout_masks, (0, 2, 1)).astype(F32)
    norm = turned(gathered_pieces(own), me)
    samples = n_masks // CHUNKS
    heads_dev = n_heads // n_parts
    items = heads_dev * samples
    exchanged = []
    for chunk in range(CHUNKS):
        both = query_key(norm, gates, w_qkv, chunk * samples, samples)
        both = both.reshape(n_parts, items, 2 * n_comps, all_rows)
        exchanged.append(lax.all_to_all(both, "inp", split_axis=0, concat_axis=0, tiled=True))
    value = values_of(norm, gates, w_qkv)
    hidden = hidden_part(norm, gates, w_up, w_down)
    key_mean = jnp.concatenate([key_weights(x, query_gain, key_gain) for x in exchanged], axis=0)
    key_mean = lax.all_to_all(
        jnp.broadcast_to(key_mean[None], (n_parts,) + key_mean.shape),
        "inp",
        split_axis=0,
        concat_axis=0,
        tiled=True,
    )
    key_mean = key_mean.reshape(n_parts, CHUNKS, heads_dev, samples, all_rows)
    key_mean = jnp.transpose(key_mean, (1, 3, 0, 2, 4)).reshape(n_masks, 1, n_heads, all_rows)
    value = value.reshape(n_masks, n_comps, n_heads, all_rows).astype(F32)
    attended = jnp.sum(value * key_mean, axis=-1).astype(BF16).reshape(n_masks, n_comps * n_heads)
    mixed_sum = jnp.dot(
        attended, w_proj.reshape(n_comps * n_heads, model_width), preferred_element_type=F32
    )
    input_sum = jnp.sum(tokens.astype(F32), axis=0, keepdims=True) / all_rows
    partial_feature = mixed_sum + hidden + input_sum
    slice_width = model_width // n_parts
    feature = jnp.sum(
        lax.all_to_all(
            partial_feature.reshape(n_masks, n_parts, slice_width),
            "inp",
            split_axis=1,
            concat_axis=0,
            tiled=True,
        ).reshape(n_parts, n_masks, slice_width),
        axis=0,
    )
    gain = lax.dynamic_slice_in_dim(final_gain, me * slice_width, slice_width, 0)
    mean, scale, raw_logits = pooled_logits(feature, gain, w_head)
    embedding = (feature - mean) * scale * gain
    logits = soft_cap * jnp.tanh(raw_logits / soft_cap)
    return (embedding[None], bald_score(logits[None]))


def local(
    tokens,
    dropout_masks,
    input_gain,
    w_qkv,
    w_up,
    query_gain,
    key_gain,
    w_proj,
    w_down,
    final_gain,
    w_head,
):
    n_parts = lax.axis_size("inp")
    local_rows, model_width = tokens.shape
    n_masks, all_rows, n_blocks = dropout_masks.shape
    block_width = model_width // n_blocks
    n_comps, three_kinds, n_heads, ignored_width = w_qkv.shape
    n_units = w_up.shape[0]
    head_dim = n_comps * n_parts
    images = all_rows // PATCHES
    qkv_cols = three_kinds * n_heads * n_comps
    items_dev = n_masks * n_heads // n_parts
    highest = lax.Precision.HIGHEST
    joined_weight = jnp.concatenate(
        [jnp.transpose(w_qkv, (1, 2, 0, 3)).reshape(qkv_cols, model_width), w_up], axis=0
    )
    row_piece = lax.all_gather(tokens, "inp", axis=0, tiled=True)
    row_count = row_piece.shape[0]
    normed = norm_last(row_piece.astype(jnp.float32), input_gain).astype(jnp.bfloat16)
    masked = (
        normed.reshape(1, row_count, n_blocks, block_width)
        * dropout_masks.astype(jnp.bfloat16)[..., None]
    )
    masked = masked.reshape(n_masks, row_count, model_width)
    result = jnp.einsum("mkd,cd->mck", masked, joined_weight, preferred_element_type=jnp.float32)
    projected = 2.0 * result
    qkv_half = (
        projected[:, :qkv_cols]
        .astype(jnp.bfloat16)
        .reshape(n_masks, three_kinds, n_heads * n_comps, all_rows)
    )
    item_shape = (n_parts, items_dev, n_comps, all_rows)
    query_send = qkv_half[:, 0].reshape(item_shape)
    key_send = qkv_half[:, 1].reshape(item_shape)
    value_send = qkv_half[:, 2].reshape(item_shape)
    activated = jax.nn.gelu(projected[:, qkv_cols:], approximate=False)
    pooled_hidden = jnp.mean(activated.reshape(n_masks, n_units, images, PATCHES), axis=-1).astype(
        jnp.bfloat16
    )
    query_in = lax.all_to_all(query_send, "inp", split_axis=0, concat_axis=2, tiled=True)
    key_in = lax.all_to_all(key_send, "inp", split_axis=0, concat_axis=2, tiled=True)
    value_in = lax.all_to_all(value_send, "inp", split_axis=0, concat_axis=2, tiled=True)
    n_items = query_in.shape[1]
    shape_four = (n_items, head_dim, images, PATCHES)
    query_norm = norm_second(query_in.reshape(shape_four).astype(jnp.float32), query_gain).astype(
        jnp.bfloat16
    )
    key_norm = norm_second(key_in.reshape(shape_four).astype(jnp.float32), key_gain).astype(
        jnp.bfloat16
    )
    scores = jnp.einsum(
        "jcip,jciq->jipq", query_norm, key_norm, preferred_element_type=jnp.float32
    ) / math.sqrt(head_dim)
    exp_scores = jnp.exp(scores)
    weights = (exp_scores / jnp.sum(exp_scores, axis=-1, keepdims=True)).astype(jnp.bfloat16)
    query_mean = jnp.sum(weights, axis=2, dtype=jnp.float32) / PATCHES
    pooled = jnp.einsum(
        "jiq,jciq->jic",
        query_mean,
        value_in.reshape(shape_four).astype(jnp.float32),
        precision=highest,
    )
    attended = pooled.astype(jnp.bfloat16)[None]
    returned = lax.all_to_all(attended, "inp", split_axis=3, concat_axis=0, tiled=True)
    returned = returned.reshape(n_masks, n_heads, images, n_comps)
    mixed_sum = jnp.einsum("mhic,chd->imd", returned, w_proj, preferred_element_type=jnp.float32)
    mixed_sum = mixed_sum + jnp.einsum(
        "mfi,fd->imd", pooled_hidden, w_down, preferred_element_type=jnp.float32
    )
    row_ids = lax.axis_index("inp") * local_rows + jnp.arange(local_rows, dtype=jnp.int32)
    row_owner = (row_ids // PATCHES)[None, :] == jnp.arange(images, dtype=jnp.int32)[:, None]
    input_sum = (
        jnp.dot(row_owner.astype(jnp.bfloat16), tokens, preferred_element_type=jnp.float32)
        / PATCHES
    )
    partial_feature = mixed_sum + input_sum[:, None, :]
    feature = lax.psum(partial_feature, "inp")
    normalized = norm_last(feature, final_gain)
    slice_width = model_width // n_parts
    embedding = lax.dynamic_slice_in_dim(
        normalized, lax.axis_index("inp") * slice_width, slice_width, 2
    )
    logit_part = jnp.einsum(
        "imd,dc->imc", embedding.astype(jnp.bfloat16), w_head, preferred_element_type=jnp.float32
    )
    raw_logits = lax.psum(logit_part, "inp")
    logits = soft_cap * jnp.tanh(raw_logits / soft_cap)
    return (embedding, bald_score(logits))


def solution(mesh):
    fits = mesh.shape["inp"] == PIPELINED_PARTS
    return jax.shard_map(
        pipelined if fits else local,
        mesh=mesh,
        in_specs=(
            P(("groups", "inp"), None),
            P(None, "groups", None),
            P(),
            P("inp", None, None, None),
            P("inp", None),
            P(),
            P(),
            P("inp", None, None),
            P("inp", None),
            P(),
            P("inp", None),
        ),
        out_specs=(P("groups", None, "inp"), P("groups")),
        check_vma=False,
    )
```

```python
import functools
import math

import jax
import jax.numpy as jnp
from jax import lax
from jax.experimental import pallas as pl
from jax.experimental.pallas import tpu as pltpu
from jax.sharding import PartitionSpec as P

PATCHES = 256


soft_cap = 20.0
PIPELINED_PARTS = 16
UNITS = 512
F32 = jnp.float32
BF16 = jnp.bfloat16
VMEM_LIMIT = 60 * 1024 * 1024


def norm_last(values, gain):
    average = jnp.mean(values, axis=-1, keepdims=True)
    centered = values - average
    spread_sq = jnp.mean(centered * centered, axis=-1, keepdims=True)
    return centered * lax.rsqrt(spread_sq + 1e-06) * gain


def norm_second(values, gain):
    average = jnp.mean(values, axis=1, keepdims=True)
    centered = values - average
    spread_sq = jnp.mean(centered * centered, axis=1, keepdims=True)
    return centered * lax.rsqrt(spread_sq + 1e-06) * gain[None, :, None, None]


def bald_score(logits):
    exp_logits = jnp.exp(logits)
    totals = jnp.sum(exp_logits, axis=-1, keepdims=True)
    sample_probs = exp_logits / totals
    entropy = jnp.log(totals[..., 0]) - jnp.sum(sample_probs * logits, axis=-1)
    mean_probs = jnp.mean(sample_probs, axis=1)
    joint = -jnp.sum(mean_probs * jnp.log(mean_probs), axis=-1)
    return joint - jnp.mean(entropy, axis=1)


def permuted(array, bits):
    count = lax.axis_size("inp")
    return lax.ppermute(array, "inp", [(i, i ^ bits) for i in range(count)])


def gathered_pieces(rows):
    half = rows.shape[1] // 2
    first, second = rows[:, :half], rows[:, half:]
    along_z = jnp.stack([first] + [permuted(first, 4 * k) for k in range(1, 4)])
    across_y = permuted(along_z, 2)
    pieces = [
        (0, [4 * k for k in range(4)], along_z),
        (0, [4 * k + 2 for k in range(4)], across_y),
    ]
    pair = jnp.stack([second, permuted(second, 2)])
    for k in range(4):
        moved = pair if k == 0 else permuted(pair, 4 * k)
        pieces.append((1, [4 * k, 4 * k + 2], moved))
    return pieces + [
        (side, [b ^ 1 for b in bits], permuted(array, 1)) for side, bits, array in pieces
    ]


def place_kernel(layout, me_ref, *refs):
    sources, out_ref = refs[:-1], refs[-1]
    me = me_ref[0]
    rows, half = sources[0].shape[1:]
    for (side, bits), source in zip(layout, sources, strict=True):
        for at, bit in enumerate(bits):
            start = pl.multiple_of((me ^ bit) * rows, rows)
            out_ref[pl.ds(start, rows), side * half : (side + 1) * half] = source[at]


def placed(pieces, me):
    rows, half = pieces[0][2].shape[1:]
    total = rows * sum(len(bits) for side, bits, _ in pieces if side == 0)
    layout = [(side, bits) for side, bits, _ in pieces]
    return pl.pallas_call(
        functools.partial(place_kernel, layout),
        out_shape=jax.ShapeDtypeStruct((total, 2 * half), BF16),
        in_specs=[pl.BlockSpec(memory_space=pltpu.SMEM)]
        + [pl.BlockSpec(memory_space=pltpu.VMEM)] * len(pieces),
        out_specs=pl.BlockSpec(memory_space=pltpu.VMEM),
        compiler_params=pltpu.CompilerParams(vmem_limit_bytes=VMEM_LIMIT),
        name="place_rows",
    )(me.reshape(1), *[array for _, _, array in pieces])


ACROSS = (((1,), (1,)), ((), ()))
TILE = 16
BLOCK = 128


def choosers(dropout_masks):
    samples, rows, blocks = dropout_masks.shape
    tiles = rows // TILE
    kept = dropout_masks.astype(BF16).reshape(samples, tiles, TILE, blocks)
    kept = jnp.transpose(kept, (1, 0, 2, 3)).reshape(tiles, samples * TILE, blocks)
    column = jnp.arange(blocks * TILE)
    spread = (column[None] // TILE == jnp.arange(blocks)[:, None]).astype(BF16)
    own = jnp.arange(samples * TILE)[:, None] % TILE == column[None] % TILE
    wide = jnp.einsum("trb,bc->trc", kept, spread, preferred_element_type=F32)
    return jnp.where(own[None], 2.0 * wide, 0.0).astype(BF16)


def block_products(norm_ref, weight, products, first):
    for j in range(weight.shape[1] // BLOCK):
        at = slice(j * BLOCK, (j + 1) * BLOCK)
        products[first + j] = lax.dot_general(
            norm_ref[:, at], weight[:, at], ACROSS, preferred_element_type=F32
        ).astype(BF16)


def summed(choose_ref, products, tile):
    blocks, _, columns = products.shape
    part = products[:, tile * TILE : (tile + 1) * TILE, :].reshape(blocks * TILE, columns)
    return jnp.dot(choose_ref[tile], part, preferred_element_type=F32)


def query_key_kernel(norm_ref, choose_ref, w_ref, out_ref, products, sums, turned):
    step = pl.program_id(0)
    rows, depth = norm_ref.shape
    comps, kinds, heads, _ = w_ref.shape
    columns = comps * kinds * heads
    block_products(
        norm_ref, w_ref[...].reshape(columns, depth), products, step * (depth // BLOCK)
    )

    @pl.when(step == pl.num_programs(0) - 1)
    def _():
        samples = sums.shape[0]
        for tile in range(rows // TILE):
            sums[:, tile * TILE : (tile + 1) * TILE, :] = summed(
                choose_ref, products, tile
            ).reshape(samples, TILE, columns)
        for m in range(samples):
            for part in range(rows // 128):
                at = slice(part * 128, (part + 1) * 128)
                turned[m * (rows // 128) + part] = sums[m, at, :].T
            for part in range(rows // 128):
                at = slice(part * 128, (part + 1) * 128)
                held = turned.at[m * (rows // 128) + part]
                for h in range(heads):
                    both = [
                        held[pl.ds(t * heads + h, comps, stride=kinds * heads), :]
                        for t in range(kinds)
                    ]
                    out_ref[h, m, :, at] = jnp.concatenate(both, axis=0).astype(BF16)


def query_key(norm, choose, w_qkv, chunk, heads):
    rows, width = norm.shape
    samples = choose.shape[1] // TILE
    comps = w_qkv.shape[0]
    depth = 1024
    columns = 2 * comps * heads
    shape = (heads, samples, 2 * comps, rows)
    return pl.pallas_call(
        query_key_kernel,
        grid=(width // depth,),
        out_shape=jax.ShapeDtypeStruct(shape, BF16),
        in_specs=[
            pl.BlockSpec((rows, depth), lambda k: (0, k)),
            pl.BlockSpec(choose.shape, lambda k: (0, 0, 0)),
            pl.BlockSpec((comps, 2, heads, depth), lambda k: (0, 0, chunk, k)),
        ],
        out_specs=pl.BlockSpec(shape, lambda k: (0, 0, 0, 0)),
        scratch_shapes=[
            pltpu.VMEM((width // BLOCK, rows, columns), BF16),
            pltpu.VMEM((samples, rows, columns), F32),
            pltpu.VMEM((samples * rows // 128, columns, 128), F32),
        ],
        compiler_params=pltpu.CompilerParams(vmem_limit_bytes=VMEM_LIMIT),
        cost_estimate=pl.CostEstimate(
            flops=8 * rows * width * columns,
            bytes_accessed=2 * (norm.size + choose.size + columns * width),
            transcendentals=0,
        ),
        name="query_key",
    )(norm, choose, w_qkv)


def value_kernel(norm_ref, choose_ref, w_ref, out_ref, products):
    step = pl.program_id(0)
    rows, depth = norm_ref.shape
    comps, _, heads, _ = w_ref.shape
    block_products(
        norm_ref, w_ref[:, 0].reshape(comps * heads, depth), products, step * (depth // BLOCK)
    )

    @pl.when(step == pl.num_programs(0) - 1)
    def _():
        samples = out_ref.shape[0]
        for tile in range(rows // TILE):
            out_ref[:, tile * TILE : (tile + 1) * TILE, :] = (
                summed(choose_ref, products, tile)
                .reshape(samples, TILE, comps * heads)
                .astype(BF16)
            )


def values_of(norm, choose, w_qkv):
    rows, width = norm.shape
    samples = choose.shape[1] // TILE
    comps, _, heads, _ = w_qkv.shape
    depth = 1024
    columns = comps * heads
    return pl.pallas_call(
        value_kernel,
        grid=(width // depth,),
        out_shape=jax.ShapeDtypeStruct((samples, rows, columns), BF16),
        in_specs=[
            pl.BlockSpec((rows, depth), lambda k: (0, k)),
            pl.BlockSpec(choose.shape, lambda k: (0, 0, 0)),
            pl.BlockSpec((comps, 1, heads, depth), lambda k: (0, 2, 0, k)),
        ],
        out_specs=pl.BlockSpec((samples, rows, columns), lambda k: (0, 0, 0)),
        scratch_shapes=[pltpu.VMEM((width // BLOCK, rows, columns), BF16)],
        compiler_params=pltpu.CompilerParams(vmem_limit_bytes=VMEM_LIMIT),
        cost_estimate=pl.CostEstimate(
            flops=8 * rows * width * columns,
            bytes_accessed=2 * (norm.size + choose.size + columns * width),
            transcendentals=0,
        ),
        name="value_rows",
    )(norm, choose, w_qkv)


def erf(x):
    x = jnp.clip(x, -4.0, 4.0)
    s = x * x
    top = s * -2.72614225801306e-10 + 2.77068142495902e-08
    for c in (
        -2.10102402082508e-06,
        -5.69250639462346e-05,
        -7.34990630326855e-04,
        -2.95459980854025e-03,
        -1.60960333262415e-02,
    ):
        top = top * s + c
    low = s * -1.45660718464996e-05 + -2.13374055278905e-04
    for c in (-1.68282697438203e-03, -7.37332916720468e-03, -1.42647390514189e-02):
        low = low * s + c
    return x * top / low


def hidden_kernel(norm_ref, choose_ref, up_ref, down_ref, out_ref, products, pooled):
    unit_tile, step = pl.program_id(0), pl.program_id(1)
    rows, depth = norm_ref.shape
    samples, units = pooled.shape
    block_products(norm_ref, up_ref, products, step * (depth // BLOCK))

    @pl.when(step == pl.num_programs(1) - 1)
    def _():
        pooled[...] = jnp.zeros_like(pooled)
        for tile in range(rows // TILE):
            v = summed(choose_ref, products, tile)
            active = (0.5 * v) * (1.0 + erf(v * math.sqrt(0.5)))
            pooled[...] += jnp.sum(active.reshape(samples, TILE, units), axis=1)
        mean = pooled[...] * (1.0 / rows)
        mean = jnp.concatenate([mean, jnp.zeros_like(mean)], axis=0).astype(BF16)
        part = jnp.dot(mean, down_ref[...], preferred_element_type=F32)[:samples]

        @pl.when(unit_tile == 0)
        def _():
            out_ref[...] = part

        @pl.when(unit_tile > 0)
        def _():
            out_ref[...] += part


def hidden_part(norm, choose, w_up, w_down, first, tiles, units):
    rows, width = norm.shape
    samples = choose.shape[1] // TILE
    depth = 1024
    return pl.pallas_call(
        hidden_kernel,
        grid=(tiles, width // depth),
        out_shape=jax.ShapeDtypeStruct((samples, width), F32),
        in_specs=[
            pl.BlockSpec((rows, depth), lambda i, k: (0, k)),
            pl.BlockSpec(choose.shape, lambda i, k: (0, 0, 0)),
            pl.BlockSpec((units, depth), lambda i, k: (first + i, k)),
            pl.BlockSpec((units, width), lambda i, k: (first + i, 0)),
        ],
        out_specs=pl.BlockSpec((samples, width), lambda i, k: (0, 0)),
        scratch_shapes=[
            pltpu.VMEM((width // BLOCK, rows, units), BF16),
            pltpu.VMEM((samples, units), F32),
        ],
        compiler_params=pltpu.CompilerParams(vmem_limit_bytes=VMEM_LIMIT),
        cost_estimate=pl.CostEstimate(
            flops=8 * rows * width * units * tiles,
            bytes_accessed=2 * (norm.size + choose.size + 2 * units * tiles * width),
            transcendentals=samples * rows * units * tiles,
        ),
        name="hidden_part",
    )(norm, choose, w_up, w_down)


def attention_kernel(items, x_ref, query_gain_ref, key_gain_ref, out_ref):
    parts, _, both, rows = x_ref.shape
    comps = both // 2
    head_dim = parts * comps

    def normed(values, gain_ref):
        values = values.reshape(head_dim, rows)
        average = jnp.mean(values, axis=0, keepdims=True)
        centered = values - average
        spread_sq = jnp.mean(centered * centered, axis=0, keepdims=True)
        return (centered * lax.rsqrt(spread_sq + 1e-06) * gain_ref[...]).astype(BF16)

    for j in range(items):
        x = x_ref[:, j].astype(F32)
        query = normed(x[:, :comps], query_gain_ref)
        key = normed(x[:, comps:], key_gain_ref)
        scores = lax.dot_general(
            query, key, (((0,), (0,)), ((), ())), preferred_element_type=F32
        ) * (1.0 / math.sqrt(head_dim))
        e = jnp.exp(scores)
        weights = (e / jnp.sum(e, axis=1, keepdims=True)).astype(BF16)
        out_ref[j : j + 1, :] = jnp.sum(weights.astype(F32), axis=0, keepdims=True) * (1.0 / rows)


def key_weights(exchanged, query_gain, key_gain):
    parts, items, both, rows = exchanged.shape
    head_dim = parts * both // 2
    return pl.pallas_call(
        functools.partial(attention_kernel, items),
        out_shape=jax.ShapeDtypeStruct((items, rows), F32),
        compiler_params=pltpu.CompilerParams(vmem_limit_bytes=VMEM_LIMIT),
        cost_estimate=pl.CostEstimate(
            flops=2 * items * rows * rows * head_dim,
            bytes_accessed=2 * exchanged.size,
            transcendentals=items * rows * rows,
        ),
        name="key_weights",
    )(exchanged, query_gain.reshape(head_dim, 1), key_gain.reshape(head_dim, 1))


def feature_kernel(key_ref, value_ref, proj_ref, hidden_refs, token_ref, out_ref, attended):
    step = pl.program_id(0)
    parts, pieces, _ = key_ref.shape
    samples, rows, columns = value_ref.shape
    chunks = pieces // samples
    heads = parts * chunks

    @pl.when(step == 0)
    def _():
        row = lax.broadcasted_iota(jnp.int32, (heads, columns), 0)
        column = lax.broadcasted_iota(jnp.int32, (heads, columns), 1)
        own = lax.rem(column, heads) == row
        results = []
        for m in range(samples):
            key = jnp.concatenate(
                [key_ref[:, c * samples + m, :] for c in range(chunks)], axis=0
            )
            high = key.astype(BF16)
            low = (key - high.astype(F32)).astype(BF16)
            product = jnp.dot(high, value_ref[m], preferred_element_type=F32)
            product = product + jnp.dot(low, value_ref[m], preferred_element_type=F32)
            results.append(jnp.sum(jnp.where(own, product, 0.0), axis=0, keepdims=True))
        results.append(jnp.zeros((16 - samples, columns), F32))
        attended[...] = jnp.concatenate(results, axis=0).astype(BF16)

    part = jnp.dot(attended[...], proj_ref[...], preferred_element_type=F32)[:samples]
    for hidden in hidden_refs:
        part = part + hidden[...]
    part = part + jnp.sum(token_ref[...].astype(F32), axis=0, keepdims=True) * (1.0 / rows)
    width = out_ref.shape[2]
    for j in range(out_ref.shape[0]):
        out_ref[j] = part[:, j * width : (j + 1) * width]


def feature_part(key_mean, value, w_proj, hidden, tokens, steps):
    parts = key_mean.shape[0]
    samples, rows, columns = value.shape
    own_rows, width = tokens.shape
    cut = width // steps

    def kernel(key_ref, value_ref, proj_ref, *refs):
        feature_kernel(key_ref, value_ref, proj_ref, refs[:-3], *refs[-3:])

    return pl.pallas_call(
        kernel,
        grid=(steps,),
        out_shape=jax.ShapeDtypeStruct((parts, samples, width // parts), F32),
        in_specs=[
            pl.BlockSpec(key_mean.shape, lambda i: (0, 0, 0)),
            pl.BlockSpec(value.shape, lambda i: (0, 0, 0)),
            pl.BlockSpec((columns, cut), lambda i: (0, i)),
        ]
        + [pl.BlockSpec((samples, cut), lambda i: (0, i))] * len(hidden)
        + [pl.BlockSpec((own_rows, cut), lambda i: (0, i))],
        out_specs=pl.BlockSpec((parts // steps, samples, width // parts), lambda i: (i, 0, 0)),
        scratch_shapes=[pltpu.VMEM((16, columns), BF16)],
        compiler_params=pltpu.CompilerParams(vmem_limit_bytes=VMEM_LIMIT),
        cost_estimate=pl.CostEstimate(
            flops=2 * samples * rows * columns * 2 + 32 * columns * width,
            bytes_accessed=2 * columns * width + 2 * value.size,
            transcendentals=0,
        ),
        name="feature_part",
    )(key_mean, value, w_proj, *hidden, tokens)


def pooled_logits(feature, final_gain, w_head):
    highest = lax.Precision.HIGHEST
    gain_head = jnp.dot(final_gain[None], w_head.astype(F32), precision=highest)
    mean = jnp.mean(feature, axis=-1, keepdims=True)
    centered = feature - mean
    spread = jnp.sum(centered * centered, axis=-1, keepdims=True)
    logits = jnp.dot(centered * final_gain, w_head.astype(F32), precision=highest)
    columns = feature.shape[1]
    samples, classes = logits.shape
    bits = 1
    while bits < lax.axis_size("inp"):
        sent = jnp.concatenate(
            [
                jnp.concatenate([logits, mean, spread], axis=1),
                jnp.pad(gain_head, ((0, 0), (0, 2))),
            ],
            axis=0,
        )
        other = permuted(sent, bits)
        other_mean = other[:samples, classes : classes + 1]
        joint = 0.5 * (mean + other_mean)
        logits = (
            logits
            + other[:samples, :classes]
            + (mean - joint) * gain_head
            + (other_mean - joint) * other[samples:, :classes]
        )
        gap = mean - other_mean
        spread = spread + other[:samples, classes + 1 :] + gap * gap * (0.5 * columns)
        gain_head = gain_head + other[samples:, :classes]
        mean = joint
        columns = 2 * columns
        bits = 2 * bits
    scale = lax.rsqrt(spread / columns + 1e-06)
    return mean, scale, logits * scale


def pipelined(
    tokens,
    dropout_masks,
    input_gain,
    w_qkv,
    w_up,
    query_gain,
    key_gain,
    w_proj,
    w_down,
    final_gain,
    w_head,
):
    n_parts = lax.axis_size("inp")
    me = lax.axis_index("inp")
    model_width = tokens.shape[1]
    n_comps, _, n_heads, _ = w_qkv.shape
    own = norm_last(tokens.astype(F32), input_gain).astype(BF16)
    choose = choosers(dropout_masks)
    norm = placed(gathered_pieces(own), me)
    together = lax.optimization_barrier

    def exchange(array):
        return lax.all_to_all(array, "inp", split_axis=0, concat_axis=0, tiled=True)

    both = [query_key(norm, choose, w_qkv, c, n_parts) for c in range(n_heads // n_parts)]
    value = values_of(norm, choose, w_qkv)
    exchanged = [exchange(both[0])]
    *both, value = together((*both[1:], value))
    units = w_up.shape[0] // UNITS
    key_mean, hidden = [], []
    for at in range(len(both) + 1):
        last = exchanged[-1]
        if at < len(both):
            exchanged.append(exchange(both[at]))
        here = range(at * units // len(both), (at + 1) * units // len(both))
        if at < len(both):
            norm_here, last = together((norm, last))
            hidden += [
                hidden_part(norm_here, choose, w_up, w_down, i, 1, UNITS) for i in here
            ]
        key_mean.append(key_weights(last, query_gain, key_gain))
        if at + 1 < len(both):
            *hidden, key_mean[-1], both[at + 1] = together((*hidden, key_mean[-1], both[at + 1]))
    *hidden, key_mean[-1] = together((*hidden, key_mean[-1]))
    key_mean = jnp.concatenate(key_mean, axis=0)
    key_mean = lax.all_to_all(
        jnp.broadcast_to(key_mean[None], (n_parts,) + key_mean.shape),
        "inp",
        split_axis=0,
        concat_axis=0,
        tiled=True,
    )
    partial_feature = feature_part(
        key_mean, value, w_proj.reshape(n_comps * n_heads, model_width), hidden, tokens, 4
    )
    slice_width = model_width // n_parts
    feature = jnp.sum(
        lax.all_to_all(partial_feature, "inp", split_axis=0, concat_axis=0, tiled=True), axis=0
    )
    gain = lax.dynamic_slice_in_dim(final_gain, me * slice_width, slice_width, 0)
    mean, scale, raw_logits = pooled_logits(feature, gain, w_head)
    embedding = (feature - mean) * scale * gain
    logits = soft_cap * jnp.tanh(raw_logits / soft_cap)
    return (embedding[None], bald_score(logits[None]))


def local(
    tokens,
    dropout_masks,
    input_gain,
    w_qkv,
    w_up,
    query_gain,
    key_gain,
    w_proj,
    w_down,
    final_gain,
    w_head,
):
    n_parts = lax.axis_size("inp")
    local_rows, model_width = tokens.shape
    n_masks, all_rows, n_blocks = dropout_masks.shape
    block_width = model_width // n_blocks
    n_comps, three_kinds, n_heads, ignored_width = w_qkv.shape
    n_units = w_up.shape[0]
    head_dim = n_comps * n_parts
    images = all_rows // PATCHES
    qkv_cols = three_kinds * n_heads * n_comps
    items_dev = n_masks * n_heads // n_parts
    highest = lax.Precision.HIGHEST
    joined_weight = jnp.concatenate(
        [jnp.transpose(w_qkv, (1, 2, 0, 3)).reshape(qkv_cols, model_width), w_up], axis=0
    )
    row_piece = lax.all_gather(tokens, "inp", axis=0, tiled=True)
    row_count = row_piece.shape[0]
    normed = norm_last(row_piece.astype(jnp.float32), input_gain).astype(jnp.bfloat16)
    masked = (
        normed.reshape(1, row_count, n_blocks, block_width)
        * dropout_masks.astype(jnp.bfloat16)[..., None]
    )
    masked = masked.reshape(n_masks, row_count, model_width)
    result = jnp.einsum("mkd,cd->mck", masked, joined_weight, preferred_element_type=jnp.float32)
    projected = 2.0 * result
    qkv_half = (
        projected[:, :qkv_cols]
        .astype(jnp.bfloat16)
        .reshape(n_masks, three_kinds, n_heads * n_comps, all_rows)
    )
    item_shape = (n_parts, items_dev, n_comps, all_rows)
    query_send = qkv_half[:, 0].reshape(item_shape)
    key_send = qkv_half[:, 1].reshape(item_shape)
    value_send = qkv_half[:, 2].reshape(item_shape)
    activated = jax.nn.gelu(projected[:, qkv_cols:], approximate=False)
    pooled_hidden = jnp.mean(activated.reshape(n_masks, n_units, images, PATCHES), axis=-1).astype(
        jnp.bfloat16
    )
    query_in = lax.all_to_all(query_send, "inp", split_axis=0, concat_axis=2, tiled=True)
    key_in = lax.all_to_all(key_send, "inp", split_axis=0, concat_axis=2, tiled=True)
    value_in = lax.all_to_all(value_send, "inp", split_axis=0, concat_axis=2, tiled=True)
    n_items = query_in.shape[1]
    shape_four = (n_items, head_dim, images, PATCHES)
    query_norm = norm_second(query_in.reshape(shape_four).astype(jnp.float32), query_gain).astype(
        jnp.bfloat16
    )
    key_norm = norm_second(key_in.reshape(shape_four).astype(jnp.float32), key_gain).astype(
        jnp.bfloat16
    )
    scores = jnp.einsum(
        "jcip,jciq->jipq", query_norm, key_norm, preferred_element_type=jnp.float32
    ) / math.sqrt(head_dim)
    exp_scores = jnp.exp(scores)
    weights = (exp_scores / jnp.sum(exp_scores, axis=-1, keepdims=True)).astype(jnp.bfloat16)
    query_mean = jnp.sum(weights, axis=2, dtype=jnp.float32) / PATCHES
    pooled = jnp.einsum(
        "jiq,jciq->jic",
        query_mean,
        value_in.reshape(shape_four).astype(jnp.float32),
        precision=highest,
    )
    attended = pooled.astype(jnp.bfloat16)[None]
    returned = lax.all_to_all(attended, "inp", split_axis=3, concat_axis=0, tiled=True)
    returned = returned.reshape(n_masks, n_heads, images, n_comps)
    mixed_sum = jnp.einsum("mhic,chd->imd", returned, w_proj, preferred_element_type=jnp.float32)
    mixed_sum = mixed_sum + jnp.einsum(
        "mfi,fd->imd", pooled_hidden, w_down, preferred_element_type=jnp.float32
    )
    row_ids = lax.axis_index("inp") * local_rows + jnp.arange(local_rows, dtype=jnp.int32)
    row_owner = (row_ids // PATCHES)[None, :] == jnp.arange(images, dtype=jnp.int32)[:, None]
    input_sum = (
        jnp.dot(row_owner.astype(jnp.bfloat16), tokens, preferred_element_type=jnp.float32)
        / PATCHES
    )
    partial_feature = mixed_sum + input_sum[:, None, :]
    feature = lax.psum(partial_feature, "inp")
    normalized = norm_last(feature, final_gain)
    slice_width = model_width // n_parts
    embedding = lax.dynamic_slice_in_dim(
        normalized, lax.axis_index("inp") * slice_width, slice_width, 2
    )
    logit_part = jnp.einsum(
        "imd,dc->imc", embedding.astype(jnp.bfloat16), w_head, preferred_element_type=jnp.float32
    )
    raw_logits = lax.psum(logit_part, "inp")
    logits = soft_cap * jnp.tanh(raw_logits / soft_cap)
    return (embedding, bald_score(logits))


def solution(mesh):
    fits = mesh.shape["inp"] == PIPELINED_PARTS
    return jax.shard_map(
        pipelined if fits else local,
        mesh=mesh,
        in_specs=(
            P(("groups", "inp"), None),
            P(None, "groups", None),
            P(),
            P("inp", None, None, None),
            P("inp", None),
            P(),
            P(),
            P("inp", None, None),
            P("inp", None),
            P(),
            P("inp", None),
        ),
        out_specs=(P("groups", None, "inp"), P("groups")),
        check_vma=False,
    )
```

```python
import functools
import math

import jax
import jax.numpy as jnp
from jax import lax
from jax.experimental import pallas as pl
from jax.experimental.pallas import tpu as pltpu
from jax.sharding import PartitionSpec as P

PATCHES = 256


soft_cap = 20.0
PIPELINED_PARTS = 16
UNITS = 256
F32 = jnp.float32
BF16 = jnp.bfloat16
MIB = 1024 * 1024


def norm_last(values, gain):
    average = jnp.mean(values, axis=-1, keepdims=True)
    centered = values - average
    spread_sq = jnp.mean(centered * centered, axis=-1, keepdims=True)
    return centered * lax.rsqrt(spread_sq + 1e-06) * gain


def norm_second(values, gain):
    average = jnp.mean(values, axis=1, keepdims=True)
    centered = values - average
    spread_sq = jnp.mean(centered * centered, axis=1, keepdims=True)
    return centered * lax.rsqrt(spread_sq + 1e-06) * gain[None, :, None, None]


def bald_score(logits):
    exp_logits = jnp.exp(logits)
    totals = jnp.sum(exp_logits, axis=-1, keepdims=True)
    sample_probs = exp_logits / totals
    entropy = jnp.log(totals[..., 0]) - jnp.sum(sample_probs * logits, axis=-1)
    mean_probs = jnp.mean(sample_probs, axis=1)
    joint = -jnp.sum(mean_probs * jnp.log(mean_probs), axis=-1)
    return joint - jnp.mean(entropy, axis=1)


def permuted(array, bits):
    count = lax.axis_size("inp")
    return lax.ppermute(array, "inp", [(i, i ^ bits) for i in range(count)])


def own_norm_kernel(x_ref, gain_ref, first_ref, second_ref):
    y = norm_last(x_ref[...].astype(F32), gain_ref[...]).astype(BF16)
    cut = first_ref.shape[1]
    first_ref[...] = y[:, :cut]
    second_ref[...] = y[:, cut:]


def own_norm(tokens, gain):
    rows, width = tokens.shape
    cut = width // 3 * 2
    return pl.pallas_call(
        own_norm_kernel,
        out_shape=(
            jax.ShapeDtypeStruct((rows, cut), BF16),
            jax.ShapeDtypeStruct((rows, width - cut), BF16),
        ),
        compiler_params=pltpu.CompilerParams(vmem_limit_bytes=8 * MIB),
        name="own_norm",
    )(tokens, gain.reshape(1, width))


def gathered_pieces(first, second, beside):
    along_z = jnp.stack([first] + [permuted(first, 4 * k) for k in range(1, 4)])
    pair = jnp.stack([second, permuted(second, 2)])
    along_z, pair, beside = lax.optimization_barrier((along_z, pair, beside))
    across_y = permuted(along_z, 2)
    moved = [permuted(pair, 4 * k) for k in range(1, 4)]
    across_y, *moved = lax.optimization_barrier((across_y, *moved))
    pieces = [
        (0, [4 * k for k in range(4)], along_z),
        (0, [4 * k + 2 for k in range(4)], across_y),
    ]
    for k, array in enumerate([pair, *moved]):
        pieces.append((first.shape[1], [4 * k, 4 * k + 2], array))
    pieces = pieces + [
        (side, [b ^ 1 for b in bits], permuted(array, 1)) for side, bits, array in pieces
    ]
    return pieces, beside


def place_kernel(layout, me_ref, *refs):
    sources, out_ref = refs[:-1], refs[-1]
    me = me_ref[0]
    for (side, bits), source in zip(layout, sources, strict=True):
        _, rows, columns = source.shape
        for at, bit in enumerate(bits):
            start = pl.multiple_of((me ^ bit) * rows, rows)
            out_ref[pl.ds(start, rows), side : side + columns] = source[at]


def placed(pieces, me):
    rows = pieces[0][2].shape[1]
    total = rows * sum(len(bits) for side, bits, _ in pieces if side == 0)
    width = sum(array.size for _, _, array in pieces) // total
    layout = [(side, bits) for side, bits, _ in pieces]
    return pl.pallas_call(
        functools.partial(place_kernel, layout),
        out_shape=jax.ShapeDtypeStruct((total, width), BF16),
        in_specs=[pl.BlockSpec(memory_space=pltpu.SMEM)]
        + [pl.BlockSpec(memory_space=pltpu.VMEM)] * len(pieces),
        out_specs=pl.BlockSpec(memory_space=pltpu.VMEM),
        compiler_params=pltpu.CompilerParams(vmem_limit_bytes=16 * MIB),
        name="place_rows",
    )(me.reshape(1), *[array for _, _, array in pieces])


ACROSS = (((1,), (1,)), ((), ()))
TILE = 16
BLOCK = 128


def choosers(dropout_masks):
    samples, rows, blocks = dropout_masks.shape
    tiles = rows // TILE
    kept = dropout_masks.astype(BF16).reshape(samples, tiles, TILE, blocks)
    kept = jnp.transpose(kept, (1, 0, 2, 3)).reshape(tiles, samples * TILE, blocks)
    column = jnp.arange(blocks * TILE)
    spread = (column[None] // TILE == jnp.arange(blocks)[:, None]).astype(BF16)
    own = jnp.arange(samples * TILE)[:, None] % TILE == column[None] % TILE
    wide = jnp.einsum("trb,bc->trc", kept, spread, preferred_element_type=F32)
    return jnp.where(own[None], 2.0 * wide, 0.0).astype(BF16)


def block_products(norm_ref, weight, products, first):
    for j in range(weight.shape[1] // BLOCK):
        at = slice(j * BLOCK, (j + 1) * BLOCK)
        products[first + j] = lax.dot_general(
            norm_ref[:, at], weight[:, at], ACROSS, preferred_element_type=F32
        ).astype(BF16)


def summed(choose_ref, products, tile):
    blocks, _, columns = products.shape
    part = products[:, tile * TILE : (tile + 1) * TILE, :].reshape(blocks * TILE, columns)
    return jnp.dot(choose_ref[tile], part, preferred_element_type=F32)


def query_key_kernel(norm_ref, choose_ref, w_ref, out_ref, products, sums, turned):
    step = pl.program_id(0)
    rows, depth = norm_ref.shape
    comps, kinds, heads, _ = w_ref.shape
    columns = comps * kinds * heads
    block_products(
        norm_ref, w_ref[...].reshape(columns, depth), products, step * (depth // BLOCK)
    )

    @pl.when(step == pl.num_programs(0) - 1)
    def _():
        samples = sums.shape[0]
        for tile in range(rows // TILE):
            sums[:, tile * TILE : (tile + 1) * TILE, :] = summed(
                choose_ref, products, tile
            ).reshape(samples, TILE, columns)
        for m in range(samples):
            for part in range(rows // 128):
                at = slice(part * 128, (part + 1) * 128)
                turned[m * (rows // 128) + part] = sums[m, at, :].T
            for part in range(rows // 128):
                at = slice(part * 128, (part + 1) * 128)
                held = turned.at[m * (rows // 128) + part]
                for h in range(heads):
                    both = [
                        held[pl.ds(t * heads + h, comps, stride=kinds * heads), :]
                        for t in range(kinds)
                    ]
                    out_ref[h, m, :, at] = jnp.concatenate(both, axis=0).astype(BF16)


def query_key(norm, choose, w_qkv, chunk, heads):
    rows, width = norm.shape
    samples = choose.shape[1] // TILE
    comps = w_qkv.shape[0]
    depth = width // 2
    columns = 2 * comps * heads
    shape = (heads, samples, 2 * comps, rows)
    return pl.pallas_call(
        query_key_kernel,
        grid=(width // depth,),
        out_shape=jax.ShapeDtypeStruct(shape, BF16),
        in_specs=[
            pl.BlockSpec((rows, depth), lambda k: (0, k)),
            pl.BlockSpec(choose.shape, lambda k: (0, 0, 0)),
            pl.BlockSpec((comps, 2, heads, depth), lambda k: (0, 0, chunk, k)),
        ],
        out_specs=pl.BlockSpec(shape, lambda k: (0, 0, 0, 0)),
        scratch_shapes=[
            pltpu.VMEM((width // BLOCK, rows, columns), BF16),
            pltpu.VMEM((samples, rows, columns), F32),
            pltpu.VMEM((samples * rows // 128, columns, 128), F32),
        ],
        compiler_params=pltpu.CompilerParams(vmem_limit_bytes=54 * MIB),
        cost_estimate=pl.CostEstimate(
            flops=8 * rows * width * columns,
            bytes_accessed=2 * (norm.size + choose.size + columns * width),
            transcendentals=0,
        ),
        name="query_key",
    )(norm, choose, w_qkv)


def value_kernel(norm_ref, choose_ref, w_ref, out_ref, products):
    step = pl.program_id(0)
    rows, depth = norm_ref.shape
    comps, _, heads, _ = w_ref.shape
    block_products(
        norm_ref, w_ref[:, 0].reshape(comps * heads, depth), products, step * (depth // BLOCK)
    )

    @pl.when(step == pl.num_programs(0) - 1)
    def _():
        samples = out_ref.shape[0]
        for tile in range(rows // TILE):
            out_ref[:, tile * TILE : (tile + 1) * TILE, :] = (
                summed(choose_ref, products, tile)
                .reshape(samples, TILE, comps * heads)
                .astype(BF16)
            )


def values_of(norm, choose, w_qkv):
    rows, width = norm.shape
    samples = choose.shape[1] // TILE
    comps, _, heads, _ = w_qkv.shape
    depth = width // 2
    columns = comps * heads
    return pl.pallas_call(
        value_kernel,
        grid=(width // depth,),
        out_shape=jax.ShapeDtypeStruct((samples, rows, columns), BF16),
        in_specs=[
            pl.BlockSpec((rows, depth), lambda k: (0, k)),
            pl.BlockSpec(choose.shape, lambda k: (0, 0, 0)),
            pl.BlockSpec((comps, 1, heads, depth), lambda k: (0, 2, 0, k)),
        ],
        out_specs=pl.BlockSpec((samples, rows, columns), lambda k: (0, 0, 0)),
        scratch_shapes=[pltpu.VMEM((width // BLOCK, rows, columns), BF16)],
        compiler_params=pltpu.CompilerParams(vmem_limit_bytes=54 * MIB),
        cost_estimate=pl.CostEstimate(
            flops=8 * rows * width * columns,
            bytes_accessed=2 * (norm.size + choose.size + columns * width),
            transcendentals=0,
        ),
        name="value_rows",
    )(norm, choose, w_qkv)


def erf(x):
    x = jnp.clip(x, -4.0, 4.0)
    s = x * x
    top = s * -2.72614225801306e-10 + 2.77068142495902e-08
    for c in (
        -2.10102402082508e-06,
        -5.69250639462346e-05,
        -7.34990630326855e-04,
        -2.95459980854025e-03,
        -1.60960333262415e-02,
    ):
        top = top * s + c
    low = s * -1.45660718464996e-05 + -2.13374055278905e-04
    for c in (-1.68282697438203e-03, -7.37332916720468e-03, -1.42647390514189e-02):
        low = low * s + c
    return x * top / low


def hidden_kernel(norm_ref, choose_ref, up_ref, out_ref, products):
    step = pl.program_id(1)
    rows, depth = norm_ref.shape
    samples, units = out_ref.shape
    block_products(norm_ref, up_ref, products, step * (depth // BLOCK))

    @pl.when(step == pl.num_programs(1) - 1)
    def _():
        total = jnp.zeros((samples, units), F32)
        for tile in range(rows // TILE):
            v = summed(choose_ref, products, tile)
            active = (0.5 * v) * (1.0 + erf(v * math.sqrt(0.5)))
            total = total + jnp.sum(active.reshape(samples, TILE, units), axis=1)
        out_ref[...] = total * (1.0 / rows)


def hidden_part(norm, choose, w_up, first, tiles):
    rows, width = norm.shape
    samples = choose.shape[1] // TILE
    depth = width // 2
    return pl.pallas_call(
        hidden_kernel,
        grid=(tiles, width // depth),
        out_shape=jax.ShapeDtypeStruct((samples, tiles * UNITS), F32),
        in_specs=[
            pl.BlockSpec((rows, depth), lambda i, k: (0, k)),
            pl.BlockSpec(choose.shape, lambda i, k: (0, 0, 0)),
            pl.BlockSpec((UNITS, depth), lambda i, k: (first + i, k)),
        ],
        out_specs=pl.BlockSpec((samples, UNITS), lambda i, k: (0, i)),
        scratch_shapes=[pltpu.VMEM((width // BLOCK, rows, UNITS), BF16)],
        compiler_params=pltpu.CompilerParams(vmem_limit_bytes=54 * MIB),
        cost_estimate=pl.CostEstimate(
            flops=8 * rows * width * UNITS * tiles,
            bytes_accessed=2 * (norm.size + choose.size + UNITS * tiles * width),
            transcendentals=samples * rows * UNITS * tiles,
        ),
        name="hidden_part",
    )(norm, choose, w_up)


def down_kernel(pooled_ref, down_ref, out_ref):
    samples = pooled_ref.shape[0]
    mean = pooled_ref[...]
    mean = jnp.concatenate([mean, jnp.zeros_like(mean)], axis=0).astype(BF16)
    part = jnp.dot(mean, down_ref[...], preferred_element_type=F32)[:samples]

    @pl.when(pl.program_id(0) == 0)
    def _():
        out_ref[...] = part

    @pl.when(pl.program_id(0) > 0)
    def _():
        out_ref[...] += part


def down_part(pooled, w_down):
    samples, units = pooled.shape
    width = w_down.shape[1]
    return pl.pallas_call(
        down_kernel,
        grid=(units // UNITS,),
        out_shape=jax.ShapeDtypeStruct((samples, width), F32),
        in_specs=[
            pl.BlockSpec((samples, UNITS), lambda i: (0, i)),
            pl.BlockSpec((UNITS, width), lambda i: (i, 0)),
        ],
        out_specs=pl.BlockSpec((samples, width), lambda i: (0, 0)),
        compiler_params=pltpu.CompilerParams(vmem_limit_bytes=54 * MIB),
        cost_estimate=pl.CostEstimate(
            flops=32 * units * width, bytes_accessed=2 * units * width, transcendentals=0
        ),
        name="down_part",
    )(pooled, w_down)


def attention_kernel(items, x_ref, query_gain_ref, key_gain_ref, out_ref):
    parts, _, both, rows = x_ref.shape
    comps = both // 2
    head_dim = parts * comps

    def normed(values, gain_ref):
        values = values.reshape(head_dim, rows)
        average = jnp.mean(values, axis=0, keepdims=True)
        centered = values - average
        spread_sq = jnp.mean(centered * centered, axis=0, keepdims=True)
        return (centered * lax.rsqrt(spread_sq + 1e-06) * gain_ref[...]).astype(BF16)

    for j in range(items):
        x = x_ref[:, j].astype(F32)
        query = normed(x[:, :comps], query_gain_ref)
        key = normed(x[:, comps:], key_gain_ref)
        scores = lax.dot_general(
            query, key, (((0,), (0,)), ((), ())), preferred_element_type=F32
        )
        e = jnp.exp2(scores * (math.log2(math.e) / math.sqrt(head_dim)))
        weights = (e * (1.0 / jnp.sum(e, axis=1, keepdims=True))).astype(BF16)
        out_ref[j : j + 1, :] = jnp.sum(weights.astype(F32), axis=0, keepdims=True) * (1.0 / rows)


def key_weights(exchanged, query_gain, key_gain):
    parts, items, both, rows = exchanged.shape
    head_dim = parts * both // 2
    return pl.pallas_call(
        functools.partial(attention_kernel, items),
        out_shape=jax.ShapeDtypeStruct((items, rows), F32),
        compiler_params=pltpu.CompilerParams(vmem_limit_bytes=16 * MIB),
        cost_estimate=pl.CostEstimate(
            flops=2 * items * rows * rows * head_dim,
            bytes_accessed=2 * exchanged.size,
            transcendentals=items * rows * rows,
        ),
        name="key_weights",
    )(exchanged, query_gain.reshape(head_dim, 1), key_gain.reshape(head_dim, 1))


def feature_kernel(key_ref, value_ref, proj_ref, hidden_ref, token_ref, out_ref, attended):
    step = pl.program_id(0)
    parts, pieces, _ = key_ref.shape
    samples, rows, columns = value_ref.shape
    chunks = pieces // samples
    heads = parts * chunks

    @pl.when(step == 0)
    def _():
        row = lax.broadcasted_iota(jnp.int32, (heads, columns), 0)
        column = lax.broadcasted_iota(jnp.int32, (heads, columns), 1)
        own = lax.rem(column, heads) == row
        results = []
        for m in range(samples):
            key = jnp.concatenate(
                [
                    key_ref[:, c * samples + m, :].astype(F32)
                    for c in range(chunks)
                ], axis=0
            )
            product = jnp.dot(key.astype(BF16), value_ref[m], preferred_element_type=F32)
            results.append(jnp.sum(jnp.where(own, product, 0.0), axis=0, keepdims=True))
        results.append(jnp.zeros((16 - samples, columns), F32))
        attended[...] = jnp.concatenate(results, axis=0).astype(BF16)

    part = jnp.dot(attended[...], proj_ref[...], preferred_element_type=F32)[:samples]
    part = part + hidden_ref[...]
    part = part + jnp.sum(token_ref[...].astype(F32), axis=0, keepdims=True) * (1.0 / rows)
    width = out_ref.shape[2]
    for j in range(out_ref.shape[0]):
        out_ref[j] = part[:, j * width : (j + 1) * width]


def feature_part(key_mean, value, w_proj, hidden, tokens, steps):
    parts = key_mean.shape[0]
    samples, rows, columns = value.shape
    own_rows, width = tokens.shape
    cut = width // steps
    return pl.pallas_call(
        feature_kernel,
        grid=(steps,),
        out_shape=jax.ShapeDtypeStruct((parts, samples, width // parts), F32),
        in_specs=[
            pl.BlockSpec(key_mean.shape, lambda i: (0, 0, 0)),
            pl.BlockSpec(value.shape, lambda i: (0, 0, 0)),
            pl.BlockSpec((columns, cut), lambda i: (0, i)),
            pl.BlockSpec((samples, cut), lambda i: (0, i)),
            pl.BlockSpec((own_rows, cut), lambda i: (0, i)),
        ],
        out_specs=pl.BlockSpec((parts // steps, samples, width // parts), lambda i: (i, 0, 0)),
        scratch_shapes=[pltpu.VMEM((16, columns), BF16)],
        compiler_params=pltpu.CompilerParams(vmem_limit_bytes=54 * MIB),
        cost_estimate=pl.CostEstimate(
            flops=2 * samples * rows * columns * 2 + 32 * columns * width,
            bytes_accessed=2 * columns * width + 2 * value.size,
            transcendentals=0,
        ),
        name="feature_part",
    )(key_mean, value, w_proj, hidden, tokens)


def pooled_logits(feature, final_gain, w_head):
    highest = lax.Precision.HIGHEST
    gain_head = jnp.dot(final_gain[None], w_head.astype(F32), precision=highest)
    mean = jnp.mean(feature, axis=-1, keepdims=True)
    centered = feature - mean
    spread = jnp.sum(centered * centered, axis=-1, keepdims=True)
    logits = jnp.dot(centered * final_gain, w_head.astype(F32), precision=highest)
    columns = feature.shape[1]
    samples, classes = logits.shape
    bits = 1
    while bits < lax.axis_size("inp"):
        sent = jnp.concatenate(
            [
                jnp.concatenate([logits, mean, spread], axis=1),
                jnp.pad(gain_head, ((0, 0), (0, 2))),
            ],
            axis=0,
        )
        other = permuted(sent, bits)
        other_mean = other[:samples, classes : classes + 1]
        joint = 0.5 * (mean + other_mean)
        logits = (
            logits
            + other[:samples, :classes]
            + (mean - joint) * gain_head
            + (other_mean - joint) * other[samples:, :classes]
        )
        gap = mean - other_mean
        spread = spread + other[:samples, classes + 1 :] + gap * gap * (0.5 * columns)
        gain_head = gain_head + other[samples:, :classes]
        mean = joint
        columns = 2 * columns
        bits = 2 * bits
    scale = lax.rsqrt(spread / columns + 1e-06)
    return mean, scale, logits * scale


def pipelined(
    tokens,
    dropout_masks,
    input_gain,
    w_qkv,
    w_up,
    query_gain,
    key_gain,
    w_proj,
    w_down,
    final_gain,
    w_head,
):
    n_parts = lax.axis_size("inp")
    me = lax.axis_index("inp")
    model_width = tokens.shape[1]
    n_comps, _, n_heads, _ = w_qkv.shape
    choose = choosers(dropout_masks)
    pieces, choose = gathered_pieces(*own_norm(tokens, input_gain), choose)
    norm = placed(pieces, me)
    together = lax.optimization_barrier

    def exchange(array):
        return lax.all_to_all(array, "inp", split_axis=0, concat_axis=0, tiled=True)

    both = [query_key(norm, choose, w_qkv, c, n_parts) for c in range(n_heads // n_parts)]
    value = values_of(norm, choose, w_qkv)
    exchanged = [exchange(both[0])]
    *both, value = together((*both[1:], value))
    tiles = w_up.shape[0] // UNITS // len(both)
    key_mean, pooled = [], []
    for at, sent in enumerate(both):
        last = exchanged[-1]
        if at > 0:
            pooled[-1], key_mean[-1], sent = together((pooled[-1], key_mean[-1], sent))
        exchanged.append(exchange(sent))
        norm_here, last = together((norm, last))
        pooled.append(hidden_part(norm_here, choose, w_up, at * tiles, tiles))
        key_mean.append(key_weights(last, query_gain, key_gain))
    key_mean.append(key_weights(exchanged[-1], query_gain, key_gain))
    pooled[-1], key_mean[-1] = together((pooled[-1], key_mean[-1]))
    key_mean = jnp.concatenate(key_mean, axis=0).astype(BF16)
    hidden = down_part(jnp.concatenate(pooled, axis=1), w_down)
    key_mean = lax.all_to_all(
        jnp.broadcast_to(key_mean[None], (n_parts,) + key_mean.shape),
        "inp",
        split_axis=0,
        concat_axis=0,
        tiled=True,
    )
    partial_feature = feature_part(
        key_mean, value, w_proj.reshape(n_comps * n_heads, model_width), hidden, tokens, 4
    )
    slice_width = model_width // n_parts
    feature = jnp.sum(
        lax.all_to_all(partial_feature, "inp", split_axis=0, concat_axis=0, tiled=True), axis=0
    )
    gain = lax.dynamic_slice_in_dim(final_gain, me * slice_width, slice_width, 0)
    mean, scale, raw_logits = pooled_logits(feature, gain, w_head)
    embedding = (feature - mean) * scale * gain
    logits = soft_cap * jnp.tanh(raw_logits / soft_cap)
    return (embedding[None], bald_score(logits[None]))


def local(
    tokens,
    dropout_masks,
    input_gain,
    w_qkv,
    w_up,
    query_gain,
    key_gain,
    w_proj,
    w_down,
    final_gain,
    w_head,
):
    n_parts = lax.axis_size("inp")
    local_rows, model_width = tokens.shape
    n_masks, all_rows, n_blocks = dropout_masks.shape
    block_width = model_width // n_blocks
    n_comps, three_kinds, n_heads, ignored_width = w_qkv.shape
    n_units = w_up.shape[0]
    head_dim = n_comps * n_parts
    images = all_rows // PATCHES
    qkv_cols = three_kinds * n_heads * n_comps
    items_dev = n_masks * n_heads // n_parts
    highest = lax.Precision.HIGHEST
    joined_weight = jnp.concatenate(
        [jnp.transpose(w_qkv, (1, 2, 0, 3)).reshape(qkv_cols, model_width), w_up], axis=0
    )
    row_piece = lax.all_gather(tokens, "inp", axis=0, tiled=True)
    row_count = row_piece.shape[0]
    normed = norm_last(row_piece.astype(jnp.float32), input_gain).astype(jnp.bfloat16)
    masked = (
        normed.reshape(1, row_count, n_blocks, block_width)
        * dropout_masks.astype(jnp.bfloat16)[..., None]
    )
    masked = masked.reshape(n_masks, row_count, model_width)
    result = jnp.einsum("mkd,cd->mck", masked, joined_weight, preferred_element_type=jnp.float32)
    projected = 2.0 * result
    qkv_half = (
        projected[:, :qkv_cols]
        .astype(jnp.bfloat16)
        .reshape(n_masks, three_kinds, n_heads * n_comps, all_rows)
    )
    item_shape = (n_parts, items_dev, n_comps, all_rows)
    query_send = qkv_half[:, 0].reshape(item_shape)
    key_send = qkv_half[:, 1].reshape(item_shape)
    value_send = qkv_half[:, 2].reshape(item_shape)
    activated = jax.nn.gelu(projected[:, qkv_cols:], approximate=False)
    pooled_hidden = jnp.mean(activated.reshape(n_masks, n_units, images, PATCHES), axis=-1).astype(
        jnp.bfloat16
    )
    query_in = lax.all_to_all(query_send, "inp", split_axis=0, concat_axis=2, tiled=True)
    key_in = lax.all_to_all(key_send, "inp", split_axis=0, concat_axis=2, tiled=True)
    value_in = lax.all_to_all(value_send, "inp", split_axis=0, concat_axis=2, tiled=True)
    n_items = query_in.shape[1]
    shape_four = (n_items, head_dim, images, PATCHES)
    query_norm = norm_second(query_in.reshape(shape_four).astype(jnp.float32), query_gain).astype(
        jnp.bfloat16
    )
    key_norm = norm_second(key_in.reshape(shape_four).astype(jnp.float32), key_gain).astype(
        jnp.bfloat16
    )
    scores = jnp.einsum(
        "jcip,jciq->jipq", query_norm, key_norm, preferred_element_type=jnp.float32
    ) / math.sqrt(head_dim)
    exp_scores = jnp.exp(scores)
    weights = (exp_scores / jnp.sum(exp_scores, axis=-1, keepdims=True)).astype(jnp.bfloat16)
    query_mean = jnp.sum(weights, axis=2, dtype=jnp.float32) / PATCHES
    pooled = jnp.einsum(
        "jiq,jciq->jic",
        query_mean,
        value_in.reshape(shape_four).astype(jnp.float32),
        precision=highest,
    )
    attended = pooled.astype(jnp.bfloat16)[None]
    returned = lax.all_to_all(attended, "inp", split_axis=3, concat_axis=0, tiled=True)
    returned = returned.reshape(n_masks, n_heads, images, n_comps)
    mixed_sum = jnp.einsum("mhic,chd->imd", returned, w_proj, preferred_element_type=jnp.float32)
    mixed_sum = mixed_sum + jnp.einsum(
        "mfi,fd->imd", pooled_hidden, w_down, preferred_element_type=jnp.float32
    )
    row_ids = lax.axis_index("inp") * local_rows + jnp.arange(local_rows, dtype=jnp.int32)
    row_owner = (row_ids // PATCHES)[None, :] == jnp.arange(images, dtype=jnp.int32)[:, None]
    input_sum = (
        jnp.dot(row_owner.astype(jnp.bfloat16), tokens, preferred_element_type=jnp.float32)
        / PATCHES
    )
    partial_feature = mixed_sum + input_sum[:, None, :]
    feature = lax.psum(partial_feature, "inp")
    normalized = norm_last(feature, final_gain)
    slice_width = model_width // n_parts
    embedding = lax.dynamic_slice_in_dim(
        normalized, lax.axis_index("inp") * slice_width, slice_width, 2
    )
    logit_part = jnp.einsum(
        "imd,dc->imc", embedding.astype(jnp.bfloat16), w_head, preferred_element_type=jnp.float32
    )
    raw_logits = lax.psum(logit_part, "inp")
    logits = soft_cap * jnp.tanh(raw_logits / soft_cap)
    return (embedding, bald_score(logits))


def solution(mesh):
    fits = mesh.shape["inp"] == PIPELINED_PARTS
    return jax.shard_map(
        pipelined if fits else local,
        mesh=mesh,
        in_specs=(
            P(("groups", "inp"), None),
            P(None, "groups", None),
            P(),
            P("inp", None, None, None),
            P("inp", None),
            P(),
            P(),
            P("inp", None, None),
            P("inp", None),
            P(),
            P("inp", None),
        ),
        out_specs=(P("groups", None, "inp"), P("groups")),
        check_vma=False,
    )
```

```python
import functools
import math

import jax
import jax.numpy as jnp
from jax import lax
from jax.experimental import pallas as pl
from jax.experimental.pallas import tpu as pltpu
from jax.sharding import PartitionSpec as P

PATCHES = 256


soft_cap = 20.0
PIPELINED_PARTS = 16
UNITS = 256
F32 = jnp.float32
BF16 = jnp.bfloat16
MIB = 1024 * 1024


def norm_last(values, gain):
    average = jnp.mean(values, axis=-1, keepdims=True)
    centered = values - average
    spread_sq = jnp.mean(centered * centered, axis=-1, keepdims=True)
    return centered * lax.rsqrt(spread_sq + 1e-06) * gain


def norm_second(values, gain):
    average = jnp.mean(values, axis=1, keepdims=True)
    centered = values - average
    spread_sq = jnp.mean(centered * centered, axis=1, keepdims=True)
    return centered * lax.rsqrt(spread_sq + 1e-06) * gain[None, :, None, None]


def bald_score(logits):
    exp_logits = jnp.exp(logits)
    totals = jnp.sum(exp_logits, axis=-1, keepdims=True)
    sample_probs = exp_logits / totals
    entropy = jnp.log(totals[..., 0]) - jnp.sum(sample_probs * logits, axis=-1)
    mean_probs = jnp.mean(sample_probs, axis=1)
    joint = -jnp.sum(mean_probs * jnp.log(mean_probs), axis=-1)
    return joint - jnp.mean(entropy, axis=1)


def permuted(array, bits):
    count = lax.axis_size("inp")
    return lax.ppermute(array, "inp", [(i, i ^ bits) for i in range(count)])


def own_norm_kernel(x_ref, gain_ref, first_ref, second_ref):
    y = norm_last(x_ref[...].astype(F32), gain_ref[...]).astype(BF16)
    cut = first_ref.shape[1]
    first_ref[...] = y[:, :cut]
    second_ref[...] = y[:, cut:]


def own_norm(tokens, gain):
    rows, width = tokens.shape
    cut = width // 3 * 2
    return pl.pallas_call(
        own_norm_kernel,
        out_shape=(
            jax.ShapeDtypeStruct((rows, cut), BF16),
            jax.ShapeDtypeStruct((rows, width - cut), BF16),
        ),
        compiler_params=pltpu.CompilerParams(vmem_limit_bytes=8 * MIB),
        name="own_norm",
    )(tokens, gain.reshape(1, width))


def gathered_pieces(first, second, beside):
    along_z = jnp.stack([first] + [permuted(first, 4 * k) for k in range(1, 4)])
    pair = jnp.stack([second, permuted(second, 2)])
    along_z, pair, beside = lax.optimization_barrier((along_z, pair, beside))
    across_y = permuted(along_z, 2)
    moved = [permuted(pair, 4 * k) for k in range(1, 4)]
    across_y, *moved = lax.optimization_barrier((across_y, *moved))
    pieces = [
        (0, [4 * k for k in range(4)], along_z),
        (0, [4 * k + 2 for k in range(4)], across_y),
    ]
    for k, array in enumerate([pair, *moved]):
        pieces.append((first.shape[1], [4 * k, 4 * k + 2], array))
    pieces = pieces + [
        (side, [b ^ 1 for b in bits], permuted(array, 1)) for side, bits, array in pieces
    ]
    return pieces, beside


def place_kernel(layout, me_ref, *refs):
    sources, out_ref = refs[:-1], refs[-1]
    me = me_ref[0]
    for (side, bits), source in zip(layout, sources, strict=True):
        _, rows, columns = source.shape
        for at, bit in enumerate(bits):
            start = pl.multiple_of((me ^ bit) * rows, rows)
            out_ref[pl.ds(start, rows), side : side + columns] = source[at]


def placed(pieces, me):
    rows = pieces[0][2].shape[1]
    total = rows * sum(len(bits) for side, bits, _ in pieces if side == 0)
    width = sum(array.size for _, _, array in pieces) // total
    layout = [(side, bits) for side, bits, _ in pieces]
    return pl.pallas_call(
        functools.partial(place_kernel, layout),
        out_shape=jax.ShapeDtypeStruct((total, width), BF16),
        in_specs=[pl.BlockSpec(memory_space=pltpu.SMEM)]
        + [pl.BlockSpec(memory_space=pltpu.VMEM)] * len(pieces),
        out_specs=pl.BlockSpec(memory_space=pltpu.VMEM),
        compiler_params=pltpu.CompilerParams(vmem_limit_bytes=16 * MIB),
        name="place_rows",
    )(me.reshape(1), *[array for _, _, array in pieces])


ACROSS = (((1,), (1,)), ((), ()))
TILE = 16
BLOCK = 128


def choosers(dropout_masks):
    samples, rows, blocks = dropout_masks.shape
    tiles = rows // TILE
    kept = dropout_masks.astype(BF16).reshape(samples, tiles, TILE, blocks)
    kept = jnp.transpose(kept, (1, 0, 2, 3)).reshape(tiles, samples * TILE, blocks)
    column = jnp.arange(blocks * TILE)
    spread = (column[None] // TILE == jnp.arange(blocks)[:, None]).astype(BF16)
    own = jnp.arange(samples * TILE)[:, None] % TILE == column[None] % TILE
    wide = jnp.einsum("trb,bc->trc", kept, spread, preferred_element_type=F32)
    return jnp.where(own[None], 2.0 * wide, 0.0).astype(BF16)


def block_products(norm_ref, weight, products, first):
    for j in range(weight.shape[1] // BLOCK):
        at = slice(j * BLOCK, (j + 1) * BLOCK)
        products[first + j] = lax.dot_general(
            norm_ref[:, at], weight[:, at], ACROSS, preferred_element_type=F32
        ).astype(BF16)


def summed(choose_ref, products, tile):
    blocks, _, columns = products.shape
    part = products[:, tile * TILE : (tile + 1) * TILE, :].reshape(blocks * TILE, columns)
    return jnp.dot(choose_ref[tile], part, preferred_element_type=F32)


def query_key_kernel(norm_ref, choose_ref, w_ref, out_ref, products, sums, turned):
    step = pl.program_id(0)
    rows, depth = norm_ref.shape
    comps, kinds, heads, _ = w_ref.shape
    columns = comps * kinds * heads
    block_products(
        norm_ref, w_ref[...].reshape(columns, depth), products, step * (depth // BLOCK)
    )

    @pl.when(step == pl.num_programs(0) - 1)
    def _():
        samples = sums.shape[0]
        for tile in range(rows // TILE):
            sums[:, tile * TILE : (tile + 1) * TILE, :] = summed(
                choose_ref, products, tile
            ).reshape(samples, TILE, columns)
        for m in range(samples):
            for part in range(rows // 128):
                at = slice(part * 128, (part + 1) * 128)
                turned[m * (rows // 128) + part] = sums[m, at, :].T
            for part in range(rows // 128):
                at = slice(part * 128, (part + 1) * 128)
                held = turned.at[m * (rows // 128) + part]
                for h in range(heads):
                    both = [
                        held[pl.ds(t * heads + h, comps, stride=kinds * heads), :]
                        for t in range(kinds)
                    ]
                    out_ref[h, m, :, at] = jnp.concatenate(both, axis=0).astype(BF16)


def query_key(norm, choose, w_qkv, chunk, heads):
    rows, width = norm.shape
    samples = choose.shape[1] // TILE
    comps = w_qkv.shape[0]
    depth = width // 2
    columns = 2 * comps * heads
    shape = (heads, samples, 2 * comps, rows)
    return pl.pallas_call(
        query_key_kernel,
        grid=(width // depth,),
        out_shape=jax.ShapeDtypeStruct(shape, BF16),
        in_specs=[
            pl.BlockSpec((rows, depth), lambda k: (0, k)),
            pl.BlockSpec(choose.shape, lambda k: (0, 0, 0)),
            pl.BlockSpec((comps, 2, heads, depth), lambda k: (0, 0, chunk, k)),
        ],
        out_specs=pl.BlockSpec(shape, lambda k: (0, 0, 0, 0)),
        scratch_shapes=[
            pltpu.VMEM((width // BLOCK, rows, columns), BF16),
            pltpu.VMEM((samples, rows, columns), F32),
            pltpu.VMEM((samples * rows // 128, columns, 128), F32),
        ],
        compiler_params=pltpu.CompilerParams(vmem_limit_bytes=54 * MIB),
        cost_estimate=pl.CostEstimate(
            flops=8 * rows * width * columns,
            bytes_accessed=2 * (norm.size + choose.size + columns * width),
            transcendentals=0,
        ),
        name="query_key",
    )(norm, choose, w_qkv)


def value_kernel(norm_ref, choose_ref, w_ref, out_ref, products):
    step = pl.program_id(0)
    rows, depth = norm_ref.shape
    comps, _, heads, _ = w_ref.shape
    block_products(
        norm_ref, w_ref[:, 0].reshape(comps * heads, depth), products, step * (depth // BLOCK)
    )

    @pl.when(step == pl.num_programs(0) - 1)
    def _():
        samples = out_ref.shape[0]
        for tile in range(rows // TILE):
            out_ref[:, tile * TILE : (tile + 1) * TILE, :] = (
                summed(choose_ref, products, tile)
                .reshape(samples, TILE, comps * heads)
                .astype(BF16)
            )


def values_of(norm, choose, w_qkv):
    rows, width = norm.shape
    samples = choose.shape[1] // TILE
    comps, _, heads, _ = w_qkv.shape
    depth = width // 2
    columns = comps * heads
    return pl.pallas_call(
        value_kernel,
        grid=(width // depth,),
        out_shape=jax.ShapeDtypeStruct((samples, rows, columns), BF16),
        in_specs=[
            pl.BlockSpec((rows, depth), lambda k: (0, k)),
            pl.BlockSpec(choose.shape, lambda k: (0, 0, 0)),
            pl.BlockSpec((comps, 1, heads, depth), lambda k: (0, 2, 0, k)),
        ],
        out_specs=pl.BlockSpec((samples, rows, columns), lambda k: (0, 0, 0)),
        scratch_shapes=[pltpu.VMEM((width // BLOCK, rows, columns), BF16)],
        compiler_params=pltpu.CompilerParams(vmem_limit_bytes=54 * MIB),
        cost_estimate=pl.CostEstimate(
            flops=8 * rows * width * columns,
            bytes_accessed=2 * (norm.size + choose.size + columns * width),
            transcendentals=0,
        ),
        name="value_rows",
    )(norm, choose, w_qkv)


def erf(x):
    x = jnp.clip(x, -4.0, 4.0)
    s = x * x
    top = s * -2.72614225801306e-10 + 2.77068142495902e-08
    for c in (
        -2.10102402082508e-06,
        -5.69250639462346e-05,
        -7.34990630326855e-04,
        -2.95459980854025e-03,
        -1.60960333262415e-02,
    ):
        top = top * s + c
    low = s * -1.45660718464996e-05 + -2.13374055278905e-04
    for c in (-1.68282697438203e-03, -7.37332916720468e-03, -1.42647390514189e-02):
        low = low * s + c
    return x * top / low


def hidden_kernel(norm_ref, choose_ref, up_ref, out_ref, products):
    step = pl.program_id(1)
    rows, depth = norm_ref.shape
    samples, units = out_ref.shape
    block_products(norm_ref, up_ref, products, step * (depth // BLOCK))

    @pl.when(step == pl.num_programs(1) - 1)
    def _():
        total = jnp.zeros((samples, units), F32)
        for tile in range(rows // TILE):
            v = summed(choose_ref, products, tile)
            active = (0.5 * v) * (1.0 + erf(v * math.sqrt(0.5)))
            total = total + jnp.sum(active.reshape(samples, TILE, units), axis=1)
        out_ref[...] = total * (1.0 / rows)


def hidden_part(norm, choose, w_up, first, tiles):
    rows, width = norm.shape
    samples = choose.shape[1] // TILE
    depth = width // 2
    return pl.pallas_call(
        hidden_kernel,
        grid=(tiles, width // depth),
        out_shape=jax.ShapeDtypeStruct((samples, tiles * UNITS), F32),
        in_specs=[
            pl.BlockSpec((rows, depth), lambda i, k: (0, k)),
            pl.BlockSpec(choose.shape, lambda i, k: (0, 0, 0)),
            pl.BlockSpec((UNITS, depth), lambda i, k: (first + i, k)),
        ],
        out_specs=pl.BlockSpec((samples, UNITS), lambda i, k: (0, i)),
        scratch_shapes=[pltpu.VMEM((width // BLOCK, rows, UNITS), BF16)],
        compiler_params=pltpu.CompilerParams(vmem_limit_bytes=54 * MIB),
        cost_estimate=pl.CostEstimate(
            flops=8 * rows * width * UNITS * tiles,
            bytes_accessed=2 * (norm.size + choose.size + UNITS * tiles * width),
            transcendentals=samples * rows * UNITS * tiles,
        ),
        name="hidden_part",
    )(norm, choose, w_up)


def down_kernel(pooled_ref, down_ref, out_ref):
    samples = pooled_ref.shape[0]
    mean = pooled_ref[...]
    mean = jnp.concatenate([mean, jnp.zeros_like(mean)], axis=0).astype(BF16)
    part = jnp.dot(mean, down_ref[...], preferred_element_type=F32)[:samples]

    @pl.when(pl.program_id(0) == 0)
    def _():
        out_ref[...] = part

    @pl.when(pl.program_id(0) > 0)
    def _():
        out_ref[...] += part


def down_part(pooled, w_down, first):
    samples, units = pooled.shape
    width = w_down.shape[1]
    return pl.pallas_call(
        down_kernel,
        grid=(units // UNITS,),
        out_shape=jax.ShapeDtypeStruct((samples, width), F32),
        in_specs=[
            pl.BlockSpec((samples, UNITS), lambda i: (0, i)),
            pl.BlockSpec((UNITS, width), lambda i: (first + i, 0)),
        ],
        out_specs=pl.BlockSpec((samples, width), lambda i: (0, 0)),
        compiler_params=pltpu.CompilerParams(vmem_limit_bytes=54 * MIB),
        cost_estimate=pl.CostEstimate(
            flops=32 * units * width, bytes_accessed=2 * units * width, transcendentals=0
        ),
        name="down_part",
    )(pooled, w_down)


def attention_kernel(items, x_ref, query_gain_ref, key_gain_ref, out_ref):
    parts, _, both, rows = x_ref.shape
    comps = both // 2
    head_dim = parts * comps

    def normed(values, gain_ref):
        values = values.reshape(head_dim, rows)
        average = jnp.mean(values, axis=0, keepdims=True)
        centered = values - average
        spread_sq = jnp.mean(centered * centered, axis=0, keepdims=True)
        return (centered * lax.rsqrt(spread_sq + 1e-06) * gain_ref[...]).astype(BF16)

    for j in range(items):
        x = x_ref[:, j].astype(F32)
        query = normed(x[:, :comps], query_gain_ref)
        key = normed(x[:, comps:], key_gain_ref)
        scores = lax.dot_general(
            query, key, (((0,), (0,)), ((), ())), preferred_element_type=F32
        )
        e = jnp.exp2(scores * (math.log2(math.e) / math.sqrt(head_dim)))
        weights = (e * (1.0 / jnp.sum(e, axis=1, keepdims=True))).astype(BF16)
        out_ref[j : j + 1, :] = jnp.sum(weights.astype(F32), axis=0, keepdims=True) * (1.0 / rows)


def key_weights(exchanged, query_gain, key_gain):
    parts, items, both, rows = exchanged.shape
    head_dim = parts * both // 2
    return pl.pallas_call(
        functools.partial(attention_kernel, items),
        out_shape=jax.ShapeDtypeStruct((items, rows), F32),
        compiler_params=pltpu.CompilerParams(vmem_limit_bytes=16 * MIB),
        cost_estimate=pl.CostEstimate(
            flops=2 * items * rows * rows * head_dim,
            bytes_accessed=2 * exchanged.size,
            transcendentals=items * rows * rows,
        ),
        name="key_weights",
    )(exchanged, query_gain.reshape(head_dim, 1), key_gain.reshape(head_dim, 1))


def feature_kernel(key_ref, value_ref, proj_ref, hidden_ref, token_ref, out_ref, attended):
    step = pl.program_id(0)
    parts, pieces, _ = key_ref.shape
    samples, rows, columns = value_ref.shape
    chunks = pieces // samples
    heads = parts * chunks

    @pl.when(step == 0)
    def _():
        row = lax.broadcasted_iota(jnp.int32, (heads, columns), 0)
        column = lax.broadcasted_iota(jnp.int32, (heads, columns), 1)
        source, piece = lax.rem(row, parts), row // parts
        head = jnp.where(
            piece == 0, heads - parts + source, source * (chunks - 1) + piece - 1
        )
        own = lax.rem(column, heads) == head
        results = []
        for m in range(samples):
            key = jnp.concatenate(
                [
                    key_ref[:, c * samples + m, :].astype(F32)
                    for c in range(chunks)
                ], axis=0
            )
            product = jnp.dot(key.astype(BF16), value_ref[m], preferred_element_type=F32)
            results.append(jnp.sum(jnp.where(own, product, 0.0), axis=0, keepdims=True))
        results.append(jnp.zeros((16 - samples, columns), F32))
        attended[...] = jnp.concatenate(results, axis=0).astype(BF16)

    part = jnp.dot(attended[...], proj_ref[...], preferred_element_type=F32)[:samples]
    part = part + hidden_ref[...]
    part = part + jnp.sum(token_ref[...].astype(F32), axis=0, keepdims=True) * (1.0 / rows)
    width = out_ref.shape[2]
    for j in range(out_ref.shape[0]):
        out_ref[j] = part[:, j * width : (j + 1) * width]


def feature_part(key_mean, value, w_proj, hidden, tokens, steps):
    parts = key_mean.shape[0]
    samples, rows, columns = value.shape
    own_rows, width = tokens.shape
    cut = width // steps
    return pl.pallas_call(
        feature_kernel,
        grid=(steps,),
        out_shape=jax.ShapeDtypeStruct((parts, samples, width // parts), F32),
        in_specs=[
            pl.BlockSpec(key_mean.shape, lambda i: (0, 0, 0)),
            pl.BlockSpec(value.shape, lambda i: (0, 0, 0)),
            pl.BlockSpec((columns, cut), lambda i: (0, i)),
            pl.BlockSpec((samples, cut), lambda i: (0, i)),
            pl.BlockSpec((own_rows, cut), lambda i: (0, i)),
        ],
        out_specs=pl.BlockSpec((parts // steps, samples, width // parts), lambda i: (i, 0, 0)),
        scratch_shapes=[pltpu.VMEM((16, columns), BF16)],
        compiler_params=pltpu.CompilerParams(vmem_limit_bytes=16 * MIB),
        cost_estimate=pl.CostEstimate(
            flops=2 * samples * rows * columns * 2 + 32 * columns * width,
            bytes_accessed=2 * columns * width + 2 * value.size,
            transcendentals=0,
        ),
        name="feature_part",
    )(key_mean, value, w_proj, hidden, tokens)


def pooled_logits(feature, final_gain, w_head):
    highest = lax.Precision.HIGHEST
    gain_head = jnp.dot(final_gain[None], w_head.astype(F32), precision=highest)
    mean = jnp.mean(feature, axis=-1, keepdims=True)
    centered = feature - mean
    spread = jnp.sum(centered * centered, axis=-1, keepdims=True)
    logits = jnp.dot(centered * final_gain, w_head.astype(F32), precision=highest)
    columns = feature.shape[1]
    samples, classes = logits.shape
    bits = 1
    while bits < lax.axis_size("inp"):
        sent = jnp.concatenate(
            [
                jnp.concatenate([logits, mean, spread], axis=1),
                jnp.pad(gain_head, ((0, 0), (0, 2))),
            ],
            axis=0,
        )
        other = permuted(sent, bits)
        other_mean = other[:samples, classes : classes + 1]
        joint = 0.5 * (mean + other_mean)
        logits = (
            logits
            + other[:samples, :classes]
            + (mean - joint) * gain_head
            + (other_mean - joint) * other[samples:, :classes]
        )
        gap = mean - other_mean
        spread = spread + other[:samples, classes + 1 :] + gap * gap * (0.5 * columns)
        gain_head = gain_head + other[samples:, :classes]
        mean = joint
        columns = 2 * columns
        bits = 2 * bits
    scale = lax.rsqrt(spread / columns + 1e-06)
    return mean, scale, logits * scale


def pipelined(
    tokens,
    dropout_masks,
    input_gain,
    w_qkv,
    w_up,
    query_gain,
    key_gain,
    w_proj,
    w_down,
    final_gain,
    w_head,
):
    n_parts = lax.axis_size("inp")
    me = lax.axis_index("inp")
    model_width = tokens.shape[1]
    n_comps, _, n_heads, _ = w_qkv.shape
    choose = choosers(dropout_masks)
    pieces, choose = gathered_pieces(*own_norm(tokens, input_gain), choose)
    norm = placed(pieces, me)
    together = lax.optimization_barrier

    def exchange(array):
        heads, samples, both, rows = array.shape
        array = array.reshape(n_parts, heads // n_parts * samples, both, rows)
        return lax.all_to_all(array, "inp", split_axis=0, concat_axis=0, tiled=True)

    ahead = n_parts
    behind = n_heads - ahead
    first = query_key(norm, choose, w_qkv, behind // ahead, ahead)
    second = query_key(norm, choose, w_qkv, 0, behind)
    value = values_of(norm, choose, w_qkv)
    first = exchange(first)
    second, value = together((second, value))
    second = exchange(second)
    norm, first = together((norm, first))
    tiles = w_up.shape[0] // UNITS // 2
    pooled = hidden_part(norm, choose, w_up, 0, tiles)
    more_pooled = hidden_part(norm, choose, w_up, tiles, tiles)
    hidden = down_part(pooled, w_down, 0)
    key_mean = key_weights(first, query_gain, key_gain)
    more = key_weights(second, query_gain, key_gain)
    hidden, more_pooled, key_mean, more = together((hidden, more_pooled, key_mean, more))
    key_mean = jnp.concatenate([key_mean, more], axis=0).astype(BF16)
    hidden = hidden + down_part(more_pooled, w_down, tiles)
    key_mean = lax.all_to_all(
        jnp.broadcast_to(key_mean[None], (n_parts,) + key_mean.shape),
        "inp",
        split_axis=0,
        concat_axis=0,
        tiled=True,
    )
    partial_feature = feature_part(
        key_mean, value, w_proj.reshape(n_comps * n_heads, model_width), hidden, tokens, 4
    )
    slice_width = model_width // n_parts
    feature = jnp.sum(
        lax.all_to_all(partial_feature, "inp", split_axis=0, concat_axis=0, tiled=True), axis=0
    )
    gain = lax.dynamic_slice_in_dim(final_gain, me * slice_width, slice_width, 0)
    mean, scale, raw_logits = pooled_logits(feature, gain, w_head)
    embedding = (feature - mean) * scale * gain
    logits = soft_cap * jnp.tanh(raw_logits / soft_cap)
    return (embedding[None], bald_score(logits[None]))


def local(
    tokens,
    dropout_masks,
    input_gain,
    w_qkv,
    w_up,
    query_gain,
    key_gain,
    w_proj,
    w_down,
    final_gain,
    w_head,
):
    n_parts = lax.axis_size("inp")
    local_rows, model_width = tokens.shape
    n_masks, all_rows, n_blocks = dropout_masks.shape
    block_width = model_width // n_blocks
    n_comps, three_kinds, n_heads, ignored_width = w_qkv.shape
    n_units = w_up.shape[0]
    head_dim = n_comps * n_parts
    images = all_rows // PATCHES
    qkv_cols = three_kinds * n_heads * n_comps
    items_dev = n_masks * n_heads // n_parts
    highest = lax.Precision.HIGHEST
    joined_weight = jnp.concatenate(
        [jnp.transpose(w_qkv, (1, 2, 0, 3)).reshape(qkv_cols, model_width), w_up], axis=0
    )
    row_piece = lax.all_gather(tokens, "inp", axis=0, tiled=True)
    row_count = row_piece.shape[0]
    normed = norm_last(row_piece.astype(jnp.float32), input_gain).astype(jnp.bfloat16)
    masked = (
        normed.reshape(1, row_count, n_blocks, block_width)
        * dropout_masks.astype(jnp.bfloat16)[..., None]
    )
    masked = masked.reshape(n_masks, row_count, model_width)
    result = jnp.einsum("mkd,cd->mck", masked, joined_weight, preferred_element_type=jnp.float32)
    projected = 2.0 * result
    qkv_half = (
        projected[:, :qkv_cols]
        .astype(jnp.bfloat16)
        .reshape(n_masks, three_kinds, n_heads * n_comps, all_rows)
    )
    item_shape = (n_parts, items_dev, n_comps, all_rows)
    query_send = qkv_half[:, 0].reshape(item_shape)
    key_send = qkv_half[:, 1].reshape(item_shape)
    value_send = qkv_half[:, 2].reshape(item_shape)
    activated = jax.nn.gelu(projected[:, qkv_cols:], approximate=False)
    pooled_hidden = jnp.mean(activated.reshape(n_masks, n_units, images, PATCHES), axis=-1).astype(
        jnp.bfloat16
    )
    query_in = lax.all_to_all(query_send, "inp", split_axis=0, concat_axis=2, tiled=True)
    key_in = lax.all_to_all(key_send, "inp", split_axis=0, concat_axis=2, tiled=True)
    value_in = lax.all_to_all(value_send, "inp", split_axis=0, concat_axis=2, tiled=True)
    n_items = query_in.shape[1]
    shape_four = (n_items, head_dim, images, PATCHES)
    query_norm = norm_second(query_in.reshape(shape_four).astype(jnp.float32), query_gain).astype(
        jnp.bfloat16
    )
    key_norm = norm_second(key_in.reshape(shape_four).astype(jnp.float32), key_gain).astype(
        jnp.bfloat16
    )
    scores = jnp.einsum(
        "jcip,jciq->jipq", query_norm, key_norm, preferred_element_type=jnp.float32
    ) / math.sqrt(head_dim)
    exp_scores = jnp.exp(scores)
    weights = (exp_scores / jnp.sum(exp_scores, axis=-1, keepdims=True)).astype(jnp.bfloat16)
    query_mean = jnp.sum(weights, axis=2, dtype=jnp.float32) / PATCHES
    pooled = jnp.einsum(
        "jiq,jciq->jic",
        query_mean,
        value_in.reshape(shape_four).astype(jnp.float32),
        precision=highest,
    )
    attended = pooled.astype(jnp.bfloat16)[None]
    returned = lax.all_to_all(attended, "inp", split_axis=3, concat_axis=0, tiled=True)
    returned = returned.reshape(n_masks, n_heads, images, n_comps)
    mixed_sum = jnp.einsum("mhic,chd->imd", returned, w_proj, preferred_element_type=jnp.float32)
    mixed_sum = mixed_sum + jnp.einsum(
        "mfi,fd->imd", pooled_hidden, w_down, preferred_element_type=jnp.float32
    )
    row_ids = lax.axis_index("inp") * local_rows + jnp.arange(local_rows, dtype=jnp.int32)
    row_owner = (row_ids // PATCHES)[None, :] == jnp.arange(images, dtype=jnp.int32)[:, None]
    input_sum = (
        jnp.dot(row_owner.astype(jnp.bfloat16), tokens, preferred_element_type=jnp.float32)
        / PATCHES
    )
    partial_feature = mixed_sum + input_sum[:, None, :]
    feature = lax.psum(partial_feature, "inp")
    normalized = norm_last(feature, final_gain)
    slice_width = model_width // n_parts
    embedding = lax.dynamic_slice_in_dim(
        normalized, lax.axis_index("inp") * slice_width, slice_width, 2
    )
    logit_part = jnp.einsum(
        "imd,dc->imc", embedding.astype(jnp.bfloat16), w_head, preferred_element_type=jnp.float32
    )
    raw_logits = lax.psum(logit_part, "inp")
    logits = soft_cap * jnp.tanh(raw_logits / soft_cap)
    return (embedding, bald_score(logits))


def solution(mesh):
    fits = mesh.shape["inp"] == PIPELINED_PARTS
    return jax.shard_map(
        pipelined if fits else local,
        mesh=mesh,
        in_specs=(
            P(("groups", "inp"), None),
            P(None, "groups", None),
            P(),
            P("inp", None, None, None),
            P("inp", None),
            P(),
            P(),
            P("inp", None, None),
            P("inp", None),
            P(),
            P("inp", None),
        ),
        out_specs=(P("groups", None, "inp"), P("groups")),
        check_vma=False,
    )
```

```python
import functools
import math

import jax
import jax.numpy as jnp
from jax import lax
from jax.experimental import pallas as pl
from jax.experimental.pallas import tpu as pltpu
from jax.sharding import PartitionSpec as P

PATCHES = 256


soft_cap = 20.0
PIPELINED_PARTS = 16
UNITS = 256
F32 = jnp.float32
BF16 = jnp.bfloat16
MIB = 1024 * 1024


def norm_last(values, gain):
    average = jnp.mean(values, axis=-1, keepdims=True)
    centered = values - average
    spread_sq = jnp.mean(centered * centered, axis=-1, keepdims=True)
    return centered * lax.rsqrt(spread_sq + 1e-06) * gain


def norm_second(values, gain):
    average = jnp.mean(values, axis=1, keepdims=True)
    centered = values - average
    spread_sq = jnp.mean(centered * centered, axis=1, keepdims=True)
    return centered * lax.rsqrt(spread_sq + 1e-06) * gain[None, :, None, None]


def bald_score(logits):
    exp_logits = jnp.exp(logits)
    totals = jnp.sum(exp_logits, axis=-1, keepdims=True)
    sample_probs = exp_logits / totals
    entropy = jnp.log(totals[..., 0]) - jnp.sum(sample_probs * logits, axis=-1)
    mean_probs = jnp.mean(sample_probs, axis=1)
    joint = -jnp.sum(mean_probs * jnp.log(mean_probs), axis=-1)
    return joint - jnp.mean(entropy, axis=1)


def permuted(array, bits):
    count = lax.axis_size("inp")
    return lax.ppermute(array, "inp", [(i, i ^ bits) for i in range(count)])


def own_norm_kernel(x_ref, gain_ref, first_ref, second_ref):
    y = norm_last(x_ref[...].astype(F32), gain_ref[...]).astype(BF16)
    cut = first_ref.shape[1]
    first_ref[...] = y[:, :cut]
    second_ref[...] = y[:, cut:]


def own_norm(tokens, gain):
    rows, width = tokens.shape
    cut = width // 3 * 2
    return pl.pallas_call(
        own_norm_kernel,
        out_shape=(
            jax.ShapeDtypeStruct((rows, cut), BF16),
            jax.ShapeDtypeStruct((rows, width - cut), BF16),
        ),
        compiler_params=pltpu.CompilerParams(vmem_limit_bytes=60 * MIB),
        name="own_norm",
    )(tokens, gain.reshape(1, width))


def gathered_pieces(first, second, beside):
    along_z = jnp.stack([first] + [permuted(first, 4 * k) for k in range(1, 4)])
    pair = jnp.stack([second, permuted(second, 2)])
    along_z, pair, beside = lax.optimization_barrier((along_z, pair, beside))
    across_y = permuted(along_z, 2)
    moved = [permuted(pair, 4 * k) for k in range(1, 4)]
    across_y, *moved = lax.optimization_barrier((across_y, *moved))
    pieces = [
        (0, [4 * k for k in range(4)], along_z),
        (0, [4 * k + 2 for k in range(4)], across_y),
    ]
    for k, array in enumerate([pair, *moved]):
        pieces.append((first.shape[1], [4 * k, 4 * k + 2], array))
    pieces = pieces + [
        (side, [b ^ 1 for b in bits], permuted(array, 1)) for side, bits, array in pieces
    ]
    return pieces, beside


def place_kernel(layout, me_ref, *refs):
    sources, out_ref = refs[:-1], refs[-1]
    me = me_ref[0]
    for (side, bits), source in zip(layout, sources, strict=True):
        _, rows, columns = source.shape
        for at, bit in enumerate(bits):
            start = pl.multiple_of((me ^ bit) * rows, rows)
            out_ref[pl.ds(start, rows), side : side + columns] = source[at]


def placed(pieces, me):
    rows = pieces[0][2].shape[1]
    total = rows * sum(len(bits) for side, bits, _ in pieces if side == 0)
    width = sum(array.size for _, _, array in pieces) // total
    layout = [(side, bits) for side, bits, _ in pieces]
    return pl.pallas_call(
        functools.partial(place_kernel, layout),
        out_shape=jax.ShapeDtypeStruct((total, width), BF16),
        in_specs=[pl.BlockSpec(memory_space=pltpu.SMEM)]
        + [pl.BlockSpec(memory_space=pltpu.VMEM)] * len(pieces),
        out_specs=pl.BlockSpec(memory_space=pltpu.VMEM),
        compiler_params=pltpu.CompilerParams(vmem_limit_bytes=50 * MIB),
        name="place_rows",
    )(me.reshape(1), *[array for _, _, array in pieces])


ACROSS = (((1,), (1,)), ((), ()))
TILE = 16
BLOCK = 128


def choosers(dropout_masks):
    samples, rows, blocks = dropout_masks.shape
    tiles = rows // TILE
    kept = dropout_masks.astype(BF16).reshape(samples, tiles, TILE, blocks)
    kept = jnp.transpose(kept, (1, 0, 2, 3)).reshape(tiles, samples * TILE, blocks)
    column = jnp.arange(blocks * TILE)
    spread = (column[None] // TILE == jnp.arange(blocks)[:, None]).astype(BF16)
    own = jnp.arange(samples * TILE)[:, None] % TILE == column[None] % TILE
    wide = jnp.einsum("trb,bc->trc", kept, spread, preferred_element_type=F32)
    return jnp.where(own[None], 2.0 * wide, 0.0).astype(BF16)


def block_products(norm_ref, weight, products, first):
    for j in range(weight.shape[1] // BLOCK):
        at = slice(j * BLOCK, (j + 1) * BLOCK)
        products[first + j] = lax.dot_general(
            norm_ref[:, at], weight[:, at], ACROSS, preferred_element_type=F32
        ).astype(BF16)


def summed(choose_ref, products, tile):
    blocks, _, columns = products.shape
    part = products[:, tile * TILE : (tile + 1) * TILE, :].reshape(blocks * TILE, columns)
    return jnp.dot(choose_ref[tile], part, preferred_element_type=F32)


def query_key_kernel(norm_ref, choose_ref, w_ref, out_ref, products, sums, turned):
    step = pl.program_id(0)
    rows, depth = norm_ref.shape
    comps, kinds, heads, _ = w_ref.shape
    columns = comps * kinds * heads
    block_products(
        norm_ref, w_ref[...].reshape(columns, depth), products, step * (depth // BLOCK)
    )

    @pl.when(step == pl.num_programs(0) - 1)
    def _():
        samples = sums.shape[0]
        for tile in range(rows // TILE):
            sums[:, tile * TILE : (tile + 1) * TILE, :] = summed(
                choose_ref, products, tile
            ).reshape(samples, TILE, columns)
        for m in range(samples):
            for part in range(rows // 128):
                at = slice(part * 128, (part + 1) * 128)
                turned[m * (rows // 128) + part] = sums[m, at, :].T
            for part in range(rows // 128):
                at = slice(part * 128, (part + 1) * 128)
                held = turned.at[m * (rows // 128) + part]
                for h in range(heads):
                    both = [
                        held[pl.ds(t * heads + h, comps, stride=kinds * heads), :]
                        for t in range(kinds)
                    ]
                    out_ref[h, m, :, at] = jnp.concatenate(both, axis=0).astype(BF16)


def query_key(norm, choose, w_qkv, chunk, heads):
    rows, width = norm.shape
    samples = choose.shape[1] // TILE
    comps = w_qkv.shape[0]
    depth = width // 2
    columns = 2 * comps * heads
    shape = (heads, samples, 2 * comps, rows)
    return pl.pallas_call(
        query_key_kernel,
        grid=(width // depth,),
        out_shape=jax.ShapeDtypeStruct(shape, BF16),
        in_specs=[
            pl.BlockSpec((rows, depth), lambda k: (0, k)),
            pl.BlockSpec(choose.shape, lambda k: (0, 0, 0)),
            pl.BlockSpec((comps, 2, heads, depth), lambda k: (0, 0, chunk, k)),
        ],
        out_specs=pl.BlockSpec(shape, lambda k: (0, 0, 0, 0)),
        scratch_shapes=[
            pltpu.VMEM((width // BLOCK, rows, columns), BF16),
            pltpu.VMEM((samples, rows, columns), F32),
            pltpu.VMEM((samples * rows // 128, columns, 128), F32),
        ],
        compiler_params=pltpu.CompilerParams(vmem_limit_bytes=50 * MIB),
        cost_estimate=pl.CostEstimate(
            flops=8 * rows * width * columns,
            bytes_accessed=2 * (norm.size + choose.size + columns * width),
            transcendentals=0,
        ),
        name="query_key",
    )(norm, choose, w_qkv)


def value_kernel(norm_ref, choose_ref, w_ref, out_ref, products):
    step = pl.program_id(0)
    rows, depth = norm_ref.shape
    comps, _, heads, _ = w_ref.shape
    block_products(
        norm_ref, w_ref[:, 0].reshape(comps * heads, depth), products, step * (depth // BLOCK)
    )

    @pl.when(step == pl.num_programs(0) - 1)
    def _():
        samples = out_ref.shape[0]
        for tile in range(rows // TILE):
            out_ref[:, tile * TILE : (tile + 1) * TILE, :] = (
                summed(choose_ref, products, tile)
                .reshape(samples, TILE, comps * heads)
                .astype(BF16)
            )


def values_of(norm, choose, w_qkv):
    rows, width = norm.shape
    samples = choose.shape[1] // TILE
    comps, _, heads, _ = w_qkv.shape
    depth = width // 2
    columns = comps * heads
    return pl.pallas_call(
        value_kernel,
        grid=(width // depth,),
        out_shape=jax.ShapeDtypeStruct((samples, rows, columns), BF16),
        in_specs=[
            pl.BlockSpec((rows, depth), lambda k: (0, k)),
            pl.BlockSpec(choose.shape, lambda k: (0, 0, 0)),
            pl.BlockSpec((comps, 1, heads, depth), lambda k: (0, 2, 0, k)),
        ],
        out_specs=pl.BlockSpec((samples, rows, columns), lambda k: (0, 0, 0)),
        scratch_shapes=[pltpu.VMEM((width // BLOCK, rows, columns), BF16)],
        compiler_params=pltpu.CompilerParams(vmem_limit_bytes=50 * MIB),
        cost_estimate=pl.CostEstimate(
            flops=8 * rows * width * columns,
            bytes_accessed=2 * (norm.size + choose.size + columns * width),
            transcendentals=0,
        ),
        name="value_rows",
    )(norm, choose, w_qkv)


def erf(x):
    x = jnp.clip(x, -4.0, 4.0)
    s = x * x
    top = s * -2.72614225801306e-10 + 2.77068142495902e-08
    for c in (
        -2.10102402082508e-06,
        -5.69250639462346e-05,
        -7.34990630326855e-04,
        -2.95459980854025e-03,
        -1.60960333262415e-02,
    ):
        top = top * s + c
    low = s * -1.45660718464996e-05 + -2.13374055278905e-04
    for c in (-1.68282697438203e-03, -7.37332916720468e-03, -1.42647390514189e-02):
        low = low * s + c
    return x * top / low


def hidden_kernel(norm_ref, choose_ref, up_ref, out_ref, products):
    step = pl.program_id(1)
    rows, depth = norm_ref.shape
    samples, units = out_ref.shape
    block_products(norm_ref, up_ref, products, step * (depth // BLOCK))

    @pl.when(step == pl.num_programs(1) - 1)
    def _():
        total = jnp.zeros((samples, units), F32)
        for tile in range(rows // TILE):
            v = summed(choose_ref, products, tile)
            active = (0.5 * v) * (1.0 + erf(v * math.sqrt(0.5)))
            total = total + jnp.sum(active.reshape(samples, TILE, units), axis=1)
        out_ref[...] = total * (1.0 / rows)


def hidden_part(norm, choose, w_up, first, tiles):
    rows, width = norm.shape
    samples = choose.shape[1] // TILE
    depth = width // 2
    return pl.pallas_call(
        hidden_kernel,
        grid=(tiles, width // depth),
        out_shape=jax.ShapeDtypeStruct((samples, tiles * UNITS), F32),
        in_specs=[
            pl.BlockSpec((rows, depth), lambda i, k: (0, k)),
            pl.BlockSpec(choose.shape, lambda i, k: (0, 0, 0)),
            pl.BlockSpec((UNITS, depth), lambda i, k: (first + i, k)),
        ],
        out_specs=pl.BlockSpec((samples, UNITS), lambda i, k: (0, i)),
        scratch_shapes=[pltpu.VMEM((width // BLOCK, rows, UNITS), BF16)],
        compiler_params=pltpu.CompilerParams(vmem_limit_bytes=50 * MIB),
        cost_estimate=pl.CostEstimate(
            flops=8 * rows * width * UNITS * tiles,
            bytes_accessed=2 * (norm.size + choose.size + UNITS * tiles * width),
            transcendentals=samples * rows * UNITS * tiles,
        ),
        name="hidden_part",
    )(norm, choose, w_up)


def down_kernel(pooled_ref, down_ref, out_ref):
    samples = pooled_ref.shape[0]
    mean = pooled_ref[...]
    mean = jnp.concatenate([mean, jnp.zeros_like(mean)], axis=0).astype(BF16)
    part = jnp.dot(mean, down_ref[...], preferred_element_type=F32)[:samples]

    @pl.when(pl.program_id(0) == 0)
    def _():
        out_ref[...] = part

    @pl.when(pl.program_id(0) > 0)
    def _():
        out_ref[...] += part


def down_part(pooled, w_down, first):
    samples, units = pooled.shape
    width = w_down.shape[1]
    return pl.pallas_call(
        down_kernel,
        grid=(units // UNITS,),
        out_shape=jax.ShapeDtypeStruct((samples, width), F32),
        in_specs=[
            pl.BlockSpec((samples, UNITS), lambda i: (0, i)),
            pl.BlockSpec((UNITS, width), lambda i: (first + i, 0)),
        ],
        out_specs=pl.BlockSpec((samples, width), lambda i: (0, 0)),
        compiler_params=pltpu.CompilerParams(vmem_limit_bytes=50 * MIB),
        cost_estimate=pl.CostEstimate(
            flops=32 * units * width, bytes_accessed=2 * units * width, transcendentals=0
        ),
        name="down_part",
    )(pooled, w_down)


def attention_kernel(items, x_ref, query_gain_ref, key_gain_ref, out_ref):
    parts, _, both, rows = x_ref.shape
    comps = both // 2
    head_dim = parts * comps

    def normed(values, gain_ref):
        values = values.reshape(head_dim, rows)
        average = jnp.mean(values, axis=0, keepdims=True)
        centered = values - average
        spread_sq = jnp.mean(centered * centered, axis=0, keepdims=True)
        return (centered * lax.rsqrt(spread_sq + 1e-06) * gain_ref[...]).astype(BF16)

    for j in range(items):
        x = x_ref[:, j].astype(F32)
        query = normed(x[:, :comps], query_gain_ref)
        key = normed(x[:, comps:], key_gain_ref)
        scores = lax.dot_general(
            query, key, (((0,), (0,)), ((), ())), preferred_element_type=F32
        )
        e = jnp.exp2(scores * (math.log2(math.e) / math.sqrt(head_dim)))
        weights = (e * (1.0 / jnp.sum(e, axis=1, keepdims=True))).astype(BF16)
        out_ref[j : j + 1, :] = jnp.sum(weights.astype(F32), axis=0, keepdims=True) * (1.0 / rows)


def key_weights(exchanged, query_gain, key_gain):
    parts, items, both, rows = exchanged.shape
    head_dim = parts * both // 2
    return pl.pallas_call(
        functools.partial(attention_kernel, items),
        out_shape=jax.ShapeDtypeStruct((items, rows), F32),
        compiler_params=pltpu.CompilerParams(vmem_limit_bytes=50 * MIB),
        cost_estimate=pl.CostEstimate(
            flops=2 * items * rows * rows * head_dim,
            bytes_accessed=2 * exchanged.size,
            transcendentals=items * rows * rows,
        ),
        name="key_weights",
    )(exchanged, query_gain.reshape(head_dim, 1), key_gain.reshape(head_dim, 1))


def feature_kernel(key_ref, value_ref, proj_ref, hidden_ref, token_ref, out_ref, attended):
    step = pl.program_id(0)
    parts, pieces, _ = key_ref.shape
    samples, rows, columns = value_ref.shape
    chunks = pieces // samples
    heads = parts * chunks

    @pl.when(step == 0)
    def _():
        row = lax.broadcasted_iota(jnp.int32, (heads, columns), 0)
        column = lax.broadcasted_iota(jnp.int32, (heads, columns), 1)
        source, piece = lax.rem(row, parts), row // parts
        head = jnp.where(
            piece == 0, heads - parts + source, source * (chunks - 1) + piece - 1
        )
        own = lax.rem(column, heads) == head
        results = []
        for m in range(samples):
            key = jnp.concatenate(
                [
                    key_ref[:, c * samples + m, :].astype(F32)
                    for c in range(chunks)
                ], axis=0
            )
            product = jnp.dot(key.astype(BF16), value_ref[m], preferred_element_type=F32)
            results.append(jnp.sum(jnp.where(own, product, 0.0), axis=0, keepdims=True))
        results.append(jnp.zeros((16 - samples, columns), F32))
        attended[...] = jnp.concatenate(results, axis=0).astype(BF16)

    part = jnp.dot(attended[...], proj_ref[...], preferred_element_type=F32)[:samples]
    part = part + hidden_ref[...]
    part = part + jnp.sum(token_ref[...].astype(F32), axis=0, keepdims=True) * (1.0 / rows)
    width = out_ref.shape[2]
    for j in range(out_ref.shape[0]):
        out_ref[j] = part[:, j * width : (j + 1) * width]


def feature_part(key_mean, value, w_proj, hidden, tokens, steps):
    parts = key_mean.shape[0]
    samples, rows, columns = value.shape
    own_rows, width = tokens.shape
    cut = width // steps
    return pl.pallas_call(
        feature_kernel,
        grid=(steps,),
        out_shape=jax.ShapeDtypeStruct((parts, samples, width // parts), F32),
        in_specs=[
            pl.BlockSpec(key_mean.shape, lambda i: (0, 0, 0)),
            pl.BlockSpec(value.shape, lambda i: (0, 0, 0)),
            pl.BlockSpec((columns, cut), lambda i: (0, i)),
            pl.BlockSpec((samples, cut), lambda i: (0, i)),
            pl.BlockSpec((own_rows, cut), lambda i: (0, i)),
        ],
        out_specs=pl.BlockSpec((parts // steps, samples, width // parts), lambda i: (i, 0, 0)),
        scratch_shapes=[pltpu.VMEM((16, columns), BF16)],
        compiler_params=pltpu.CompilerParams(vmem_limit_bytes=40 * MIB),
        cost_estimate=pl.CostEstimate(
            flops=2 * samples * rows * columns * 2 + 32 * columns * width,
            bytes_accessed=2 * columns * width + 2 * value.size,
            transcendentals=0,
        ),
        name="feature_part",
    )(key_mean, value, w_proj, hidden, tokens)


def joined(mine, other, columns):
    classes = mine.shape[1] - 2
    samples = mine.shape[0] - 1
    mean, other_mean = (x[:samples, classes : classes + 1] for x in (mine, other))
    joint = 0.5 * (mean + other_mean)
    logits = (
        mine[:samples, :classes]
        + other[:samples, :classes]
        + (mean - joint) * mine[samples:, :classes]
        + (other_mean - joint) * other[samples:, :classes]
    )
    gap = mean - other_mean
    spread = mine[:samples, classes + 1 :] + other[:samples, classes + 1 :]
    spread = spread + gap * gap * (0.5 * columns)
    return logits, joint, spread, mine[samples:, :classes] + other[samples:, :classes]


def packed(logits, mean, spread, gain_head):
    rows = jnp.concatenate([logits, mean, spread], axis=1)
    return jnp.concatenate([rows, jnp.pad(gain_head, ((0, 0), (0, 2)))], axis=0)


def finish_kernel(columns, mine_ref, other_ref, feature_ref, gain_ref, out_ref, bald_ref):
    logits, mean, spread, _ = joined(mine_ref[...], other_ref[...], columns)
    scale = lax.rsqrt(spread / (2 * columns) + 1e-06)
    out_ref[...] = (feature_ref[...] - mean) * scale * gain_ref[...]
    logits = soft_cap * jnp.tanh(logits * scale / soft_cap)
    samples = logits.shape[0]
    exp_logits = jnp.exp(logits)
    totals = jnp.sum(exp_logits, axis=1, keepdims=True)
    probs = exp_logits / totals
    entropy = jnp.log(totals) - jnp.sum(probs * logits, axis=1, keepdims=True)
    mean_probs = jnp.sum(probs, axis=0, keepdims=True) * (1.0 / samples)
    whole = -jnp.sum(mean_probs * jnp.log(mean_probs), axis=1, keepdims=True)
    bald_ref[...] = whole - jnp.sum(entropy, axis=0, keepdims=True) * (1.0 / samples)


def finished(feature, final_gain, w_head):
    highest = lax.Precision.HIGHEST
    gain_head = jnp.dot(final_gain[None], w_head.astype(F32), precision=highest)
    mean = jnp.mean(feature, axis=-1, keepdims=True)
    centered = feature - mean
    spread = jnp.sum(centered * centered, axis=-1, keepdims=True)
    logits = jnp.dot(centered * final_gain, w_head.astype(F32), precision=highest)
    columns = feature.shape[1]
    mine = packed(logits, mean, spread, gain_head)
    bits = 1
    while 2 * bits < lax.axis_size("inp"):
        mine = packed(*joined(mine, permuted(mine, bits), columns))
        columns = 2 * columns
        bits = 2 * bits
    embedding, score = pl.pallas_call(
        functools.partial(finish_kernel, columns),
        out_shape=(
            jax.ShapeDtypeStruct(feature.shape, F32),
            jax.ShapeDtypeStruct((1, 1), F32),
        ),
        compiler_params=pltpu.CompilerParams(vmem_limit_bytes=16 * MIB),
        name="finish",
    )(mine, permuted(mine, bits), feature, final_gain[None])
    return embedding[None], score.reshape(1)


def pipelined(
    tokens,
    dropout_masks,
    input_gain,
    w_qkv,
    w_up,
    query_gain,
    key_gain,
    w_proj,
    w_down,
    final_gain,
    w_head,
):
    n_parts = lax.axis_size("inp")
    me = lax.axis_index("inp")
    model_width = tokens.shape[1]
    n_comps, _, n_heads, _ = w_qkv.shape
    choose = choosers(dropout_masks)
    pieces, choose = gathered_pieces(*own_norm(tokens, input_gain), choose)
    norm = placed(pieces, me)
    together = lax.optimization_barrier

    def exchange(array):
        heads, samples, both, rows = array.shape
        array = array.reshape(n_parts, heads // n_parts * samples, both, rows)
        return lax.all_to_all(array, "inp", split_axis=0, concat_axis=0, tiled=True)

    ahead = n_parts
    behind = n_heads - ahead
    first = query_key(norm, choose, w_qkv, behind // ahead, ahead)
    second = query_key(norm, choose, w_qkv, 0, behind)
    value = values_of(norm, choose, w_qkv)
    first = exchange(first)
    second, value = together((second, value))
    second = exchange(second)
    norm, first = together((norm, first))
    tiles = w_up.shape[0] // UNITS // 2
    pooled = hidden_part(norm, choose, w_up, 0, tiles)
    more_pooled = hidden_part(norm, choose, w_up, tiles, tiles)
    hidden = down_part(pooled, w_down, 0)
    key_mean = key_weights(first, query_gain, key_gain)
    more = key_weights(second, query_gain, key_gain)
    hidden, more_pooled, key_mean, more = together((hidden, more_pooled, key_mean, more))
    key_mean = jnp.concatenate([key_mean, more], axis=0).astype(BF16)
    hidden = hidden + down_part(more_pooled, w_down, tiles)
    key_mean = lax.all_to_all(
        jnp.broadcast_to(key_mean[None], (n_parts,) + key_mean.shape),
        "inp",
        split_axis=0,
        concat_axis=0,
        tiled=True,
    )
    partial_feature = feature_part(
        key_mean, value, w_proj.reshape(n_comps * n_heads, model_width), hidden, tokens, 4
    )
    slice_width = model_width // n_parts
    feature = jnp.sum(
        lax.all_to_all(partial_feature, "inp", split_axis=0, concat_axis=0, tiled=True), axis=0
    )
    gain = lax.dynamic_slice_in_dim(final_gain, me * slice_width, slice_width, 0)
    return finished(feature, gain, w_head)


def local(
    tokens,
    dropout_masks,
    input_gain,
    w_qkv,
    w_up,
    query_gain,
    key_gain,
    w_proj,
    w_down,
    final_gain,
    w_head,
):
    n_parts = lax.axis_size("inp")
    local_rows, model_width = tokens.shape
    n_masks, all_rows, n_blocks = dropout_masks.shape
    block_width = model_width // n_blocks
    n_comps, three_kinds, n_heads, ignored_width = w_qkv.shape
    n_units = w_up.shape[0]
    head_dim = n_comps * n_parts
    images = all_rows // PATCHES
    qkv_cols = three_kinds * n_heads * n_comps
    items_dev = n_masks * n_heads // n_parts
    highest = lax.Precision.HIGHEST
    joined_weight = jnp.concatenate(
        [jnp.transpose(w_qkv, (1, 2, 0, 3)).reshape(qkv_cols, model_width), w_up], axis=0
    )
    row_piece = lax.all_gather(tokens, "inp", axis=0, tiled=True)
    row_count = row_piece.shape[0]
    normed = norm_last(row_piece.astype(jnp.float32), input_gain).astype(jnp.bfloat16)
    masked = (
        normed.reshape(1, row_count, n_blocks, block_width)
        * dropout_masks.astype(jnp.bfloat16)[..., None]
    )
    masked = masked.reshape(n_masks, row_count, model_width)
    result = jnp.einsum("mkd,cd->mck", masked, joined_weight, preferred_element_type=jnp.float32)
    projected = 2.0 * result
    qkv_half = (
        projected[:, :qkv_cols]
        .astype(jnp.bfloat16)
        .reshape(n_masks, three_kinds, n_heads * n_comps, all_rows)
    )
    item_shape = (n_parts, items_dev, n_comps, all_rows)
    query_send = qkv_half[:, 0].reshape(item_shape)
    key_send = qkv_half[:, 1].reshape(item_shape)
    value_send = qkv_half[:, 2].reshape(item_shape)
    activated = jax.nn.gelu(projected[:, qkv_cols:], approximate=False)
    pooled_hidden = jnp.mean(activated.reshape(n_masks, n_units, images, PATCHES), axis=-1).astype(
        jnp.bfloat16
    )
    query_in = lax.all_to_all(query_send, "inp", split_axis=0, concat_axis=2, tiled=True)
    key_in = lax.all_to_all(key_send, "inp", split_axis=0, concat_axis=2, tiled=True)
    value_in = lax.all_to_all(value_send, "inp", split_axis=0, concat_axis=2, tiled=True)
    n_items = query_in.shape[1]
    shape_four = (n_items, head_dim, images, PATCHES)
    query_norm = norm_second(query_in.reshape(shape_four).astype(jnp.float32), query_gain).astype(
        jnp.bfloat16
    )
    key_norm = norm_second(key_in.reshape(shape_four).astype(jnp.float32), key_gain).astype(
        jnp.bfloat16
    )
    scores = jnp.einsum(
        "jcip,jciq->jipq", query_norm, key_norm, preferred_element_type=jnp.float32
    ) / math.sqrt(head_dim)
    exp_scores = jnp.exp(scores)
    weights = (exp_scores / jnp.sum(exp_scores, axis=-1, keepdims=True)).astype(jnp.bfloat16)
    query_mean = jnp.sum(weights, axis=2, dtype=jnp.float32) / PATCHES
    pooled = jnp.einsum(
        "jiq,jciq->jic",
        query_mean,
        value_in.reshape(shape_four).astype(jnp.float32),
        precision=highest,
    )
    attended = pooled.astype(jnp.bfloat16)[None]
    returned = lax.all_to_all(attended, "inp", split_axis=3, concat_axis=0, tiled=True)
    returned = returned.reshape(n_masks, n_heads, images, n_comps)
    mixed_sum = jnp.einsum("mhic,chd->imd", returned, w_proj, preferred_element_type=jnp.float32)
    mixed_sum = mixed_sum + jnp.einsum(
        "mfi,fd->imd", pooled_hidden, w_down, preferred_element_type=jnp.float32
    )
    row_ids = lax.axis_index("inp") * local_rows + jnp.arange(local_rows, dtype=jnp.int32)
    row_owner = (row_ids // PATCHES)[None, :] == jnp.arange(images, dtype=jnp.int32)[:, None]
    input_sum = (
        jnp.dot(row_owner.astype(jnp.bfloat16), tokens, preferred_element_type=jnp.float32)
        / PATCHES
    )
    partial_feature = mixed_sum + input_sum[:, None, :]
    feature = lax.psum(partial_feature, "inp")
    normalized = norm_last(feature, final_gain)
    slice_width = model_width // n_parts
    embedding = lax.dynamic_slice_in_dim(
        normalized, lax.axis_index("inp") * slice_width, slice_width, 2
    )
    logit_part = jnp.einsum(
        "imd,dc->imc", embedding.astype(jnp.bfloat16), w_head, preferred_element_type=jnp.float32
    )
    raw_logits = lax.psum(logit_part, "inp")
    logits = soft_cap * jnp.tanh(raw_logits / soft_cap)
    return (embedding, bald_score(logits))


def solution(mesh):
    fits = mesh.shape["inp"] == PIPELINED_PARTS
    return jax.shard_map(
        pipelined if fits else local,
        mesh=mesh,
        in_specs=(
            P(("groups", "inp"), None),
            P(None, "groups", None),
            P(),
            P("inp", None, None, None),
            P("inp", None),
            P(),
            P(),
            P("inp", None, None),
            P("inp", None),
            P(),
            P("inp", None),
        ),
        out_specs=(P("groups", None, "inp"), P("groups")),
        check_vma=False,
    )
```

```python
import functools
import math

import jax
import jax.numpy as jnp
from jax import lax
from jax.experimental import pallas as pl
from jax.experimental.pallas import tpu as pltpu
from jax.sharding import PartitionSpec as P

PATCHES = 256


soft_cap = 20.0
PIPELINED_PARTS = 16
UNITS = 256
F32 = jnp.float32
BF16 = jnp.bfloat16
MIB = 1024 * 1024


def norm_last(values, gain):
    average = jnp.mean(values, axis=-1, keepdims=True)
    centered = values - average
    spread_sq = jnp.mean(centered * centered, axis=-1, keepdims=True)
    return centered * lax.rsqrt(spread_sq + 1e-06) * gain


def norm_second(values, gain):
    average = jnp.mean(values, axis=1, keepdims=True)
    centered = values - average
    spread_sq = jnp.mean(centered * centered, axis=1, keepdims=True)
    return centered * lax.rsqrt(spread_sq + 1e-06) * gain[None, :, None, None]


def bald_score(logits):
    exp_logits = jnp.exp(logits)
    totals = jnp.sum(exp_logits, axis=-1, keepdims=True)
    sample_probs = exp_logits / totals
    entropy = jnp.log(totals[..., 0]) - jnp.sum(sample_probs * logits, axis=-1)
    mean_probs = jnp.mean(sample_probs, axis=1)
    joint = -jnp.sum(mean_probs * jnp.log(mean_probs), axis=-1)
    return joint - jnp.mean(entropy, axis=1)


def permuted(array, bits):
    count = lax.axis_size("inp")
    return lax.ppermute(array, "inp", [(i, i ^ bits) for i in range(count)])


def own_norm_kernel(x_ref, gain_ref, first_ref, second_ref):
    y = norm_last(x_ref[...].astype(F32), gain_ref[...]).astype(BF16)
    cut = first_ref.shape[1]
    first_ref[...] = y[:, :cut]
    second_ref[...] = y[:, cut:]


def own_norm(tokens, gain):
    rows, width = tokens.shape
    cut = width // 3 * 2
    return pl.pallas_call(
        own_norm_kernel,
        out_shape=(
            jax.ShapeDtypeStruct((rows, cut), BF16),
            jax.ShapeDtypeStruct((rows, width - cut), BF16),
        ),
        compiler_params=pltpu.CompilerParams(vmem_limit_bytes=60 * MIB),
        name="own_norm",
    )(tokens, gain.reshape(1, width))


def gathered_pieces(first, second, beside):
    along_z = jnp.stack([first] + [permuted(first, 4 * k) for k in range(1, 4)])
    pair = jnp.stack([second, permuted(second, 2)])
    along_z, pair, beside = lax.optimization_barrier((along_z, pair, beside))
    across_y = permuted(along_z, 2)
    moved = [permuted(pair, 4 * k) for k in range(1, 4)]
    across_y, *moved = lax.optimization_barrier((across_y, *moved))
    pieces = [
        (0, [4 * k for k in range(4)], along_z),
        (0, [4 * k + 2 for k in range(4)], across_y),
    ]
    for k, array in enumerate([pair, *moved]):
        pieces.append((first.shape[1], [4 * k, 4 * k + 2], array))
    pieces = pieces + [
        (side, [b ^ 1 for b in bits], permuted(array, 1)) for side, bits, array in pieces
    ]
    return pieces, beside


def place_kernel(layout, me_ref, *refs):
    sources, out_ref = refs[:-1], refs[-1]
    me = me_ref[0]
    for (side, bits), source in zip(layout, sources, strict=True):
        _, rows, columns = source.shape
        for at, bit in enumerate(bits):
            start = pl.multiple_of((me ^ bit) * rows, rows)
            out_ref[pl.ds(start, rows), side : side + columns] = source[at]


def placed(pieces, me):
    rows = pieces[0][2].shape[1]
    total = rows * sum(len(bits) for side, bits, _ in pieces if side == 0)
    width = sum(array.size for _, _, array in pieces) // total
    layout = [(side, bits) for side, bits, _ in pieces]
    return pl.pallas_call(
        functools.partial(place_kernel, layout),
        out_shape=jax.ShapeDtypeStruct((total, width), BF16),
        in_specs=[pl.BlockSpec(memory_space=pltpu.SMEM)]
        + [pl.BlockSpec(memory_space=pltpu.VMEM)] * len(pieces),
        out_specs=pl.BlockSpec(memory_space=pltpu.VMEM),
        compiler_params=pltpu.CompilerParams(vmem_limit_bytes=50 * MIB),
        name="place_rows",
    )(me.reshape(1), *[array for _, _, array in pieces])


ACROSS = (((1,), (1,)), ((), ()))
TILE = 16
BLOCK = 128


def choosers(dropout_masks):
    samples, rows, blocks = dropout_masks.shape
    tiles = rows // TILE
    kept = dropout_masks.astype(BF16).reshape(samples, tiles, TILE, blocks)
    kept = jnp.transpose(kept, (1, 0, 2, 3)).reshape(tiles, samples * TILE, blocks)
    column = jnp.arange(blocks * TILE)
    spread = (column[None] // TILE == jnp.arange(blocks)[:, None]).astype(BF16)
    own = jnp.arange(samples * TILE)[:, None] % TILE == column[None] % TILE
    wide = jnp.einsum("trb,bc->trc", kept, spread, preferred_element_type=F32)
    return jnp.where(own[None], 2.0 * wide, 0.0).astype(BF16)


def block_products(norm_ref, weight, products, first):
    for j in range(weight.shape[1] // BLOCK):
        at = slice(j * BLOCK, (j + 1) * BLOCK)
        products[first + j] = lax.dot_general(
            norm_ref[:, at], weight[:, at], ACROSS, preferred_element_type=F32
        ).astype(BF16)


def summed(choose_ref, products, tile):
    blocks, _, columns = products.shape
    part = products[:, tile * TILE : (tile + 1) * TILE, :].reshape(blocks * TILE, columns)
    return jnp.dot(choose_ref[tile], part, preferred_element_type=F32)


def query_key_kernel(norm_ref, choose_ref, w_ref, out_ref, products, sums, turned):
    step = pl.program_id(0)
    rows, depth = norm_ref.shape
    comps, kinds, heads, _ = w_ref.shape
    columns = comps * kinds * heads
    block_products(
        norm_ref, w_ref[...].reshape(columns, depth), products, step * (depth // BLOCK)
    )

    @pl.when(step == pl.num_programs(0) - 1)
    def _():
        samples = sums.shape[0]
        for tile in range(rows // TILE):
            sums[:, tile * TILE : (tile + 1) * TILE, :] = summed(
                choose_ref, products, tile
            ).reshape(samples, TILE, columns)
        for m in range(samples):
            for part in range(rows // 128):
                at = slice(part * 128, (part + 1) * 128)
                turned[m * (rows // 128) + part] = sums[m, at, :].T
            for part in range(rows // 128):
                at = slice(part * 128, (part + 1) * 128)
                held = turned.at[m * (rows // 128) + part]
                for h in range(heads):
                    both = [
                        held[pl.ds(t * heads + h, comps, stride=kinds * heads), :]
                        for t in range(kinds)
                    ]
                    out_ref[h, m, :, at] = jnp.concatenate(both, axis=0).astype(BF16)


def query_key(norm, choose, w_qkv, chunk, heads):
    rows, width = norm.shape
    samples = choose.shape[1] // TILE
    comps = w_qkv.shape[0]
    depth = width // 2
    columns = 2 * comps * heads
    shape = (heads, samples, 2 * comps, rows)
    return pl.pallas_call(
        query_key_kernel,
        grid=(width // depth,),
        out_shape=jax.ShapeDtypeStruct(shape, BF16),
        in_specs=[
            pl.BlockSpec((rows, depth), lambda k: (0, k)),
            pl.BlockSpec(choose.shape, lambda k: (0, 0, 0)),
            pl.BlockSpec((comps, 2, heads, depth), lambda k: (0, 0, chunk, k)),
        ],
        out_specs=pl.BlockSpec(shape, lambda k: (0, 0, 0, 0)),
        scratch_shapes=[
            pltpu.VMEM((width // BLOCK, rows, columns), BF16),
            pltpu.VMEM((samples, rows, columns), F32),
            pltpu.VMEM((samples * rows // 128, columns, 128), F32),
        ],
        compiler_params=pltpu.CompilerParams(vmem_limit_bytes=50 * MIB),
        cost_estimate=pl.CostEstimate(
            flops=8 * rows * width * columns,
            bytes_accessed=2 * (norm.size + choose.size + columns * width),
            transcendentals=0,
        ),
        name="query_key",
    )(norm, choose, w_qkv)


def value_kernel(norm_ref, choose_ref, w_ref, out_ref, products):
    step = pl.program_id(0)
    rows, depth = norm_ref.shape
    comps, _, heads, _ = w_ref.shape
    block_products(
        norm_ref, w_ref[:, 0].reshape(comps * heads, depth), products, step * (depth // BLOCK)
    )

    @pl.when(step == pl.num_programs(0) - 1)
    def _():
        samples = out_ref.shape[0]
        for tile in range(rows // TILE):
            out_ref[:, tile * TILE : (tile + 1) * TILE, :] = (
                summed(choose_ref, products, tile)
                .reshape(samples, TILE, comps * heads)
                .astype(BF16)
            )


def values_of(norm, choose, w_qkv):
    rows, width = norm.shape
    samples = choose.shape[1] // TILE
    comps, _, heads, _ = w_qkv.shape
    depth = width // 2
    columns = comps * heads
    return pl.pallas_call(
        value_kernel,
        grid=(width // depth,),
        out_shape=jax.ShapeDtypeStruct((samples, rows, columns), BF16),
        in_specs=[
            pl.BlockSpec((rows, depth), lambda k: (0, k)),
            pl.BlockSpec(choose.shape, lambda k: (0, 0, 0)),
            pl.BlockSpec((comps, 1, heads, depth), lambda k: (0, 2, 0, k)),
        ],
        out_specs=pl.BlockSpec((samples, rows, columns), lambda k: (0, 0, 0)),
        scratch_shapes=[pltpu.VMEM((width // BLOCK, rows, columns), BF16)],
        compiler_params=pltpu.CompilerParams(vmem_limit_bytes=50 * MIB),
        cost_estimate=pl.CostEstimate(
            flops=8 * rows * width * columns,
            bytes_accessed=2 * (norm.size + choose.size + columns * width),
            transcendentals=0,
        ),
        name="value_rows",
    )(norm, choose, w_qkv)


def erf(x):
    x = jnp.clip(x, -4.0, 4.0)
    s = x * x
    top = s * -2.72614225801306e-10 + 2.77068142495902e-08
    for c in (
        -2.10102402082508e-06,
        -5.69250639462346e-05,
        -7.34990630326855e-04,
        -2.95459980854025e-03,
        -1.60960333262415e-02,
    ):
        top = top * s + c
    low = s * -1.45660718464996e-05 + -2.13374055278905e-04
    for c in (-1.68282697438203e-03, -7.37332916720468e-03, -1.42647390514189e-02):
        low = low * s + c
    return x * top / low


def hidden_kernel(norm_ref, choose_ref, up_ref, out_ref, products):
    step = pl.program_id(1)
    rows, depth = norm_ref.shape
    samples, units = out_ref.shape
    block_products(norm_ref, up_ref, products, step * (depth // BLOCK))

    @pl.when(step == pl.num_programs(1) - 1)
    def _():
        total = jnp.zeros((samples, units), F32)
        for tile in range(rows // TILE):
            v = summed(choose_ref, products, tile)
            active = (0.5 * v) * (1.0 + erf(v * math.sqrt(0.5)))
            total = total + jnp.sum(active.reshape(samples, TILE, units), axis=1)
        out_ref[...] = total * (1.0 / rows)


def hidden_part(norm, choose, w_up, first, tiles):
    rows, width = norm.shape
    samples = choose.shape[1] // TILE
    depth = width // 2
    return pl.pallas_call(
        hidden_kernel,
        grid=(tiles, width // depth),
        out_shape=jax.ShapeDtypeStruct((samples, tiles * UNITS), F32),
        in_specs=[
            pl.BlockSpec((rows, depth), lambda i, k: (0, k)),
            pl.BlockSpec(choose.shape, lambda i, k: (0, 0, 0)),
            pl.BlockSpec((UNITS, depth), lambda i, k: (first + i, k)),
        ],
        out_specs=pl.BlockSpec((samples, UNITS), lambda i, k: (0, i)),
        scratch_shapes=[pltpu.VMEM((width // BLOCK, rows, UNITS), BF16)],
        compiler_params=pltpu.CompilerParams(vmem_limit_bytes=50 * MIB),
        cost_estimate=pl.CostEstimate(
            flops=8 * rows * width * UNITS * tiles,
            bytes_accessed=2 * (norm.size + choose.size + UNITS * tiles * width),
            transcendentals=samples * rows * UNITS * tiles,
        ),
        name="hidden_part",
    )(norm, choose, w_up)


def down_kernel(pooled_ref, down_ref, out_ref):
    samples = pooled_ref.shape[0]
    mean = pooled_ref[...]
    mean = jnp.concatenate([mean, jnp.zeros_like(mean)], axis=0).astype(BF16)
    part = jnp.dot(mean, down_ref[...], preferred_element_type=F32)[:samples]

    @pl.when(pl.program_id(0) == 0)
    def _():
        out_ref[...] = part

    @pl.when(pl.program_id(0) > 0)
    def _():
        out_ref[...] += part


def down_part(pooled, w_down, first):
    samples, units = pooled.shape
    width = w_down.shape[1]
    return pl.pallas_call(
        down_kernel,
        grid=(units // UNITS,),
        out_shape=jax.ShapeDtypeStruct((samples, width), F32),
        in_specs=[
            pl.BlockSpec((samples, UNITS), lambda i: (0, i)),
            pl.BlockSpec((UNITS, width), lambda i: (first + i, 0)),
        ],
        out_specs=pl.BlockSpec((samples, width), lambda i: (0, 0)),
        compiler_params=pltpu.CompilerParams(vmem_limit_bytes=50 * MIB),
        cost_estimate=pl.CostEstimate(
            flops=32 * units * width, bytes_accessed=2 * units * width, transcendentals=0
        ),
        name="down_part",
    )(pooled, w_down)


def attention_kernel(items, x_ref, query_gain_ref, key_gain_ref, *refs):
    *before, out_ref, held = refs
    parts, _, both, rows = x_ref.shape
    comps = both // 2
    head_dim = parts * comps
    ones = jnp.ones((16, rows), BF16)
    first = held.shape[0] - items

    def normed(values, gain_ref):
        values = values.reshape(head_dim, rows)
        average = jnp.mean(values, axis=0, keepdims=True)
        centered = values - average
        spread_sq = jnp.mean(centered * centered, axis=0, keepdims=True)
        return (centered * lax.rsqrt(spread_sq + 1e-06) * gain_ref[...]).astype(BF16)

    if before:
        held[:first] = before[0][...]
    for j in range(items):
        x = x_ref[:, j].astype(F32)
        query = normed(x[:, :comps], query_gain_ref)
        key = normed(x[:, comps:], key_gain_ref)
        scores = lax.dot_general(
            key, query, (((0,), (0,)), ((), ())), preferred_element_type=F32
        )
        e = jnp.exp2(scores * (math.log2(math.e) / math.sqrt(head_dim)))
        weights = (e * (1.0 / jnp.sum(e, axis=0, keepdims=True))).astype(BF16)
        mean = lax.dot_general(ones, weights, ACROSS, preferred_element_type=F32)[:1]
        held[first + j : first + j + 1, :] = mean * (1.0 / rows)
    if before:
        for part in range(parts):
            out_ref[part] = held[...].astype(BF16)
    else:
        out_ref[...] = held[...]


def key_weights(exchanged, query_gain, key_gain, *before):
    parts, items, both, rows = exchanged.shape
    head_dim = parts * both // 2
    count = items + sum(x.shape[0] for x in before)
    shape = jax.ShapeDtypeStruct((items, rows), F32)
    if before:
        shape = jax.ShapeDtypeStruct((parts, count, rows), BF16)
    return pl.pallas_call(
        functools.partial(attention_kernel, items),
        out_shape=shape,
        scratch_shapes=[pltpu.VMEM((count, rows), F32)],
        compiler_params=pltpu.CompilerParams(vmem_limit_bytes=50 * MIB),
        cost_estimate=pl.CostEstimate(
            flops=2 * items * rows * rows * head_dim,
            bytes_accessed=2 * exchanged.size,
            transcendentals=items * rows * rows,
        ),
        name="key_weights",
    )(exchanged, query_gain.reshape(head_dim, 1), key_gain.reshape(head_dim, 1), *before)


def feature_kernel(key_ref, value_ref, proj_ref, hidden_ref, token_ref, out_ref, attended):
    step = pl.program_id(0)
    parts, pieces, _ = key_ref.shape
    samples, rows, columns = value_ref.shape
    chunks = pieces // samples
    heads = parts * chunks

    @pl.when(step == 0)
    def _():
        row = lax.broadcasted_iota(jnp.int32, (heads, columns), 0)
        column = lax.broadcasted_iota(jnp.int32, (heads, columns), 1)
        source, piece = lax.rem(row, parts), row // parts
        head = jnp.where(
            piece == 0, heads - parts + source, source * (chunks - 1) + piece - 1
        )
        own = lax.rem(column, heads) == head
        results = []
        for m in range(samples):
            key = jnp.concatenate(
                [
                    key_ref[:, c * samples + m, :].astype(F32)
                    for c in range(chunks)
                ], axis=0
            )
            product = jnp.dot(key.astype(BF16), value_ref[m], preferred_element_type=F32)
            results.append(jnp.sum(jnp.where(own, product, 0.0), axis=0, keepdims=True))
        results.append(jnp.zeros((16 - samples, columns), F32))
        attended[...] = jnp.concatenate(results, axis=0).astype(BF16)

    part = jnp.dot(attended[...], proj_ref[...], preferred_element_type=F32)[:samples]
    part = part + hidden_ref[...]
    part = part + jnp.sum(token_ref[...].astype(F32), axis=0, keepdims=True) * (1.0 / rows)
    width = out_ref.shape[2]
    for j in range(out_ref.shape[0]):
        out_ref[j] = part[:, j * width : (j + 1) * width]


def feature_part(key_mean, value, w_proj, hidden, tokens, steps):
    parts = key_mean.shape[0]
    samples, rows, columns = value.shape
    own_rows, width = tokens.shape
    cut = width // steps
    return pl.pallas_call(
        feature_kernel,
        grid=(steps,),
        out_shape=jax.ShapeDtypeStruct((parts, samples, width // parts), F32),
        in_specs=[
            pl.BlockSpec(key_mean.shape, lambda i: (0, 0, 0)),
            pl.BlockSpec(value.shape, lambda i: (0, 0, 0)),
            pl.BlockSpec((columns, cut), lambda i: (0, i)),
            pl.BlockSpec((samples, cut), lambda i: (0, i)),
            pl.BlockSpec((own_rows, cut), lambda i: (0, i)),
        ],
        out_specs=pl.BlockSpec((parts // steps, samples, width // parts), lambda i: (i, 0, 0)),
        scratch_shapes=[pltpu.VMEM((16, columns), BF16)],
        compiler_params=pltpu.CompilerParams(vmem_limit_bytes=40 * MIB),
        cost_estimate=pl.CostEstimate(
            flops=2 * samples * rows * columns * 2 + 32 * columns * width,
            bytes_accessed=2 * columns * width + 2 * value.size,
            transcendentals=0,
        ),
        name="feature_part",
    )(key_mean, value, w_proj, hidden, tokens)


def joined(mine, other, columns):
    classes = mine.shape[1] - 2
    samples = mine.shape[0] - 1
    mean, other_mean = (x[:samples, classes : classes + 1] for x in (mine, other))
    joint = 0.5 * (mean + other_mean)
    logits = (
        mine[:samples, :classes]
        + other[:samples, :classes]
        + (mean - joint) * mine[samples:, :classes]
        + (other_mean - joint) * other[samples:, :classes]
    )
    gap = mean - other_mean
    spread = mine[:samples, classes + 1 :] + other[:samples, classes + 1 :]
    spread = spread + gap * gap * (0.5 * columns)
    return logits, joint, spread, mine[samples:, :classes] + other[samples:, :classes]


def packed(logits, mean, spread, gain_head):
    rows = jnp.concatenate([logits, mean, spread], axis=1)
    return jnp.concatenate([rows, jnp.pad(gain_head, ((0, 0), (0, 2)))], axis=0)


def finish_kernel(columns, mine_ref, other_ref, feature_ref, gain_ref, out_ref, bald_ref):
    logits, mean, spread, _ = joined(mine_ref[...], other_ref[...], columns)
    scale = lax.rsqrt(spread / (2 * columns) + 1e-06)
    out_ref[...] = (feature_ref[...] - mean) * scale * gain_ref[...]
    logits = soft_cap * jnp.tanh(logits * scale / soft_cap)
    samples = logits.shape[0]
    exp_logits = jnp.exp(logits)
    totals = jnp.sum(exp_logits, axis=1, keepdims=True)
    probs = exp_logits / totals
    entropy = jnp.log(totals) - jnp.sum(probs * logits, axis=1, keepdims=True)
    mean_probs = jnp.sum(probs, axis=0, keepdims=True) * (1.0 / samples)
    whole = -jnp.sum(mean_probs * jnp.log(mean_probs), axis=1, keepdims=True)
    bald_ref[...] = whole - jnp.sum(entropy, axis=0, keepdims=True) * (1.0 / samples)


def finished(feature, final_gain, w_head):
    highest = lax.Precision.HIGHEST
    gain_head = jnp.dot(final_gain[None], w_head.astype(F32), precision=highest)
    mean = jnp.mean(feature, axis=-1, keepdims=True)
    centered = feature - mean
    spread = jnp.sum(centered * centered, axis=-1, keepdims=True)
    logits = jnp.dot(centered * final_gain, w_head.astype(F32), precision=highest)
    columns = feature.shape[1]
    mine = packed(logits, mean, spread, gain_head)
    bits = 1
    while 2 * bits < lax.axis_size("inp"):
        mine = packed(*joined(mine, permuted(mine, bits), columns))
        columns = 2 * columns
        bits = 2 * bits
    embedding, score = pl.pallas_call(
        functools.partial(finish_kernel, columns),
        out_shape=(
            jax.ShapeDtypeStruct(feature.shape, F32),
            jax.ShapeDtypeStruct((1, 1), F32),
        ),
        compiler_params=pltpu.CompilerParams(vmem_limit_bytes=16 * MIB),
        name="finish",
    )(mine, permuted(mine, bits), feature, final_gain[None])
    return embedding[None], score.reshape(1)


def pipelined(
    tokens,
    dropout_masks,
    input_gain,
    w_qkv,
    w_up,
    query_gain,
    key_gain,
    w_proj,
    w_down,
    final_gain,
    w_head,
):
    n_parts = lax.axis_size("inp")
    me = lax.axis_index("inp")
    model_width = tokens.shape[1]
    n_comps, _, n_heads, _ = w_qkv.shape
    choose = choosers(dropout_masks)
    pieces, choose = gathered_pieces(*own_norm(tokens, input_gain), choose)
    norm = placed(pieces, me)
    together = lax.optimization_barrier

    def exchange(array):
        heads, samples, both, rows = array.shape
        array = array.reshape(n_parts, heads // n_parts * samples, both, rows)
        return lax.all_to_all(array, "inp", split_axis=0, concat_axis=0, tiled=True)

    ahead = n_parts
    behind = n_heads - ahead
    first = query_key(norm, choose, w_qkv, behind // ahead, ahead)
    second = query_key(norm, choose, w_qkv, 0, behind)
    value = values_of(norm, choose, w_qkv)
    first = exchange(first)
    second, value = together((second, value))
    second = exchange(second)
    norm, first = together((norm, first))
    tiles = w_up.shape[0] // UNITS // 2
    pooled = hidden_part(norm, choose, w_up, 0, tiles)
    more_pooled = hidden_part(norm, choose, w_up, tiles, tiles)
    hidden = down_part(pooled, w_down, 0)
    key_mean = key_weights(first, query_gain, key_gain)
    hidden, more_pooled, key_mean, second = together((hidden, more_pooled, key_mean, second))
    key_mean = key_weights(second, query_gain, key_gain, key_mean)
    more_pooled, key_mean = together((more_pooled, key_mean))
    hidden = hidden + down_part(more_pooled, w_down, tiles)
    key_mean = lax.all_to_all(key_mean, "inp", split_axis=0, concat_axis=0, tiled=True)
    partial_feature = feature_part(
        key_mean, value, w_proj.reshape(n_comps * n_heads, model_width), hidden, tokens, 4
    )
    slice_width = model_width // n_parts
    feature = jnp.sum(
        lax.all_to_all(partial_feature, "inp", split_axis=0, concat_axis=0, tiled=True), axis=0
    )
    gain = lax.dynamic_slice_in_dim(final_gain, me * slice_width, slice_width, 0)
    return finished(feature, gain, w_head)


def local(
    tokens,
    dropout_masks,
    input_gain,
    w_qkv,
    w_up,
    query_gain,
    key_gain,
    w_proj,
    w_down,
    final_gain,
    w_head,
):
    n_parts = lax.axis_size("inp")
    local_rows, model_width = tokens.shape
    n_masks, all_rows, n_blocks = dropout_masks.shape
    block_width = model_width // n_blocks
    n_comps, three_kinds, n_heads, ignored_width = w_qkv.shape
    n_units = w_up.shape[0]
    head_dim = n_comps * n_parts
    images = all_rows // PATCHES
    qkv_cols = three_kinds * n_heads * n_comps
    items_dev = n_masks * n_heads // n_parts
    highest = lax.Precision.HIGHEST
    joined_weight = jnp.concatenate(
        [jnp.transpose(w_qkv, (1, 2, 0, 3)).reshape(qkv_cols, model_width), w_up], axis=0
    )
    row_piece = lax.all_gather(tokens, "inp", axis=0, tiled=True)
    row_count = row_piece.shape[0]
    normed = norm_last(row_piece.astype(jnp.float32), input_gain).astype(jnp.bfloat16)
    masked = (
        normed.reshape(1, row_count, n_blocks, block_width)
        * dropout_masks.astype(jnp.bfloat16)[..., None]
    )
    masked = masked.reshape(n_masks, row_count, model_width)
    result = jnp.einsum("mkd,cd->mck", masked, joined_weight, preferred_element_type=jnp.float32)
    projected = 2.0 * result
    qkv_half = (
        projected[:, :qkv_cols]
        .astype(jnp.bfloat16)
        .reshape(n_masks, three_kinds, n_heads * n_comps, all_rows)
    )
    item_shape = (n_parts, items_dev, n_comps, all_rows)
    query_send = qkv_half[:, 0].reshape(item_shape)
    key_send = qkv_half[:, 1].reshape(item_shape)
    value_send = qkv_half[:, 2].reshape(item_shape)
    activated = jax.nn.gelu(projected[:, qkv_cols:], approximate=False)
    pooled_hidden = jnp.mean(activated.reshape(n_masks, n_units, images, PATCHES), axis=-1).astype(
        jnp.bfloat16
    )
    query_in = lax.all_to_all(query_send, "inp", split_axis=0, concat_axis=2, tiled=True)
    key_in = lax.all_to_all(key_send, "inp", split_axis=0, concat_axis=2, tiled=True)
    value_in = lax.all_to_all(value_send, "inp", split_axis=0, concat_axis=2, tiled=True)
    n_items = query_in.shape[1]
    shape_four = (n_items, head_dim, images, PATCHES)
    query_norm = norm_second(query_in.reshape(shape_four).astype(jnp.float32), query_gain).astype(
        jnp.bfloat16
    )
    key_norm = norm_second(key_in.reshape(shape_four).astype(jnp.float32), key_gain).astype(
        jnp.bfloat16
    )
    scores = jnp.einsum(
        "jcip,jciq->jipq", query_norm, key_norm, preferred_element_type=jnp.float32
    ) / math.sqrt(head_dim)
    exp_scores = jnp.exp(scores)
    weights = (exp_scores / jnp.sum(exp_scores, axis=-1, keepdims=True)).astype(jnp.bfloat16)
    query_mean = jnp.sum(weights, axis=2, dtype=jnp.float32) / PATCHES
    pooled = jnp.einsum(
        "jiq,jciq->jic",
        query_mean,
        value_in.reshape(shape_four).astype(jnp.float32),
        precision=highest,
    )
    attended = pooled.astype(jnp.bfloat16)[None]
    returned = lax.all_to_all(attended, "inp", split_axis=3, concat_axis=0, tiled=True)
    returned = returned.reshape(n_masks, n_heads, images, n_comps)
    mixed_sum = jnp.einsum("mhic,chd->imd", returned, w_proj, preferred_element_type=jnp.float32)
    mixed_sum = mixed_sum + jnp.einsum(
        "mfi,fd->imd", pooled_hidden, w_down, preferred_element_type=jnp.float32
    )
    row_ids = lax.axis_index("inp") * local_rows + jnp.arange(local_rows, dtype=jnp.int32)
    row_owner = (row_ids // PATCHES)[None, :] == jnp.arange(images, dtype=jnp.int32)[:, None]
    input_sum = (
        jnp.dot(row_owner.astype(jnp.bfloat16), tokens, preferred_element_type=jnp.float32)
        / PATCHES
    )
    partial_feature = mixed_sum + input_sum[:, None, :]
    feature = lax.psum(partial_feature, "inp")
    normalized = norm_last(feature, final_gain)
    slice_width = model_width // n_parts
    embedding = lax.dynamic_slice_in_dim(
        normalized, lax.axis_index("inp") * slice_width, slice_width, 2
    )
    logit_part = jnp.einsum(
        "imd,dc->imc", embedding.astype(jnp.bfloat16), w_head, preferred_element_type=jnp.float32
    )
    raw_logits = lax.psum(logit_part, "inp")
    logits = soft_cap * jnp.tanh(raw_logits / soft_cap)
    return (embedding, bald_score(logits))


def solution(mesh):
    fits = mesh.shape["inp"] == PIPELINED_PARTS
    return jax.shard_map(
        pipelined if fits else local,
        mesh=mesh,
        in_specs=(
            P(("groups", "inp"), None),
            P(None, "groups", None),
            P(),
            P("inp", None, None, None),
            P("inp", None),
            P(),
            P(),
            P("inp", None, None),
            P("inp", None),
            P(),
            P("inp", None),
        ),
        out_specs=(P("groups", None, "inp"), P("groups")),
        check_vma=False,
    )
```

```python
import functools
import math

import jax
import jax.numpy as jnp
from jax import lax
from jax.experimental import pallas as pl
from jax.experimental.pallas import tpu as pltpu
from jax.sharding import PartitionSpec as P

PATCHES = 256


soft_cap = 20.0
PIPELINED_PARTS = 16
UNITS = 256
F32 = jnp.float32
BF16 = jnp.bfloat16
MIB = 1024 * 1024


def norm_last(values, gain):
    average = jnp.mean(values, axis=-1, keepdims=True)
    centered = values - average
    spread_sq = jnp.mean(centered * centered, axis=-1, keepdims=True)
    return centered * lax.rsqrt(spread_sq + 1e-06) * gain


def norm_second(values, gain):
    average = jnp.mean(values, axis=1, keepdims=True)
    centered = values - average
    spread_sq = jnp.mean(centered * centered, axis=1, keepdims=True)
    return centered * lax.rsqrt(spread_sq + 1e-06) * gain[None, :, None, None]


def bald_score(logits):
    exp_logits = jnp.exp(logits)
    totals = jnp.sum(exp_logits, axis=-1, keepdims=True)
    sample_probs = exp_logits / totals
    entropy = jnp.log(totals[..., 0]) - jnp.sum(sample_probs * logits, axis=-1)
    mean_probs = jnp.mean(sample_probs, axis=1)
    joint = -jnp.sum(mean_probs * jnp.log(mean_probs), axis=-1)
    return joint - jnp.mean(entropy, axis=1)


def permuted(array, bits):
    count = lax.axis_size("inp")
    return lax.ppermute(array, "inp", [(i, i ^ bits) for i in range(count)])


def own_norm_kernel(x_ref, gain_ref, first_ref, second_ref):
    y = norm_last(x_ref[...].astype(F32), gain_ref[...]).astype(BF16)
    cut = first_ref.shape[1]
    first_ref[...] = y[:, :cut]
    second_ref[...] = y[:, cut:]


def own_norm(tokens, gain):
    rows, width = tokens.shape
    cut = width // 3 * 2
    return pl.pallas_call(
        own_norm_kernel,
        out_shape=(
            jax.ShapeDtypeStruct((rows, cut), BF16),
            jax.ShapeDtypeStruct((rows, width - cut), BF16),
        ),
        compiler_params=pltpu.CompilerParams(vmem_limit_bytes=60 * MIB),
        name="own_norm",
    )(tokens, gain.reshape(1, width))


def gathered_pieces(first, second, beside):
    along_z = jnp.stack([first] + [permuted(first, 4 * k) for k in range(1, 4)])
    pair = jnp.stack([second, permuted(second, 2)])
    along_z, pair, beside = lax.optimization_barrier((along_z, pair, beside))
    across_y = permuted(along_z, 2)
    moved = [permuted(pair, 4 * k) for k in range(1, 4)]
    across_y, *moved = lax.optimization_barrier((across_y, *moved))
    pieces = [
        (0, [4 * k for k in range(4)], along_z),
        (0, [4 * k + 2 for k in range(4)], across_y),
    ]
    for k, array in enumerate([pair, *moved]):
        pieces.append((first.shape[1], [4 * k, 4 * k + 2], array))
    pieces = pieces + [
        (side, [b ^ 1 for b in bits], permuted(array, 1)) for side, bits, array in pieces
    ]
    return pieces, beside


def place_kernel(layout, me_ref, *refs):
    sources, out_ref = refs[:-1], refs[-1]
    me = me_ref[0]
    for (side, bits), source in zip(layout, sources, strict=True):
        _, rows, columns = source.shape
        for at, bit in enumerate(bits):
            start = pl.multiple_of((me ^ bit) * rows, rows)
            out_ref[pl.ds(start, rows), side : side + columns] = source[at]


def placed(pieces, me):
    rows = pieces[0][2].shape[1]
    total = rows * sum(len(bits) for side, bits, _ in pieces if side == 0)
    width = sum(array.size for _, _, array in pieces) // total
    layout = [(side, bits) for side, bits, _ in pieces]
    return pl.pallas_call(
        functools.partial(place_kernel, layout),
        out_shape=jax.ShapeDtypeStruct((total, width), BF16),
        in_specs=[pl.BlockSpec(memory_space=pltpu.SMEM)]
        + [pl.BlockSpec(memory_space=pltpu.VMEM)] * len(pieces),
        out_specs=pl.BlockSpec(memory_space=pltpu.VMEM),
        compiler_params=pltpu.CompilerParams(vmem_limit_bytes=50 * MIB),
        name="place_rows",
    )(me.reshape(1), *[array for _, _, array in pieces])


ACROSS = (((1,), (1,)), ((), ()))
TILE = 16
BLOCK = 128


def choosers(dropout_masks):
    samples, rows, blocks = dropout_masks.shape
    tiles = rows // TILE
    kept = dropout_masks.astype(BF16).reshape(samples, tiles, TILE, blocks)
    kept = jnp.transpose(kept, (1, 0, 2, 3)).reshape(tiles, samples * TILE, blocks)
    column = jnp.arange(blocks * TILE)
    spread = (column[None] // TILE == jnp.arange(blocks)[:, None]).astype(BF16)
    own = jnp.arange(samples * TILE)[:, None] % TILE == column[None] % TILE
    wide = jnp.einsum("trb,bc->trc", kept, spread, preferred_element_type=F32)
    return jnp.where(own[None], 2.0 * wide, 0.0).astype(BF16)


def block_products(norm_ref, weight, products, first):
    for j in range(weight.shape[1] // BLOCK):
        at = slice(j * BLOCK, (j + 1) * BLOCK)
        products[first + j] = lax.dot_general(
            norm_ref[:, at], weight[:, at], ACROSS, preferred_element_type=F32
        ).astype(BF16)


def summed(choose_ref, products, tile):
    blocks, _, columns = products.shape
    part = products[:, tile * TILE : (tile + 1) * TILE, :].reshape(blocks * TILE, columns)
    return jnp.dot(choose_ref[tile], part, preferred_element_type=F32)


def query_key_kernel(norm_ref, choose_ref, w_ref, out_ref, products, sums, turned):
    step = pl.program_id(0)
    rows, depth = norm_ref.shape
    comps, kinds, heads, _ = w_ref.shape
    columns = comps * kinds * heads
    block_products(
        norm_ref, w_ref[...].reshape(columns, depth), products, step * (depth // BLOCK)
    )

    @pl.when(step == pl.num_programs(0) - 1)
    def _():
        samples = sums.shape[0]
        for tile in range(rows // TILE):
            sums[:, tile * TILE : (tile + 1) * TILE, :] = summed(
                choose_ref, products, tile
            ).reshape(samples, TILE, columns)
        for m in range(samples):
            for part in range(rows // 128):
                at = slice(part * 128, (part + 1) * 128)
                turned[m * (rows // 128) + part] = sums[m, at, :].T
            for part in range(rows // 128):
                at = slice(part * 128, (part + 1) * 128)
                held = turned.at[m * (rows // 128) + part]
                for h in range(heads):
                    both = [
                        held[pl.ds(t * heads + h, comps, stride=kinds * heads), :]
                        for t in range(kinds)
                    ]
                    out_ref[h, m, :, at] = jnp.concatenate(both, axis=0).astype(BF16)


def query_key(norm, choose, w_qkv, chunk, heads):
    rows, width = norm.shape
    samples = choose.shape[1] // TILE
    comps = w_qkv.shape[0]
    depth = width // 2
    columns = 2 * comps * heads
    shape = (heads, samples, 2 * comps, rows)
    return pl.pallas_call(
        query_key_kernel,
        grid=(width // depth,),
        out_shape=jax.ShapeDtypeStruct(shape, BF16),
        in_specs=[
            pl.BlockSpec((rows, depth), lambda k: (0, k)),
            pl.BlockSpec(choose.shape, lambda k: (0, 0, 0)),
            pl.BlockSpec((comps, 2, heads, depth), lambda k: (0, 0, chunk, k)),
        ],
        out_specs=pl.BlockSpec(shape, lambda k: (0, 0, 0, 0)),
        scratch_shapes=[
            pltpu.VMEM((width // BLOCK, rows, columns), BF16),
            pltpu.VMEM((samples, rows, columns), F32),
            pltpu.VMEM((samples * rows // 128, columns, 128), F32),
        ],
        compiler_params=pltpu.CompilerParams(vmem_limit_bytes=50 * MIB),
        cost_estimate=pl.CostEstimate(
            flops=8 * rows * width * columns,
            bytes_accessed=2 * (norm.size + choose.size + columns * width),
            transcendentals=0,
        ),
        name="query_key",
    )(norm, choose, w_qkv)


def value_kernel(norm_ref, choose_ref, w_ref, out_ref, products):
    step = pl.program_id(0)
    rows, depth = norm_ref.shape
    comps, _, heads, _ = w_ref.shape
    block_products(
        norm_ref, w_ref[:, 0].reshape(comps * heads, depth), products, step * (depth // BLOCK)
    )

    @pl.when(step == pl.num_programs(0) - 1)
    def _():
        samples = out_ref.shape[0]
        for tile in range(rows // TILE):
            out_ref[:, tile * TILE : (tile + 1) * TILE, :] = (
                summed(choose_ref, products, tile)
                .reshape(samples, TILE, comps * heads)
                .astype(BF16)
            )


def values_of(norm, choose, w_qkv):
    rows, width = norm.shape
    samples = choose.shape[1] // TILE
    comps, _, heads, _ = w_qkv.shape
    depth = width // 2
    columns = comps * heads
    return pl.pallas_call(
        value_kernel,
        grid=(width // depth,),
        out_shape=jax.ShapeDtypeStruct((samples, rows, columns), BF16),
        in_specs=[
            pl.BlockSpec((rows, depth), lambda k: (0, k)),
            pl.BlockSpec(choose.shape, lambda k: (0, 0, 0)),
            pl.BlockSpec((comps, 1, heads, depth), lambda k: (0, 2, 0, k)),
        ],
        out_specs=pl.BlockSpec((samples, rows, columns), lambda k: (0, 0, 0)),
        scratch_shapes=[pltpu.VMEM((width // BLOCK, rows, columns), BF16)],
        compiler_params=pltpu.CompilerParams(vmem_limit_bytes=50 * MIB),
        cost_estimate=pl.CostEstimate(
            flops=8 * rows * width * columns,
            bytes_accessed=2 * (norm.size + choose.size + columns * width),
            transcendentals=0,
        ),
        name="value_rows",
    )(norm, choose, w_qkv)


def erf(x):
    x = jnp.clip(x, -4.0, 4.0)
    s = x * x
    top = s * -2.72614225801306e-10 + 2.77068142495902e-08
    for c in (
        -2.10102402082508e-06,
        -5.69250639462346e-05,
        -7.34990630326855e-04,
        -2.95459980854025e-03,
        -1.60960333262415e-02,
    ):
        top = top * s + c
    low = s * -1.45660718464996e-05 + -2.13374055278905e-04
    for c in (-1.68282697438203e-03, -7.37332916720468e-03, -1.42647390514189e-02):
        low = low * s + c
    return x * top / low


def hidden_kernel(norm_ref, choose_ref, up_ref, out_ref, products):
    step = pl.program_id(1)
    rows, depth = norm_ref.shape
    samples, units = out_ref.shape
    block_products(norm_ref, up_ref, products, step * (depth // BLOCK))

    @pl.when(step == pl.num_programs(1) - 1)
    def _():
        total = jnp.zeros((samples, units), F32)
        for tile in range(rows // TILE):
            v = summed(choose_ref, products, tile)
            active = (0.5 * v) * (1.0 + erf(v * math.sqrt(0.5)))
            total = total + jnp.sum(active.reshape(samples, TILE, units), axis=1)
        out_ref[...] = total * (1.0 / rows)


def hidden_part(norm, choose, w_up, first, tiles):
    rows, width = norm.shape
    samples = choose.shape[1] // TILE
    depth = width // 2
    return pl.pallas_call(
        hidden_kernel,
        grid=(tiles, width // depth),
        out_shape=jax.ShapeDtypeStruct((samples, tiles * UNITS), F32),
        in_specs=[
            pl.BlockSpec((rows, depth), lambda i, k: (0, k)),
            pl.BlockSpec(choose.shape, lambda i, k: (0, 0, 0)),
            pl.BlockSpec((UNITS, depth), lambda i, k: (first + i, k)),
        ],
        out_specs=pl.BlockSpec((samples, UNITS), lambda i, k: (0, i)),
        scratch_shapes=[pltpu.VMEM((width // BLOCK, rows, UNITS), BF16)],
        compiler_params=pltpu.CompilerParams(vmem_limit_bytes=50 * MIB),
        cost_estimate=pl.CostEstimate(
            flops=8 * rows * width * UNITS * tiles,
            bytes_accessed=2 * (norm.size + choose.size + UNITS * tiles * width),
            transcendentals=samples * rows * UNITS * tiles,
        ),
        name="hidden_part",
    )(norm, choose, w_up)


def down_kernel(pooled_ref, down_ref, out_ref):
    samples = pooled_ref.shape[0]
    mean = pooled_ref[...]
    mean = jnp.concatenate([mean, jnp.zeros_like(mean)], axis=0).astype(BF16)
    part = jnp.dot(mean, down_ref[...], preferred_element_type=F32)[:samples]

    @pl.when(pl.program_id(0) == 0)
    def _():
        out_ref[...] = part

    @pl.when(pl.program_id(0) > 0)
    def _():
        out_ref[...] += part


def down_part(pooled, w_down, first):
    samples, units = pooled.shape
    width = w_down.shape[1]
    return pl.pallas_call(
        down_kernel,
        grid=(units // UNITS,),
        out_shape=jax.ShapeDtypeStruct((samples, width), F32),
        in_specs=[
            pl.BlockSpec((samples, UNITS), lambda i: (0, i)),
            pl.BlockSpec((UNITS, width), lambda i: (first + i, 0)),
        ],
        out_specs=pl.BlockSpec((samples, width), lambda i: (0, 0)),
        compiler_params=pltpu.CompilerParams(vmem_limit_bytes=50 * MIB),
        cost_estimate=pl.CostEstimate(
            flops=32 * units * width, bytes_accessed=2 * units * width, transcendentals=0
        ),
        name="down_part",
    )(pooled, w_down)


def attention_kernel(items, x_ref, query_gain_ref, key_gain_ref, *refs):
    *before, out_ref, held = refs
    parts, _, both, rows = x_ref.shape
    comps = both // 2
    head_dim = parts * comps
    ones = jnp.ones((16, rows), BF16)
    first = held.shape[0] - items

    def normed(values, gain_ref):
        values = values.reshape(head_dim, rows)
        average = jnp.mean(values, axis=0, keepdims=True)
        centered = values - average
        spread_sq = jnp.mean(centered * centered, axis=0, keepdims=True)
        return (centered * lax.rsqrt(spread_sq + 1e-06) * gain_ref[...]).astype(BF16)

    if before:
        held[:first] = before[0][...]
    for j in range(items):
        x = x_ref[:, j].astype(F32)
        query = normed(x[:, :comps], query_gain_ref)
        key = normed(x[:, comps:], key_gain_ref)
        scores = lax.dot_general(
            key, query, (((0,), (0,)), ((), ())), preferred_element_type=F32
        )
        e = jnp.exp2(scores * (math.log2(math.e) / math.sqrt(head_dim)))
        weights = (e * (1.0 / jnp.sum(e, axis=0, keepdims=True))).astype(BF16)
        mean = lax.dot_general(ones, weights, ACROSS, preferred_element_type=F32)[:1]
        held[first + j : first + j + 1, :] = mean * (1.0 / rows)
    if before:
        for part in range(parts):
            out_ref[part] = held[...].astype(BF16)
    else:
        out_ref[...] = held[...]


def key_weights(exchanged, query_gain, key_gain, *before):
    parts, items, both, rows = exchanged.shape
    head_dim = parts * both // 2
    count = items + sum(x.shape[0] for x in before)
    shape = jax.ShapeDtypeStruct((items, rows), F32)
    if before:
        shape = jax.ShapeDtypeStruct((parts, count, rows), BF16)
    return pl.pallas_call(
        functools.partial(attention_kernel, items),
        out_shape=shape,
        scratch_shapes=[pltpu.VMEM((count, rows), F32)],
        compiler_params=pltpu.CompilerParams(vmem_limit_bytes=50 * MIB),
        cost_estimate=pl.CostEstimate(
            flops=2 * items * rows * rows * head_dim,
            bytes_accessed=2 * exchanged.size,
            transcendentals=items * rows * rows,
        ),
        name="key_weights",
    )(exchanged, query_gain.reshape(head_dim, 1), key_gain.reshape(head_dim, 1), *before)


def feature_kernel(key_ref, value_ref, proj_ref, hidden_ref, token_ref, out_ref, attended):
    step = pl.program_id(0)
    parts, pieces, _ = key_ref.shape
    samples, rows, columns = value_ref.shape
    chunks = pieces // samples
    heads = parts * chunks

    @pl.when(step == 0)
    def _():
        row = lax.broadcasted_iota(jnp.int32, (heads, columns), 0)
        column = lax.broadcasted_iota(jnp.int32, (heads, columns), 1)
        source, piece = lax.rem(row, parts), row // parts
        head = jnp.where(
            piece == 0, heads - parts + source, source * (chunks - 1) + piece - 1
        )
        own = lax.rem(column, heads) == head
        results = []
        for m in range(samples):
            key = jnp.concatenate(
                [
                    key_ref[:, c * samples + m, :].astype(F32)
                    for c in range(chunks)
                ], axis=0
            )
            product = jnp.dot(key.astype(BF16), value_ref[m], preferred_element_type=F32)
            results.append(jnp.sum(jnp.where(own, product, 0.0), axis=0, keepdims=True))
        results.append(jnp.zeros((16 - samples, columns), F32))
        attended[...] = jnp.concatenate(results, axis=0).astype(BF16)

    part = jnp.dot(attended[...], proj_ref[...], preferred_element_type=F32)[:samples]
    part = part + hidden_ref[...]
    part = part + jnp.sum(token_ref[...].astype(F32), axis=0, keepdims=True) * (1.0 / rows)
    width = out_ref.shape[2]
    for j in range(out_ref.shape[0]):
        out_ref[j] = part[:, j * width : (j + 1) * width]


def feature_part(key_mean, value, w_proj, hidden, tokens, steps):
    parts = key_mean.shape[0]
    samples, rows, columns = value.shape
    own_rows, width = tokens.shape
    cut = width // steps
    return pl.pallas_call(
        feature_kernel,
        grid=(steps,),
        out_shape=jax.ShapeDtypeStruct((parts, samples, width // parts), F32),
        in_specs=[
            pl.BlockSpec(key_mean.shape, lambda i: (0, 0, 0)),
            pl.BlockSpec(value.shape, lambda i: (0, 0, 0)),
            pl.BlockSpec((columns, cut), lambda i: (0, i)),
            pl.BlockSpec((samples, cut), lambda i: (0, i)),
            pl.BlockSpec((own_rows, cut), lambda i: (0, i)),
        ],
        out_specs=pl.BlockSpec((parts // steps, samples, width // parts), lambda i: (i, 0, 0)),
        scratch_shapes=[pltpu.VMEM((16, columns), BF16)],
        compiler_params=pltpu.CompilerParams(vmem_limit_bytes=60 * MIB),
        cost_estimate=pl.CostEstimate(
            flops=2 * samples * rows * columns * 2 + 32 * columns * width,
            bytes_accessed=2 * columns * width + 2 * value.size,
            transcendentals=0,
        ),
        name="feature_part",
    )(key_mean, value, w_proj, hidden, tokens)


def joined(mine, other, columns):
    classes = mine.shape[1] - 2
    samples = mine.shape[0] - 1
    mean, other_mean = (x[:samples, classes : classes + 1] for x in (mine, other))
    joint = 0.5 * (mean + other_mean)
    logits = (
        mine[:samples, :classes]
        + other[:samples, :classes]
        + (mean - joint) * mine[samples:, :classes]
        + (other_mean - joint) * other[samples:, :classes]
    )
    gap = mean - other_mean
    spread = mine[:samples, classes + 1 :] + other[:samples, classes + 1 :]
    spread = spread + gap * gap * (0.5 * columns)
    return logits, joint, spread, mine[samples:, :classes] + other[samples:, :classes]


def packed(logits, mean, spread, gain_head):
    rows = jnp.concatenate([logits, mean, spread], axis=1)
    return jnp.concatenate([rows, jnp.pad(gain_head, ((0, 0), (0, 2)))], axis=0)


def finish_kernel(columns, mine_ref, other_ref, feature_ref, gain_ref, out_ref, bald_ref):
    logits, mean, spread, _ = joined(mine_ref[...], other_ref[...], columns)
    scale = lax.rsqrt(spread / (2 * columns) + 1e-06)
    out_ref[...] = (feature_ref[...] - mean) * scale * gain_ref[...]
    logits = soft_cap * jnp.tanh(logits * scale / soft_cap)
    samples = logits.shape[0]
    exp_logits = jnp.exp(logits)
    totals = jnp.sum(exp_logits, axis=1, keepdims=True)
    probs = exp_logits / totals
    entropy = jnp.log(totals) - jnp.sum(probs * logits, axis=1, keepdims=True)
    mean_probs = jnp.sum(probs, axis=0, keepdims=True) * (1.0 / samples)
    whole = -jnp.sum(mean_probs * jnp.log(mean_probs), axis=1, keepdims=True)
    bald_ref[...] = whole - jnp.sum(entropy, axis=0, keepdims=True) * (1.0 / samples)


def finished(feature, final_gain, w_head):
    highest = lax.Precision.HIGHEST
    gain_head = jnp.dot(final_gain[None], w_head.astype(F32), precision=highest)
    mean = jnp.mean(feature, axis=-1, keepdims=True)
    centered = feature - mean
    spread = jnp.sum(centered * centered, axis=-1, keepdims=True)
    logits = jnp.dot(centered * final_gain, w_head.astype(F32), precision=highest)
    columns = feature.shape[1]
    mine = packed(logits, mean, spread, gain_head)
    bits = 1
    while 2 * bits < lax.axis_size("inp"):
        mine = packed(*joined(mine, permuted(mine, bits), columns))
        columns = 2 * columns
        bits = 2 * bits
    embedding, score = pl.pallas_call(
        functools.partial(finish_kernel, columns),
        out_shape=(
            jax.ShapeDtypeStruct(feature.shape, F32),
            jax.ShapeDtypeStruct((1, 1), F32),
        ),
        compiler_params=pltpu.CompilerParams(vmem_limit_bytes=16 * MIB),
        name="finish",
    )(mine, permuted(mine, bits), feature, final_gain[None])
    return embedding[None], score.reshape(1)


def pipelined(
    tokens,
    dropout_masks,
    input_gain,
    w_qkv,
    w_up,
    query_gain,
    key_gain,
    w_proj,
    w_down,
    final_gain,
    w_head,
):
    n_parts = lax.axis_size("inp")
    me = lax.axis_index("inp")
    model_width = tokens.shape[1]
    n_comps, _, n_heads, _ = w_qkv.shape
    choose = choosers(dropout_masks)
    pieces, choose = gathered_pieces(*own_norm(tokens, input_gain), choose)
    norm = placed(pieces, me)
    together = lax.optimization_barrier

    def exchange(array):
        heads, samples, both, rows = array.shape
        array = array.reshape(n_parts, heads // n_parts * samples, both, rows)
        return lax.all_to_all(array, "inp", split_axis=0, concat_axis=0, tiled=True)

    ahead = n_parts
    behind = n_heads - ahead
    first = query_key(norm, choose, w_qkv, behind // ahead, ahead)
    second = query_key(norm, choose, w_qkv, 0, behind)
    value = values_of(norm, choose, w_qkv)
    first = exchange(first)
    second, value = together((second, value))
    second = exchange(second)
    norm, first = together((norm, first))
    tiles = w_up.shape[0] // UNITS // 2
    pooled = hidden_part(norm, choose, w_up, 0, tiles)
    more_pooled = hidden_part(norm, choose, w_up, tiles, tiles)
    hidden = down_part(pooled, w_down, 0)
    key_mean = key_weights(first, query_gain, key_gain)
    hidden, more_pooled, key_mean, second = together((hidden, more_pooled, key_mean, second))
    key_mean = key_weights(second, query_gain, key_gain, key_mean)
    more_pooled, key_mean = together((more_pooled, key_mean))
    hidden = hidden + down_part(more_pooled, w_down, tiles)
    key_mean = lax.all_to_all(key_mean, "inp", split_axis=0, concat_axis=0, tiled=True)
    partial_feature = feature_part(
        key_mean, value, w_proj.reshape(n_comps * n_heads, model_width), hidden, tokens, 8
    )
    slice_width = model_width // n_parts
    feature = jnp.sum(
        lax.all_to_all(partial_feature, "inp", split_axis=0, concat_axis=0, tiled=True), axis=0
    )
    gain = lax.dynamic_slice_in_dim(final_gain, me * slice_width, slice_width, 0)
    return finished(feature, gain, w_head)


def local(
    tokens,
    dropout_masks,
    input_gain,
    w_qkv,
    w_up,
    query_gain,
    key_gain,
    w_proj,
    w_down,
    final_gain,
    w_head,
):
    n_parts = lax.axis_size("inp")
    local_rows, model_width = tokens.shape
    n_masks, all_rows, n_blocks = dropout_masks.shape
    block_width = model_width // n_blocks
    n_comps, three_kinds, n_heads, ignored_width = w_qkv.shape
    n_units = w_up.shape[0]
    head_dim = n_comps * n_parts
    images = all_rows // PATCHES
    qkv_cols = three_kinds * n_heads * n_comps
    items_dev = n_masks * n_heads // n_parts
    highest = lax.Precision.HIGHEST
    joined_weight = jnp.concatenate(
        [jnp.transpose(w_qkv, (1, 2, 0, 3)).reshape(qkv_cols, model_width), w_up], axis=0
    )
    row_piece = lax.all_gather(tokens, "inp", axis=0, tiled=True)
    row_count = row_piece.shape[0]
    normed = norm_last(row_piece.astype(jnp.float32), input_gain).astype(jnp.bfloat16)
    masked = (
        normed.reshape(1, row_count, n_blocks, block_width)
        * dropout_masks.astype(jnp.bfloat16)[..., None]
    )
    masked = masked.reshape(n_masks, row_count, model_width)
    result = jnp.einsum("mkd,cd->mck", masked, joined_weight, preferred_element_type=jnp.float32)
    projected = 2.0 * result
    qkv_half = (
        projected[:, :qkv_cols]
        .astype(jnp.bfloat16)
        .reshape(n_masks, three_kinds, n_heads * n_comps, all_rows)
    )
    item_shape = (n_parts, items_dev, n_comps, all_rows)
    query_send = qkv_half[:, 0].reshape(item_shape)
    key_send = qkv_half[:, 1].reshape(item_shape)
    value_send = qkv_half[:, 2].reshape(item_shape)
    activated = jax.nn.gelu(projected[:, qkv_cols:], approximate=False)
    pooled_hidden = jnp.mean(activated.reshape(n_masks, n_units, images, PATCHES), axis=-1).astype(
        jnp.bfloat16
    )
    query_in = lax.all_to_all(query_send, "inp", split_axis=0, concat_axis=2, tiled=True)
    key_in = lax.all_to_all(key_send, "inp", split_axis=0, concat_axis=2, tiled=True)
    value_in = lax.all_to_all(value_send, "inp", split_axis=0, concat_axis=2, tiled=True)
    n_items = query_in.shape[1]
    shape_four = (n_items, head_dim, images, PATCHES)
    query_norm = norm_second(query_in.reshape(shape_four).astype(jnp.float32), query_gain).astype(
        jnp.bfloat16
    )
    key_norm = norm_second(key_in.reshape(shape_four).astype(jnp.float32), key_gain).astype(
        jnp.bfloat16
    )
    scores = jnp.einsum(
        "jcip,jciq->jipq", query_norm, key_norm, preferred_element_type=jnp.float32
    ) / math.sqrt(head_dim)
    exp_scores = jnp.exp(scores)
    weights = (exp_scores / jnp.sum(exp_scores, axis=-1, keepdims=True)).astype(jnp.bfloat16)
    query_mean = jnp.sum(weights, axis=2, dtype=jnp.float32) / PATCHES
    pooled = jnp.einsum(
        "jiq,jciq->jic",
        query_mean,
        value_in.reshape(shape_four).astype(jnp.float32),
        precision=highest,
    )
    attended = pooled.astype(jnp.bfloat16)[None]
    returned = lax.all_to_all(attended, "inp", split_axis=3, concat_axis=0, tiled=True)
    returned = returned.reshape(n_masks, n_heads, images, n_comps)
    mixed_sum = jnp.einsum("mhic,chd->imd", returned, w_proj, preferred_element_type=jnp.float32)
    mixed_sum = mixed_sum + jnp.einsum(
        "mfi,fd->imd", pooled_hidden, w_down, preferred_element_type=jnp.float32
    )
    row_ids = lax.axis_index("inp") * local_rows + jnp.arange(local_rows, dtype=jnp.int32)
    row_owner = (row_ids // PATCHES)[None, :] == jnp.arange(images, dtype=jnp.int32)[:, None]
    input_sum = (
        jnp.dot(row_owner.astype(jnp.bfloat16), tokens, preferred_element_type=jnp.float32)
        / PATCHES
    )
    partial_feature = mixed_sum + input_sum[:, None, :]
    feature = lax.psum(partial_feature, "inp")
    normalized = norm_last(feature, final_gain)
    slice_width = model_width // n_parts
    embedding = lax.dynamic_slice_in_dim(
        normalized, lax.axis_index("inp") * slice_width, slice_width, 2
    )
    logit_part = jnp.einsum(
        "imd,dc->imc", embedding.astype(jnp.bfloat16), w_head, preferred_element_type=jnp.float32
    )
    raw_logits = lax.psum(logit_part, "inp")
    logits = soft_cap * jnp.tanh(raw_logits / soft_cap)
    return (embedding, bald_score(logits))


def solution(mesh):
    fits = mesh.shape["inp"] == PIPELINED_PARTS
    return jax.shard_map(
        pipelined if fits else local,
        mesh=mesh,
        in_specs=(
            P(("groups", "inp"), None),
            P(None, "groups", None),
            P(),
            P("inp", None, None, None),
            P("inp", None),
            P(),
            P(),
            P("inp", None, None),
            P("inp", None),
            P(),
            P("inp", None),
        ),
        out_specs=(P("groups", None, "inp"), P("groups")),
        check_vma=False,
    )
```

```python
import functools
import math

import jax
import jax.numpy as jnp
from jax import lax
from jax.experimental import pallas as pl
from jax.experimental.pallas import tpu as pltpu
from jax.sharding import PartitionSpec as P

PATCHES = 256


soft_cap = 20.0
PIPELINED_PARTS = 16
UNITS = 256
F32 = jnp.float32
BF16 = jnp.bfloat16
MIB = 1024 * 1024


def norm_last(values, gain):
    average = jnp.mean(values, axis=-1, keepdims=True)
    centered = values - average
    spread_sq = jnp.mean(centered * centered, axis=-1, keepdims=True)
    return centered * lax.rsqrt(spread_sq + 1e-06) * gain


def norm_second(values, gain):
    average = jnp.mean(values, axis=1, keepdims=True)
    centered = values - average
    spread_sq = jnp.mean(centered * centered, axis=1, keepdims=True)
    return centered * lax.rsqrt(spread_sq + 1e-06) * gain[None, :, None, None]


def bald_score(logits):
    exp_logits = jnp.exp(logits)
    totals = jnp.sum(exp_logits, axis=-1, keepdims=True)
    sample_probs = exp_logits / totals
    entropy = jnp.log(totals[..., 0]) - jnp.sum(sample_probs * logits, axis=-1)
    mean_probs = jnp.mean(sample_probs, axis=1)
    joint = -jnp.sum(mean_probs * jnp.log(mean_probs), axis=-1)
    return joint - jnp.mean(entropy, axis=1)


def permuted(array, bits):
    count = lax.axis_size("inp")
    return lax.ppermute(array, "inp", [(i, i ^ bits) for i in range(count)])


def own_norm_kernel(x_ref, gain_ref, first_ref, second_ref):
    y = norm_last(x_ref[...].astype(F32), gain_ref[...]).astype(BF16)
    cut = first_ref.shape[1]
    first_ref[...] = y[:, :cut]
    second_ref[...] = y[:, cut:]


def own_norm(tokens, gain):
    rows, width = tokens.shape
    cut = width // 3 * 2
    return pl.pallas_call(
        own_norm_kernel,
        out_shape=(
            jax.ShapeDtypeStruct((rows, cut), BF16),
            jax.ShapeDtypeStruct((rows, width - cut), BF16),
        ),
        compiler_params=pltpu.CompilerParams(vmem_limit_bytes=60 * MIB),
        name="own_norm",
    )(tokens, gain.reshape(1, width))


def gathered_pieces(first, second, beside):
    along_z = jnp.stack([first] + [permuted(first, 4 * k) for k in range(1, 4)])
    pair = jnp.stack([second, permuted(second, 2)])
    along_z, pair, beside = lax.optimization_barrier((along_z, pair, beside))
    across_y = permuted(along_z, 2)
    moved = [permuted(pair, 4 * k) for k in range(1, 4)]
    across_y, *moved = lax.optimization_barrier((across_y, *moved))
    pieces = [
        (0, [4 * k for k in range(4)], along_z),
        (0, [4 * k + 2 for k in range(4)], across_y),
    ]
    for k, array in enumerate([pair, *moved]):
        pieces.append((first.shape[1], [4 * k, 4 * k + 2], array))
    pieces = pieces + [
        (side, [b ^ 1 for b in bits], permuted(array, 1)) for side, bits, array in pieces
    ]
    return pieces, beside


def place_kernel(layout, me_ref, *refs):
    sources, out_ref = refs[:-1], refs[-1]
    me = me_ref[0]
    for (side, bits), source in zip(layout, sources, strict=True):
        _, rows, columns = source.shape
        for at, bit in enumerate(bits):
            start = pl.multiple_of((me ^ bit) * rows, rows)
            out_ref[pl.ds(start, rows), side : side + columns] = source[at]


def placed(pieces, me):
    rows = pieces[0][2].shape[1]
    total = rows * sum(len(bits) for side, bits, _ in pieces if side == 0)
    width = sum(array.size for _, _, array in pieces) // total
    layout = [(side, bits) for side, bits, _ in pieces]
    return pl.pallas_call(
        functools.partial(place_kernel, layout),
        out_shape=jax.ShapeDtypeStruct((total, width), BF16),
        in_specs=[pl.BlockSpec(memory_space=pltpu.SMEM)]
        + [pl.BlockSpec(memory_space=pltpu.VMEM)] * len(pieces),
        out_specs=pl.BlockSpec(memory_space=pltpu.VMEM),
        compiler_params=pltpu.CompilerParams(vmem_limit_bytes=50 * MIB),
        name="place_rows",
    )(me.reshape(1), *[array for _, _, array in pieces])


ACROSS = (((1,), (1,)), ((), ()))
TILE = 16
BLOCK = 128


def choosers(dropout_masks):
    samples, rows, blocks = dropout_masks.shape
    tiles = rows // TILE
    kept = dropout_masks.astype(BF16).reshape(samples, tiles, TILE, blocks)
    kept = jnp.transpose(kept, (1, 0, 2, 3)).reshape(tiles, samples * TILE, blocks)
    column = jnp.arange(blocks * TILE)
    spread = (column[None] // TILE == jnp.arange(blocks)[:, None]).astype(BF16)
    own = jnp.arange(samples * TILE)[:, None] % TILE == column[None] % TILE
    wide = jnp.einsum("trb,bc->trc", kept, spread, preferred_element_type=F32)
    return jnp.where(own[None], 2.0 * wide, 0.0).astype(BF16)


def block_products(norm_ref, weight, products, first):
    for j in range(weight.shape[1] // BLOCK):
        at = slice(j * BLOCK, (j + 1) * BLOCK)
        products[first + j] = lax.dot_general(
            norm_ref[:, at], weight[:, at], ACROSS, preferred_element_type=F32
        ).astype(BF16)


def summed(choose_ref, products, tile):
    blocks, _, columns = products.shape
    part = products[:, tile * TILE : (tile + 1) * TILE, :].reshape(blocks * TILE, columns)
    return jnp.dot(choose_ref[tile], part, preferred_element_type=F32)


def query_key_kernel(norm_ref, choose_ref, w_ref, out_ref, products, sums, turned):
    step = pl.program_id(0)
    rows, depth = norm_ref.shape
    comps, kinds, heads, _ = w_ref.shape
    columns = comps * kinds * heads
    block_products(
        norm_ref, w_ref[...].reshape(columns, depth), products, step * (depth // BLOCK)
    )

    @pl.when(step == pl.num_programs(0) - 1)
    def _():
        samples = sums.shape[0]
        for tile in range(rows // TILE):
            sums[:, tile * TILE : (tile + 1) * TILE, :] = summed(
                choose_ref, products, tile
            ).reshape(samples, TILE, columns)
        for m in range(samples):
            for part in range(rows // 128):
                at = slice(part * 128, (part + 1) * 128)
                turned[m * (rows // 128) + part] = sums[m, at, :].T
            for part in range(rows // 128):
                at = slice(part * 128, (part + 1) * 128)
                held = turned.at[m * (rows // 128) + part]
                for h in range(heads):
                    both = [
                        held[pl.ds(t * heads + h, comps, stride=kinds * heads), :]
                        for t in range(kinds)
                    ]
                    out_ref[h, m, :, at] = jnp.concatenate(both, axis=0).astype(BF16)


def query_key(norm, choose, w_qkv, chunk, heads):
    rows, width = norm.shape
    samples = choose.shape[1] // TILE
    comps = w_qkv.shape[0]
    depth = width // 2
    columns = 2 * comps * heads
    shape = (heads, samples, 2 * comps, rows)
    return pl.pallas_call(
        query_key_kernel,
        grid=(width // depth,),
        out_shape=jax.ShapeDtypeStruct(shape, BF16),
        in_specs=[
            pl.BlockSpec((rows, depth), lambda k: (0, k)),
            pl.BlockSpec(choose.shape, lambda k: (0, 0, 0)),
            pl.BlockSpec((comps, 2, heads, depth), lambda k: (0, 0, chunk, k)),
        ],
        out_specs=pl.BlockSpec(shape, lambda k: (0, 0, 0, 0)),
        scratch_shapes=[
            pltpu.VMEM((width // BLOCK, rows, columns), BF16),
            pltpu.VMEM((samples, rows, columns), F32),
            pltpu.VMEM((samples * rows // 128, columns, 128), F32),
        ],
        compiler_params=pltpu.CompilerParams(vmem_limit_bytes=50 * MIB),
        cost_estimate=pl.CostEstimate(
            flops=8 * rows * width * columns,
            bytes_accessed=2 * (norm.size + choose.size + columns * width),
            transcendentals=0,
        ),
        name="query_key",
    )(norm, choose, w_qkv)


def value_kernel(norm_ref, choose_ref, w_ref, out_ref, products):
    step = pl.program_id(0)
    rows, depth = norm_ref.shape
    comps, _, heads, _ = w_ref.shape
    block_products(
        norm_ref, w_ref[:, 0].reshape(comps * heads, depth), products, step * (depth // BLOCK)
    )

    @pl.when(step == pl.num_programs(0) - 1)
    def _():
        samples = out_ref.shape[0]
        for tile in range(rows // TILE):
            out_ref[:, tile * TILE : (tile + 1) * TILE, :] = (
                summed(choose_ref, products, tile)
                .reshape(samples, TILE, comps * heads)
                .astype(BF16)
            )


def values_of(norm, choose, w_qkv):
    rows, width = norm.shape
    samples = choose.shape[1] // TILE
    comps, _, heads, _ = w_qkv.shape
    depth = width // 2
    columns = comps * heads
    return pl.pallas_call(
        value_kernel,
        grid=(width // depth,),
        out_shape=jax.ShapeDtypeStruct((samples, rows, columns), BF16),
        in_specs=[
            pl.BlockSpec((rows, depth), lambda k: (0, k)),
            pl.BlockSpec(choose.shape, lambda k: (0, 0, 0)),
            pl.BlockSpec((comps, 1, heads, depth), lambda k: (0, 2, 0, k)),
        ],
        out_specs=pl.BlockSpec((samples, rows, columns), lambda k: (0, 0, 0)),
        scratch_shapes=[pltpu.VMEM((width // BLOCK, rows, columns), BF16)],
        compiler_params=pltpu.CompilerParams(vmem_limit_bytes=50 * MIB),
        cost_estimate=pl.CostEstimate(
            flops=8 * rows * width * columns,
            bytes_accessed=2 * (norm.size + choose.size + columns * width),
            transcendentals=0,
        ),
        name="value_rows",
    )(norm, choose, w_qkv)


def erf(x):
    x = jnp.clip(x, -4.0, 4.0)
    s = x * x
    top = s * -2.72614225801306e-10 + 2.77068142495902e-08
    for c in (
        -2.10102402082508e-06,
        -5.69250639462346e-05,
        -7.34990630326855e-04,
        -2.95459980854025e-03,
        -1.60960333262415e-02,
    ):
        top = top * s + c
    low = s * -1.45660718464996e-05 + -2.13374055278905e-04
    for c in (-1.68282697438203e-03, -7.37332916720468e-03, -1.42647390514189e-02):
        low = low * s + c
    return x * top / low


def hidden_kernel(norm_ref, choose_ref, up_ref, out_ref, products):
    step = pl.program_id(1)
    rows, depth = norm_ref.shape
    samples, units = out_ref.shape
    block_products(norm_ref, up_ref, products, step * (depth // BLOCK))

    @pl.when(step == pl.num_programs(1) - 1)
    def _():
        total = jnp.zeros((samples, units), F32)
        for tile in range(rows // TILE):
            v = summed(choose_ref, products, tile)
            active = (0.5 * v) * (1.0 + erf(v * math.sqrt(0.5)))
            total = total + jnp.sum(active.reshape(samples, TILE, units), axis=1)
        out_ref[...] = total * (1.0 / rows)


def hidden_part(norm, choose, w_up, first, tiles):
    rows, width = norm.shape
    samples = choose.shape[1] // TILE
    depth = width // 2
    return pl.pallas_call(
        hidden_kernel,
        grid=(tiles, width // depth),
        out_shape=jax.ShapeDtypeStruct((samples, tiles * UNITS), F32),
        in_specs=[
            pl.BlockSpec((rows, depth), lambda i, k: (0, k)),
            pl.BlockSpec(choose.shape, lambda i, k: (0, 0, 0)),
            pl.BlockSpec((UNITS, depth), lambda i, k: (first + i, k)),
        ],
        out_specs=pl.BlockSpec((samples, UNITS), lambda i, k: (0, i)),
        scratch_shapes=[pltpu.VMEM((width // BLOCK, rows, UNITS), BF16)],
        compiler_params=pltpu.CompilerParams(vmem_limit_bytes=50 * MIB),
        cost_estimate=pl.CostEstimate(
            flops=8 * rows * width * UNITS * tiles,
            bytes_accessed=2 * (norm.size + choose.size + UNITS * tiles * width),
            transcendentals=samples * rows * UNITS * tiles,
        ),
        name="hidden_part",
    )(norm, choose, w_up)


def down_kernel(pooled_ref, down_ref, out_ref):
    samples = pooled_ref.shape[0]
    mean = pooled_ref[...]
    mean = jnp.concatenate([mean, jnp.zeros_like(mean)], axis=0).astype(BF16)
    part = jnp.dot(mean, down_ref[...], preferred_element_type=F32)[:samples]

    @pl.when(pl.program_id(0) == 0)
    def _():
        out_ref[...] = part

    @pl.when(pl.program_id(0) > 0)
    def _():
        out_ref[...] += part


def down_part(pooled, w_down, first):
    samples, units = pooled.shape
    width = w_down.shape[1]
    return pl.pallas_call(
        down_kernel,
        grid=(units // UNITS,),
        out_shape=jax.ShapeDtypeStruct((samples, width), F32),
        in_specs=[
            pl.BlockSpec((samples, UNITS), lambda i: (0, i)),
            pl.BlockSpec((UNITS, width), lambda i: (first + i, 0)),
        ],
        out_specs=pl.BlockSpec((samples, width), lambda i: (0, 0)),
        compiler_params=pltpu.CompilerParams(vmem_limit_bytes=50 * MIB),
        cost_estimate=pl.CostEstimate(
            flops=32 * units * width, bytes_accessed=2 * units * width, transcendentals=0
        ),
        name="down_part",
    )(pooled, w_down)


def attention_kernel(items, x_ref, query_gain_ref, key_gain_ref, *refs):
    *before, out_ref, held = refs
    parts, _, both, rows = x_ref.shape
    comps = both // 2
    head_dim = parts * comps
    ones = jnp.ones((16, rows), BF16)
    first = held.shape[0] - items

    def normed(values, gain_ref):
        values = values.reshape(head_dim, rows)
        average = jnp.mean(values, axis=0, keepdims=True)
        centered = values - average
        spread_sq = jnp.mean(centered * centered, axis=0, keepdims=True)
        return (centered * lax.rsqrt(spread_sq + 1e-06) * gain_ref[...]).astype(BF16)

    if before:
        held[:first] = before[0][...]
    for j in range(items):
        x = x_ref[:, j].astype(F32)
        query = normed(x[:, :comps], query_gain_ref)
        key = normed(x[:, comps:], key_gain_ref)
        scores = lax.dot_general(
            key, query, (((0,), (0,)), ((), ())), preferred_element_type=F32
        )
        e = jnp.exp2(scores * (math.log2(math.e) / math.sqrt(head_dim)))
        weights = (e * (1.0 / jnp.sum(e, axis=0, keepdims=True))).astype(BF16)
        mean = lax.dot_general(ones, weights, ACROSS, preferred_element_type=F32)[:1]
        held[first + j : first + j + 1, :] = mean * (1.0 / rows)
    if before:
        for part in range(parts):
            out_ref[part] = held[...].astype(BF16)
    else:
        out_ref[...] = held[...]


def key_weights(exchanged, query_gain, key_gain, *before):
    parts, items, both, rows = exchanged.shape
    head_dim = parts * both // 2
    count = items + sum(x.shape[0] for x in before)
    shape = jax.ShapeDtypeStruct((items, rows), F32)
    if before:
        shape = jax.ShapeDtypeStruct((parts, count, rows), BF16)
    return pl.pallas_call(
        functools.partial(attention_kernel, items),
        out_shape=shape,
        scratch_shapes=[pltpu.VMEM((count, rows), F32)],
        compiler_params=pltpu.CompilerParams(vmem_limit_bytes=50 * MIB),
        cost_estimate=pl.CostEstimate(
            flops=2 * items * rows * rows * head_dim,
            bytes_accessed=2 * exchanged.size,
            transcendentals=items * rows * rows,
        ),
        name="key_weights",
    )(exchanged, query_gain.reshape(head_dim, 1), key_gain.reshape(head_dim, 1), *before)


def feature_kernel(key_ref, value_ref, proj_ref, hidden_ref, token_ref, out_ref, attended):
    step = pl.program_id(0)
    parts, pieces, _ = key_ref.shape
    samples, rows, columns = value_ref.shape
    chunks = pieces // samples
    heads = parts * chunks

    @pl.when(step == 0)
    def _():
        row = lax.broadcasted_iota(jnp.int32, (heads, columns), 0)
        column = lax.broadcasted_iota(jnp.int32, (heads, columns), 1)
        source, piece = lax.rem(row, parts), row // parts
        head = jnp.where(
            piece == 0, heads - parts + source, source * (chunks - 1) + piece - 1
        )
        own = lax.rem(column, heads) == head
        results = []
        for m in range(samples):
            key = jnp.concatenate(
                [
                    key_ref[:, c * samples + m, :].astype(F32)
                    for c in range(chunks)
                ], axis=0
            )
            product = jnp.dot(key.astype(BF16), value_ref[m], preferred_element_type=F32)
            results.append(jnp.sum(jnp.where(own, product, 0.0), axis=0, keepdims=True))
        results.append(jnp.zeros((16 - samples, columns), F32))
        attended[...] = jnp.concatenate(results, axis=0).astype(BF16)

    part = jnp.dot(attended[...], proj_ref[...], preferred_element_type=F32)[:samples]
    part = part + hidden_ref[...]
    part = part + jnp.sum(token_ref[...].astype(F32), axis=0, keepdims=True) * (1.0 / rows)
    width = out_ref.shape[2]
    for j in range(out_ref.shape[0]):
        out_ref[j] = part[:, j * width : (j + 1) * width]


def feature_part(key_mean, value, w_proj, hidden, tokens, steps):
    parts = key_mean.shape[0]
    samples, rows, columns = value.shape
    own_rows, width = tokens.shape
    cut = width // steps
    return pl.pallas_call(
        feature_kernel,
        grid=(steps,),
        out_shape=jax.ShapeDtypeStruct((parts, samples, width // parts), F32),
        in_specs=[
            pl.BlockSpec(key_mean.shape, lambda i: (0, 0, 0)),
            pl.BlockSpec(value.shape, lambda i: (0, 0, 0)),
            pl.BlockSpec((columns, cut), lambda i: (0, i)),
            pl.BlockSpec((samples, cut), lambda i: (0, i)),
            pl.BlockSpec((own_rows, cut), lambda i: (0, i)),
        ],
        out_specs=pl.BlockSpec((parts // steps, samples, width // parts), lambda i: (i, 0, 0)),
        scratch_shapes=[pltpu.VMEM((16, columns), BF16)],
        compiler_params=pltpu.CompilerParams(vmem_limit_bytes=40 * MIB),
        cost_estimate=pl.CostEstimate(
            flops=2 * samples * rows * columns * 2 + 32 * columns * width,
            bytes_accessed=2 * columns * width + 2 * value.size,
            transcendentals=0,
        ),
        name="feature_part",
    )(key_mean, value, w_proj, hidden, tokens)


def joined(mine, other, columns):
    classes = mine.shape[1] - 2
    samples = mine.shape[0] - 1
    mean, other_mean = (x[:samples, classes : classes + 1] for x in (mine, other))
    joint = 0.5 * (mean + other_mean)
    logits = (
        mine[:samples, :classes]
        + other[:samples, :classes]
        + (mean - joint) * mine[samples:, :classes]
        + (other_mean - joint) * other[samples:, :classes]
    )
    gap = mean - other_mean
    spread = mine[:samples, classes + 1 :] + other[:samples, classes + 1 :]
    spread = spread + gap * gap * (0.5 * columns)
    return logits, joint, spread, mine[samples:, :classes] + other[samples:, :classes]


def packed(logits, mean, spread, gain_head):
    rows = jnp.concatenate([logits, mean, spread], axis=1)
    return jnp.concatenate([rows, jnp.pad(gain_head, ((0, 0), (0, 2)))], axis=0)


def finish_kernel(columns, mine_ref, other_ref, feature_ref, gain_ref, out_ref, bald_ref):
    logits, mean, spread, _ = joined(mine_ref[...], other_ref[...], columns)
    scale = lax.rsqrt(spread / (2 * columns) + 1e-06)
    out_ref[...] = (feature_ref[...] - mean) * scale * gain_ref[...]
    logits = soft_cap * jnp.tanh(logits * scale / soft_cap)
    samples = logits.shape[0]
    exp_logits = jnp.exp(logits)
    totals = jnp.sum(exp_logits, axis=1, keepdims=True)
    probs = exp_logits / totals
    entropy = jnp.log(totals) - jnp.sum(probs * logits, axis=1, keepdims=True)
    mean_probs = jnp.sum(probs, axis=0, keepdims=True) * (1.0 / samples)
    whole = -jnp.sum(mean_probs * jnp.log(mean_probs), axis=1, keepdims=True)
    bald_ref[...] = whole - jnp.sum(entropy, axis=0, keepdims=True) * (1.0 / samples)


def finished(feature, final_gain, w_head):
    highest = lax.Precision.HIGHEST
    gain_head = jnp.dot(final_gain[None], w_head.astype(F32), precision=highest)
    mean = jnp.mean(feature, axis=-1, keepdims=True)
    centered = feature - mean
    spread = jnp.sum(centered * centered, axis=-1, keepdims=True)
    logits = jnp.dot(centered * final_gain, w_head.astype(F32), precision=highest)
    columns = feature.shape[1]
    mine = packed(logits, mean, spread, gain_head)
    bits = 1
    while 2 * bits < lax.axis_size("inp"):
        mine = packed(*joined(mine, permuted(mine, bits), columns))
        columns = 2 * columns
        bits = 2 * bits
    embedding, score = pl.pallas_call(
        functools.partial(finish_kernel, columns),
        out_shape=(
            jax.ShapeDtypeStruct(feature.shape, F32),
            jax.ShapeDtypeStruct((1, 1), F32),
        ),
        compiler_params=pltpu.CompilerParams(vmem_limit_bytes=16 * MIB),
        name="finish",
    )(mine, permuted(mine, bits), feature, final_gain[None])
    return embedding[None], score.reshape(1)


def pipelined(
    tokens,
    dropout_masks,
    input_gain,
    w_qkv,
    w_up,
    query_gain,
    key_gain,
    w_proj,
    w_down,
    final_gain,
    w_head,
):
    n_parts = lax.axis_size("inp")
    me = lax.axis_index("inp")
    model_width = tokens.shape[1]
    n_comps, _, n_heads, _ = w_qkv.shape
    choose = choosers(dropout_masks)
    pieces, choose = gathered_pieces(*own_norm(tokens, input_gain), choose)
    norm = placed(pieces, me)
    together = lax.optimization_barrier

    def exchange(array):
        heads, samples, both, rows = array.shape
        array = array.reshape(n_parts, heads // n_parts * samples, both, rows)
        return lax.all_to_all(array, "inp", split_axis=0, concat_axis=0, tiled=True)

    ahead = n_parts
    behind = n_heads - ahead
    first = query_key(norm, choose, w_qkv, behind // ahead, ahead)
    second = query_key(norm, choose, w_qkv, 0, behind)
    value = values_of(norm, choose, w_qkv)
    first = exchange(first)
    second, value = together((second, value))
    second = exchange(second)
    norm, first = together((norm, first))
    tiles = w_up.shape[0] // UNITS // 2
    pooled = hidden_part(norm, choose, w_up, 0, tiles)
    more_pooled = hidden_part(norm, choose, w_up, tiles, tiles)
    hidden = down_part(pooled, w_down, 0)
    key_mean = key_weights(first, query_gain, key_gain)
    hidden, more_pooled, key_mean, second = together((hidden, more_pooled, key_mean, second))
    key_mean = key_weights(second, query_gain, key_gain, key_mean)
    more_pooled, key_mean = together((more_pooled, key_mean))
    hidden = hidden + down_part(more_pooled, w_down, tiles)
    key_mean = lax.all_to_all(key_mean, "inp", split_axis=0, concat_axis=0, tiled=True)
    partial_feature = feature_part(
        key_mean, value, w_proj.reshape(n_comps * n_heads, model_width), hidden, tokens, 2
    )
    slice_width = model_width // n_parts
    feature = jnp.sum(
        lax.all_to_all(partial_feature, "inp", split_axis=0, concat_axis=0, tiled=True), axis=0
    )
    gain = lax.dynamic_slice_in_dim(final_gain, me * slice_width, slice_width, 0)
    return finished(feature, gain, w_head)


def local(
    tokens,
    dropout_masks,
    input_gain,
    w_qkv,
    w_up,
    query_gain,
    key_gain,
    w_proj,
    w_down,
    final_gain,
    w_head,
):
    n_parts = lax.axis_size("inp")
    local_rows, model_width = tokens.shape
    n_masks, all_rows, n_blocks = dropout_masks.shape
    block_width = model_width // n_blocks
    n_comps, three_kinds, n_heads, ignored_width = w_qkv.shape
    n_units = w_up.shape[0]
    head_dim = n_comps * n_parts
    images = all_rows // PATCHES
    qkv_cols = three_kinds * n_heads * n_comps
    items_dev = n_masks * n_heads // n_parts
    highest = lax.Precision.HIGHEST
    joined_weight = jnp.concatenate(
        [jnp.transpose(w_qkv, (1, 2, 0, 3)).reshape(qkv_cols, model_width), w_up], axis=0
    )
    row_piece = lax.all_gather(tokens, "inp", axis=0, tiled=True)
    row_count = row_piece.shape[0]
    normed = norm_last(row_piece.astype(jnp.float32), input_gain).astype(jnp.bfloat16)
    masked = (
        normed.reshape(1, row_count, n_blocks, block_width)
        * dropout_masks.astype(jnp.bfloat16)[..., None]
    )
    masked = masked.reshape(n_masks, row_count, model_width)
    result = jnp.einsum("mkd,cd->mck", masked, joined_weight, preferred_element_type=jnp.float32)
    projected = 2.0 * result
    qkv_half = (
        projected[:, :qkv_cols]
        .astype(jnp.bfloat16)
        .reshape(n_masks, three_kinds, n_heads * n_comps, all_rows)
    )
    item_shape = (n_parts, items_dev, n_comps, all_rows)
    query_send = qkv_half[:, 0].reshape(item_shape)
    key_send = qkv_half[:, 1].reshape(item_shape)
    value_send = qkv_half[:, 2].reshape(item_shape)
    activated = jax.nn.gelu(projected[:, qkv_cols:], approximate=False)
    pooled_hidden = jnp.mean(activated.reshape(n_masks, n_units, images, PATCHES), axis=-1).astype(
        jnp.bfloat16
    )
    query_in = lax.all_to_all(query_send, "inp", split_axis=0, concat_axis=2, tiled=True)
    key_in = lax.all_to_all(key_send, "inp", split_axis=0, concat_axis=2, tiled=True)
    value_in = lax.all_to_all(value_send, "inp", split_axis=0, concat_axis=2, tiled=True)
    n_items = query_in.shape[1]
    shape_four = (n_items, head_dim, images, PATCHES)
    query_norm = norm_second(query_in.reshape(shape_four).astype(jnp.float32), query_gain).astype(
        jnp.bfloat16
    )
    key_norm = norm_second(key_in.reshape(shape_four).astype(jnp.float32), key_gain).astype(
        jnp.bfloat16
    )
    scores = jnp.einsum(
        "jcip,jciq->jipq", query_norm, key_norm, preferred_element_type=jnp.float32
    ) / math.sqrt(head_dim)
    exp_scores = jnp.exp(scores)
    weights = (exp_scores / jnp.sum(exp_scores, axis=-1, keepdims=True)).astype(jnp.bfloat16)
    query_mean = jnp.sum(weights, axis=2, dtype=jnp.float32) / PATCHES
    pooled = jnp.einsum(
        "jiq,jciq->jic",
        query_mean,
        value_in.reshape(shape_four).astype(jnp.float32),
        precision=highest,
    )
    attended = pooled.astype(jnp.bfloat16)[None]
    returned = lax.all_to_all(attended, "inp", split_axis=3, concat_axis=0, tiled=True)
    returned = returned.reshape(n_masks, n_heads, images, n_comps)
    mixed_sum = jnp.einsum("mhic,chd->imd", returned, w_proj, preferred_element_type=jnp.float32)
    mixed_sum = mixed_sum + jnp.einsum(
        "mfi,fd->imd", pooled_hidden, w_down, preferred_element_type=jnp.float32
    )
    row_ids = lax.axis_index("inp") * local_rows + jnp.arange(local_rows, dtype=jnp.int32)
    row_owner = (row_ids // PATCHES)[None, :] == jnp.arange(images, dtype=jnp.int32)[:, None]
    input_sum = (
        jnp.dot(row_owner.astype(jnp.bfloat16), tokens, preferred_element_type=jnp.float32)
        / PATCHES
    )
    partial_feature = mixed_sum + input_sum[:, None, :]
    feature = lax.psum(partial_feature, "inp")
    normalized = norm_last(feature, final_gain)
    slice_width = model_width // n_parts
    embedding = lax.dynamic_slice_in_dim(
        normalized, lax.axis_index("inp") * slice_width, slice_width, 2
    )
    logit_part = jnp.einsum(
        "imd,dc->imc", embedding.astype(jnp.bfloat16), w_head, preferred_element_type=jnp.float32
    )
    raw_logits = lax.psum(logit_part, "inp")
    logits = soft_cap * jnp.tanh(raw_logits / soft_cap)
    return (embedding, bald_score(logits))


def solution(mesh):
    fits = mesh.shape["inp"] == PIPELINED_PARTS
    return jax.shard_map(
        pipelined if fits else local,
        mesh=mesh,
        in_specs=(
            P(("groups", "inp"), None),
            P(None, "groups", None),
            P(),
            P("inp", None, None, None),
            P("inp", None),
            P(),
            P(),
            P("inp", None, None),
            P("inp", None),
            P(),
            P("inp", None),
        ),
        out_specs=(P("groups", None, "inp"), P("groups")),
        check_vma=False,
    )
```
